256 devices in a mesh: row: 32 (over z_lo, y, core), col: 8 (over x, z_hi).
Axes of the slice: x: 4, y: 4, z: 8 (z_hi: 2, z_lo: 4; z = z_hi * 4 + z_lo), core: 2. Of those that a mesh axis runs over, the one named last changes fastest.
Arguments:
- blocks: bfloat16 [3072, 512, 512], P(('row', 'col')), as said below
- block_rows: int32 [3072], P(('row', 'col')), may hold values from 0 to 511, as said below
- block_cols: int32 [3072], P(('row', 'col')), may hold values from 0 to 511
- inter_counts: int32 [256], P(('row', 'col')), may hold values from 1 to 8, as said below
- keep_mask: int32 [262144], P('row'), may hold values 0 or 1
Outputs:
- bias_final: float32 [262144], P('row')
- balance: float32 [262144], P('row')
The draws below stay inside these ranges and needn't reach their ends.
Inputs may be any that keep to these rules, and one draw needn't show every extreme that they name: `block_rows`: slots of device row index r have block rows from r * 16 to (r + 1) * 16 - 1. The band slots of the devices sharing r hold, in some order, for each such block row i the blocks (i, i) and (i, i - 1), where block row 0's second block is (0, 0) again. Inter-region blocks have block columns not below their block rows. `inter_counts`: some device has all 8 inter-region slots live. `blocks`: positive counts.
All inputs are finite; a program needn't handle non-finite values. No bound on the sum of `keep_mask` on one device may be relied on, other than what follows from the above.
Results may differ from the reference program's by a relative error of at most 0.0004.
Values sent between devices are 32-bit elements; how exact they have to be, the bound alone decides.
A program may use at most 64 MiB of HBM per device.

```python
import jax
import jax.numpy as jnp
from jax import lax

BS = 512
RB = 16
IR_MAX = 8
SWEEPS = 3
NBIN = 262144
N_ROW = 32
N_COL = 8


def layout(key):
    total_rows = RB * N_ROW
    band_slots = 2 * RB // N_COL
    key = jax.random.fold_in(key, 101)
    keys = jax.random.split(key, 5)
    row_base = jnp.arange(N_ROW, dtype=jnp.int32) * RB
    local_rows = row_base[:, None] + jnp.arange(RB, dtype=jnp.int32)[None, :]
    prev_rows = jnp.maximum(local_rows - 1, 0)
    band_rows = jnp.concatenate([local_rows, local_rows], axis=1)
    band_cols = jnp.concatenate([local_rows, prev_rows], axis=1)
    orders = jax.vmap(lambda sub_key: jax.random.permutation(sub_key, 2 * RB))(jax.random.split(keys[0], N_ROW))
    band_rows = jnp.take_along_axis(band_rows, orders, axis=1).reshape(N_ROW, N_COL, band_slots)
    band_cols = jnp.take_along_axis(band_cols, orders, axis=1).reshape(N_ROW, N_COL, band_slots)
    inter_rows = row_base[:, None, None] + jax.random.randint(keys[1], (N_ROW, N_COL, IR_MAX), 0, RB)
    inter_cols = inter_rows + jax.random.randint(keys[2], (N_ROW, N_COL, IR_MAX), 0, total_rows - inter_rows)
    counts = jax.random.randint(keys[3], (N_ROW * N_COL,), 1, IR_MAX + 1)
    chosen = jax.random.randint(keys[4], (), 0, N_ROW * N_COL)
    counts = jnp.where(jnp.arange(N_ROW * N_COL) == chosen, IR_MAX, counts).astype(jnp.int32)
    rows_all = jnp.concatenate([band_rows, inter_rows], axis=2).reshape(-1).astype(jnp.int32)
    cols_all = jnp.concatenate([band_cols, inter_cols], axis=2).reshape(-1).astype(jnp.int32)
    return (rows_all, cols_all, counts)


def draw_block_rows(key, part):
    rows_all, cols_all, counts = layout(key)
    return rows_all


def draw_block_cols(key, part):
    rows_all, cols_all, counts = layout(key)
    return cols_all


def draw_inter_counts(key, part):
    rows_all, cols_all, counts = layout(key)
    return counts


def draw_blocks(key, part):
    rows_all, cols_all, counts = layout(key)
    key = jax.random.fold_in(key, 4)
    keys = jax.random.split(key, 2)
    total_rows = RB * N_ROW
    spread = jnp.log(10.0)
    values = jax.random.uniform(keys[0], (rows_all.shape[0], BS, BS), jnp.float32, 0.5, 1.5)
    bin_scale = jnp.exp(jax.random.uniform(keys[1], (total_rows, BS), jnp.float32) * spread)
    ramp = 1.0 + 2.0 * jnp.arange(total_rows, dtype=jnp.float32) / max(total_rows - 1, 1)
    left = bin_scale[rows_all] * ramp[rows_all][:, None]
    right = bin_scale[cols_all]
    values = values * left[:, :, None] * right[:, None, :]
    return values.astype(jnp.bfloat16)


def set_ends(entries, key, smallest, high):
    dims = entries.shape
    spot = [jax.random.randint(jax.random.fold_in(key, axis), (), 0, dims[axis]) for axis in range(len(dims))]
    entries = entries.at[tuple(spot)].set(smallest)
    longest = dims.index(max(dims))
    spot[longest] = (spot[longest] + 1) % dims[longest]
    return entries.at[tuple(spot)].set(high)


def setup_inputs(seed: int = 0) -> dict:
    key_list = jax.random.split(jax.random.key(seed), 6)
    blocks = draw_blocks(jax.random.fold_in(key_list[5], 71), 0)
    block_rows = draw_block_rows(jax.random.fold_in(key_list[5], 71), 0)
    block_cols = draw_block_cols(jax.random.fold_in(key_list[5], 71), 0)
    inter_counts = draw_inter_counts(jax.random.fold_in(key_list[5], 71), 0)
    keep_mask = set_ends((jax.random.randint(key_list[4], (NBIN,), 0, 10) < 9).astype(jnp.int32), jax.random.fold_in(key_list[4], 1), 0, 1)
    return {"blocks": blocks, "block_rows": block_rows, "block_cols": block_cols, "inter_counts": inter_counts, "keep_mask": keep_mask}


def reference(blocks, block_rows, block_cols, inter_counts, keep_mask):
    devices_all = N_ROW * N_COL
    slot_count = blocks.shape[0] // devices_all
    band_slots = slot_count - IR_MAX
    total_rows = RB * N_ROW
    grouped = blocks.reshape(devices_all, slot_count, BS, BS)
    rows_grouped = block_rows.reshape(devices_all, slot_count)
    cols_grouped = block_cols.reshape(devices_all, slot_count)
    slot_ids = jnp.arange(slot_count)
    active = ((slot_ids[None, :] < band_slots) | (slot_ids[None, :] - band_slots < inter_counts[:, None])).astype(jnp.float32)
    mask_float = keep_mask.astype(jnp.float32)
    bias_now = jnp.ones((NBIN,), jnp.float32)
    balance = jnp.zeros((NBIN,), jnp.float32)
    for sweep_index in range(SWEEPS):
        weights = mask_float / bias_now
        w_table = weights.reshape(total_rows, BS)

        def add_device(totals, device_item):
            block_group, row_ids, col_ids, live_group = device_item
            block_float = block_group.astype(jnp.float32)
            row_part = jnp.einsum("kab,kb->ka", block_float, w_table[col_ids], precision=lax.Precision.HIGHEST) * live_group[:, None]
            col_part = jnp.einsum("kab,ka->kb", block_float, w_table[row_ids], precision=lax.Precision.HIGHEST) * live_group[:, None]
            totals = totals.at[row_ids].add(row_part).at[col_ids].add(col_part)
            return totals, None

        totals, unused = lax.scan(add_device, jnp.zeros((total_rows, BS), jnp.float32), (grouped, rows_grouped, cols_grouped, active))
        bin_sums = weights * totals.reshape(-1)
        mean_sum = jnp.sum(bin_sums * mask_float) / jnp.sum(mask_float)
        bias_now = jnp.where(keep_mask > 0, bias_now * bin_sums / mean_sum, bias_now)
        balance = bin_sums / mean_sum
    return bias_now, balance
```

```python
import jax
import jax.numpy as jnp
from jax import lax
from jax.experimental import pallas as pl
from jax.experimental.pallas import tpu as pltpu
from jax.sharding import PartitionSpec as P

IR_MAX = 8
SWEEPS = 3
RB = 16
BS = 512
SLOTS = 12
BAND = SLOTS - IR_MAX
SEL = 64

F32 = jnp.float32
BF16 = jnp.bfloat16
MESH = pl.DeviceIdType.MESH
Z_OFFSETS = (1, 7, 2)
YC_OFFSETS = (4, 3, 5, 2, 6, 1, 7)
X_OFFSETS = (2, 1, 3)


def split2(v):
    hi = v.astype(BF16)
    lo = (v - hi.astype(F32)).astype(BF16)
    return jnp.concatenate([hi, lo], axis=0)


def exact_pick(pick, v):
    out = None
    for _ in range(3):
        term = v.astype(BF16)
        v = v - term.astype(F32)
        part = jnp.dot(pick, term, preferred_element_type=F32)
        out = part if out is None else out + part
    return out


def full_max(v):
    m = jnp.max(jnp.max(v, axis=1, keepdims=True), axis=0, keepdims=True)
    return jnp.where(m > 0, m, 1.0)


def kernel(
    rows_ref, cols_ref, cnt_ref, mask_ref, blocks_ref,
    bias_ref, bal_ref,
    blk, keep, tbuf, ubuf, uloc, ids, pick, pickt,
    tab, selm, rsel, uprev, cparts, pprev, prevp, dense, rz, xp, zh, stz, styc,
    blk_sem, ids_ss, ids_rs, tab_ss, tab_rs, sel_ss, sel_rs, up_ss, up_rs,
    cp_ss, cp_rs, pp_ss, pp_rs, dz_ss, dz_rs, x_ss, x_rs, zh_ss, zh_rs,
    sz_ss, sz_rs, sy_ss, sy_rs,
):
    row = lax.axis_index("row")
    col = lax.axis_index("col")
    zl = row // 8
    yc = lax.rem(row, 8)
    x = col // 2
    z = lax.rem(col, 2) * 4 + zl

    def z_peer(o):
        q = lax.rem(z + o, 8)
        return (lax.rem(q, 4) * 8 + yc, x * 2 + q // 4)

    def yc_peer(o):
        return (zl * 8 + lax.rem(yc + o, 8), col)

    def x_peer(o):
        return (row, lax.rem(x + o, 4) * 2 + lax.rem(col, 2))

    def send(src, dst, ss, rs, dev):
        c = pltpu.make_async_remote_copy(
            src_ref=src, dst_ref=dst, send_sem=ss, recv_sem=rs,
            device_id=dev, device_id_type=MESH,
        )
        c.start()
        return c

    loads = [
        pltpu.make_async_copy(blocks_ref.at[k], blk.at[k], blk_sem.at[k])
        for k in range(SLOTS)
    ]
    for c in loads:
        c.start()

    barrier = pltpu.get_barrier_semaphore()
    peers = (
        [yc_peer(o) for o in range(1, 8)]
        + [z_peer(o) for o in (1, 2, 4, 6, 7)]
        + [x_peer(o) for o in range(1, 4)]
    )
    for dev in peers:
        pl.semaphore_signal(barrier, inc=1, device_id=dev, device_id_type=MESH)

    live = cnt_ref[0]
    row_l = [lax.rem(rows_ref[k], RB) for k in range(SLOTS)]
    col_l = [cols_ref[k] - row * RB for k in range(SLOTS)]
    lane = lax.broadcasted_iota(jnp.int32, (8, 128), 1)
    idv = jnp.zeros((8, 128), jnp.int32)
    for k in range(IR_MAX):
        code = jnp.where(k < live, cols_ref[BAND + k] + 1, 0)
        idv = jnp.where(lane == yc * 8 + k, code, idv)
    ids[yc] = idv
    for q in range(4):
        keep[:, q * 128:(q + 1) * 128] = mask_ref[pl.ds(q, RB, stride=4), :].astype(F32)
    tbuf[0] = jnp.full((RB, BS), 4.0, F32)
    uloc[...] = jnp.zeros_like(uloc)

    pl.semaphore_wait(barrier, len(peers))
    id_copies = [
        send(ids.at[yc], ids.at[yc], ids_ss.at[o - 1], ids_rs.at[o - 1], yc_peer(o))
        for o in YC_OFFSETS
    ]
    for c in loads:
        c.wait()
    for c in id_copies:
        c.wait()
    code = ids[0]
    for p in range(1, 8):
        code = code + ids[p]
    code = code[0:1]
    cc = jnp.maximum(code - 1, 0)
    want = jnp.where(
        (code > 0) & (((cc // 16) % 8) == yc), (cc // 128) * 16 + cc % 16, -1
    )
    full = jnp.where(lax.broadcasted_iota(jnp.int32, (128, 128), 0) == want, 1.0, 0.0)
    pick[...] = full[:SEL, :SEL].astype(BF16)
    pickt[...] = full.T[:SEL, :SEL].astype(BF16)

    iota16 = lax.broadcasted_iota(jnp.int32, (RB, BS), 0)
    iota32 = lax.broadcasted_iota(jnp.int32, (2 * RB, BS), 0)

    def sweep(s, carry):
        u = jnp.where(keep[...] > 0, 4.0 / tbuf[s], 0.0)
        ubuf[s] = u
        own = pl.ds(pl.multiple_of(zl * RB, RB), RB)
        tab[s, own] = u
        c_tab = [
            send(tab.at[s, own], tab.at[s, own], tab_ss.at[s, i], tab_rs.at[s, i], z_peer(o))
            for i, o in enumerate(Z_OFFSETS)
        ]
        uloc[0:RB] = u

        m = full_max(u)
        inv = 1.0 / m
        acc = None
        for k in range(SLOTS):
            if k < BAND:
                target = jnp.where(col_l[k] >= 0, col_l[k], 2 * RB - 8)
            else:
                target = jnp.where(k - BAND < live, RB + k - BAND, -1)
            vec = uloc[pl.ds(row_l[k], 1), :] * inv
            lhs = split2(jnp.where(iota32 == target, vec, 0.0))
            part = jnp.dot(lhs, blk[k], preferred_element_type=F32)
            acc = part if acc is None else acc + part
        acc = (acc[:2 * RB] + acc[2 * RB:]) * m
        band = acc[0:RB]
        cparts[s, yc] = acc[RB:RB + 8]
        pprev[s] = acc[RB + 8:]
        c_cp = [
            send(cparts.at[s, yc], cparts.at[s, yc], cp_ss.at[s, o - 1], cp_rs.at[s, o - 1], yc_peer(o))
            for o in YC_OFFSETS
        ]
        c_pp = send(pprev.at[s], prevp.at[s], pp_ss.at[s], pp_rs.at[s], yc_peer(7))

        for c in c_tab:
            c.wait()
        selm[s] = exact_pick(pickt[...], tab[s])
        c_sel = [
            send(
                selm.at[s, pl.ds(pl.multiple_of(lax.rem(yc + o, 8) * 8, 8), 8)],
                rsel.at[s, yc], sel_ss.at[s, o - 1], sel_rs.at[s, o - 1], yc_peer(o),
            )
            for o in YC_OFFSETS
        ]
        zsel = jnp.where(yc < 7, zl, jnp.maximum(zl - 1, 0))
        c_up = send(
            tab.at[s, pl.ds(pl.multiple_of(zsel * RB + 8, 8), 8)],
            uprev.at[s], up_ss.at[s], up_rs.at[s], yc_peer(1),
        )

        for c in c_cp:
            c.wait()
        c_pp.wait()
        got = jnp.concatenate([cparts[s, p] for p in range(8)], axis=0)
        d = exact_pick(pick[...], got)
        jprev = jnp.where(yc < 7, zl, zl - 1) * RB + RB - 1
        iota64 = lax.broadcasted_iota(jnp.int32, (SEL, BS), 0)
        d = d + jnp.where(iota64 == jprev, prevp[s, 0:1], 0.0)
        dense[s] = d
        c_dz = [
            send(
                dense.at[s, pl.ds(pl.multiple_of(lax.rem(zl + o, 4) * RB, RB), RB)],
                rz.at[s, i], dz_ss.at[s, i], dz_rs.at[s, i], z_peer(o),
            )
            for i, o in enumerate(Z_OFFSETS)
        ]

        for c in c_sel:
            c.wait()
        c_up.wait()
        ucol = selm[s, pl.ds(pl.multiple_of(yc * 8, 8), 8)]
        for o in range(1, 8):
            ucol = ucol + rsel[s, lax.rem(yc + o, 8)]
        uloc[RB:RB + 8] = uprev[s]
        m2 = full_max(jnp.concatenate([uloc[...], ucol], axis=0))
        inv2 = 1.0 / m2
        acc = None
        for k in range(SLOTS):
            if k < BAND:
                vec = uloc[pl.ds(jnp.where((col_l[k] >= 0) & (col_l[k] < RB), col_l[k], RB + 7), 1), :]
                target = row_l[k]
            else:
                vec = ucol[k - BAND:k - BAND + 1]
                target = jnp.where(k - BAND < live, row_l[k], -1)
            lhs = split2(jnp.where(iota16 == target, vec * inv2, 0.0))
            part = lax.dot_general(
                lhs, blk[k], (((1,), (1,)), ((), ())), preferred_element_type=F32
            )
            acc = part if acc is None else acc + part
        total = (acc[:RB] + acc[RB:]) * m2 + band

        for c in c_dz:
            c.wait()
        total = total + dense[s, own] + rz[s, 0] + rz[s, 1] + rz[s, 2]

        xp[s, x] = total
        c_x = [
            send(xp.at[s, x], xp.at[s, x], x_ss.at[s, o - 1], x_rs.at[s, o - 1], x_peer(o))
            for o in X_OFFSETS
        ]
        for c in c_x:
            c.wait()
        zh[s, 0] = (xp[s, 0] + xp[s, 1]) + (xp[s, 2] + xp[s, 3])
        c_zh = send(zh.at[s, 0], zh.at[s, 1], zh_ss.at[s], zh_rs.at[s], z_peer(4))
        c_zh.wait()
        tbuf[s + 1] = zh[s, 0] + zh[s, 1]
        return carry

    lax.fori_loop(0, SWEEPS, sweep, 0)

    kept = keep[...]
    terms = [
        kept,
        tbuf[1] * kept,
        tbuf[2] * ubuf[1],
        tbuf[3] * ubuf[2],
    ]
    sub = lax.broadcasted_iota(jnp.int32, (8, 128), 0)
    stat = jnp.zeros((8, 128), F32)
    for i, v in enumerate(terms):
        v = jnp.sum(jnp.sum(v, axis=1, keepdims=True), axis=0, keepdims=True)
        stat = jnp.where(sub == i, v, stat)
    stz[zl] = stat
    c_sz = [
        send(stz.at[zl], stz.at[zl], sz_ss.at[i], sz_rs.at[i], z_peer(o))
        for i, o in enumerate(Z_OFFSETS)
    ]
    for c in c_sz:
        c.wait()
    styc[yc] = (stz[0] + stz[1]) + (stz[2] + stz[3])
    c_sy = [
        send(styc.at[yc], styc.at[yc], sy_ss.at[o - 1], sy_rs.at[o - 1], yc_peer(o))
        for o in YC_OFFSETS
    ]
    for c in c_sy:
        c.wait()
    stat = styc[0]
    for p in range(1, 8):
        stat = stat + styc[p]
    count = stat[0:1, 0:1]
    mean1 = stat[1:2, 0:1] / count
    mean2 = stat[2:3, 0:1] / count
    mean3 = stat[3:4, 0:1] / count
    scale = mean1 * mean2 * 0.0625 * mean3
    b3 = tbuf[3]
    bias = jnp.where(kept > 0, b3 / scale, 1.0)
    balance = b3 * ubuf[2] / mean3
    for q in range(4):
        bias_ref[pl.ds(q, RB, stride=4), :] = bias[:, q * 128:(q + 1) * 128]
        bal_ref[pl.ds(q, RB, stride=4), :] = balance[:, q * 128:(q + 1) * 128]


def body(blocks, block_rows, block_cols, inter_counts, keep_mask):
    seg = keep_mask.shape[0]
    vm = pl.BlockSpec(memory_space=pltpu.VMEM)
    sm = pl.BlockSpec(memory_space=pltpu.SMEM)
    S = SWEEPS
    dma = pltpu.SemaphoreType.DMA
    out = jax.ShapeDtypeStruct((seg // 128, 128), F32)
    bias, balance = pl.pallas_call(
        kernel,
        out_shape=(out, out),
        in_specs=[sm, sm, sm, vm, pl.BlockSpec(memory_space=pl.ANY)],
        out_specs=(vm, vm),
        scratch_shapes=[
            pltpu.VMEM((SLOTS, BS, BS), BF16),
            pltpu.VMEM((RB, BS), F32),
            pltpu.VMEM((S + 1, RB, BS), F32),
            pltpu.VMEM((S, RB, BS), F32),
            pltpu.VMEM((RB + 8, BS), F32),
            pltpu.VMEM((8, 8, 128), jnp.int32),
            pltpu.VMEM((SEL, SEL), BF16),
            pltpu.VMEM((SEL, SEL), BF16),
            pltpu.VMEM((S, SEL, BS), F32),
            pltpu.VMEM((S, SEL, BS), F32),
            pltpu.VMEM((S, 8, 8, BS), F32),
            pltpu.VMEM((S, 8, BS), F32),
            pltpu.VMEM((S, 8, 8, BS), F32),
            pltpu.VMEM((S, 8, BS), F32),
            pltpu.VMEM((S, 8, BS), F32),
            pltpu.VMEM((S, SEL, BS), F32),
            pltpu.VMEM((S, 3, RB, BS), F32),
            pltpu.VMEM((S, 4, RB, BS), F32),
            pltpu.VMEM((S, 2, RB, BS), F32),
            pltpu.VMEM((4, 8, 128), F32),
            pltpu.VMEM((8, 8, 128), F32),
            dma((SLOTS,)),
            dma((7,)), dma((7,)),
            dma((S, 3)), dma((S, 3)),
            dma((S, 7)), dma((S, 7)),
            dma((S,)), dma((S,)),
            dma((S, 7)), dma((S, 7)),
            dma((S,)), dma((S,)),
            dma((S, 3)), dma((S, 3)),
            dma((S, 3)), dma((S, 3)),
            dma((S,)), dma((S,)),
            dma((3,)), dma((3,)),
            dma((7,)), dma((7,)),
        ],
        compiler_params=pltpu.CompilerParams(
            collective_id=0, has_side_effects=True, vmem_limit_bytes=48 * 2**20
        ),
        name="balance",
    )(block_rows, block_cols, inter_counts, keep_mask.reshape(seg // 128, 128), blocks)
    return bias.reshape(seg), balance.reshape(seg)


def solution(mesh):
    return jax.shard_map(
        body,
        mesh=mesh,
        in_specs=(
            P(("row", "col"), None, None),
            P(("row", "col")),
            P(("row", "col")),
            P(("row", "col")),
            P("row"),
        ),
        out_specs=(P("row"), P("row")),
        check_vma=False,
    )
```

```python
import jax
import jax.numpy as jnp
from jax import lax
from jax.experimental import pallas as pl
from jax.experimental.pallas import tpu as pltpu
from jax.sharding import PartitionSpec as P

IR_MAX = 8
SWEEPS = 3
RB = 16
BS = 512
SLOTS = 12
BAND = SLOTS - IR_MAX
SEL = 64

F32 = jnp.float32
BF16 = jnp.bfloat16
MESH = pl.DeviceIdType.MESH
YC_OFFSETS = (4, 5, 3, 2, 6, 1, 7)
X_OFFSETS = ((2, 1), (1, 1), (3, 1), (0, 1), (2, 0), (1, 0), (3, 0))


def split2(v):
    hi = v.astype(BF16)
    lo = (v - hi.astype(F32)).astype(BF16)
    return jnp.concatenate([hi, lo], axis=0)


def exact_pick(pick, v):
    out = None
    for _ in range(3):
        term = v.astype(BF16)
        v = v - term.astype(F32)
        part = jnp.dot(pick, term, preferred_element_type=F32)
        out = part if out is None else out + part
    return out


def full_max(v):
    m = jnp.max(jnp.max(v, axis=1, keepdims=True), axis=0, keepdims=True)
    return jnp.where(m > 0, m, 1.0)


def kernel(
    rows_hbm, cols_hbm, cnt_hbm, mask_hbm, blocks_ref,
    bias_ref, bal_ref,
    rows_ref, cols_ref, cnt_ref, mask_ref,
    blk, keep, tbuf, ubuf, uloc, ids, pick, pickt, stat, rowband, colband,
    tab, selm, rsel, uprev, cparts, pprev, prevp, dense, rz, xp, stz, styc, stx,
    in_sem, blk_sem, ids_ss, ids_rs, tab_ss, tab_rs, sel_ss, sel_rs, up_ss, up_rs,
    cp_ss, cp_rs, pp_ss, pp_rs, dz_ss, dz_rs, x_ss, x_rs,
    sz_ss, sz_rs, sy_ss, sy_rs, sx_ss, sx_rs,
):
    row = lax.axis_index("row")
    col = lax.axis_index("col")
    zl = row // 8
    yc = lax.rem(row, 8)
    x = col // 2
    zh = lax.rem(col, 2)
    z = zh * 4 + zl
    z_offsets = (jnp.where(lax.rem(row, 2) == 0, 2, 6), 1, 7)

    def z_peer(o):
        q = lax.rem(z + o, 8)
        return (lax.rem(q, 4) * 8 + yc, x * 2 + q // 4)

    def yc_peer(o):
        return (zl * 8 + lax.rem(yc + o, 8), col)

    def x_peer(o, h):
        return (row, lax.rem(x + o, 4) * 2 + lax.rem(zh + h, 2))

    def step_peer(o):
        wrap = 7 if o == 1 else 0
        q = jnp.where(yc == wrap, lax.rem(z + o, 8), z)
        return (lax.rem(q, 4) * 8 + lax.rem(yc + o, 8), x * 2 + q // 4)

    def copy(src, dst, ss, rs, dev):
        return pltpu.make_async_remote_copy(
            src_ref=src, dst_ref=dst, send_sem=ss, recv_sem=rs,
            device_id=dev, device_id_type=MESH,
        )

    def seg(i):
        return pl.ds(pl.multiple_of(i * RB, RB), RB)

    def eight(i):
        return pl.ds(pl.multiple_of(i * 8, 8), 8)

    own = seg(zl)

    def tab_copies(s):
        return [
            copy(tab.at[s, own], tab.at[s, own], tab_ss.at[s, i], tab_rs.at[s, i], z_peer(o))
            for i, o in enumerate(z_offsets)
        ]

    def up_copy(s):
        return copy(
            tab.at[s, pl.ds(pl.multiple_of(zl * RB + 8, 8), 8)],
            uprev.at[s], up_ss.at[s], up_rs.at[s], step_peer(1),
        )

    def cp_copies(s):
        return [
            copy(cparts.at[s, eight(yc)], cparts.at[s, eight(yc)],
                 cp_ss.at[s, o - 1], cp_rs.at[s, o - 1], yc_peer(o))
            for o in YC_OFFSETS
        ]

    def pp_copy(s):
        return copy(pprev.at[s], prevp.at[s], pp_ss.at[s], pp_rs.at[s], step_peer(7))

    def sel_copies(s):
        return [
            copy(selm.at[s, eight(lax.rem(yc + o, 8))], rsel.at[s, yc],
                 sel_ss.at[s, o - 1], sel_rs.at[s, o - 1], yc_peer(o))
            for o in YC_OFFSETS
        ]

    def dz_copies(s):
        return [
            copy(dense.at[s, seg(lax.rem(zl + o, 4))], rz.at[s, i],
                 dz_ss.at[s, i], dz_rs.at[s, i], z_peer(o))
            for i, o in enumerate(z_offsets)
        ]

    def x_copies(s):
        return [
            copy(xp.at[s, col], xp.at[s, col], x_ss.at[s, o * 2 + h - 1],
                 x_rs.at[s, o * 2 + h - 1], x_peer(o, h))
            for o, h in X_OFFSETS
        ]

    loads = [
        pltpu.make_async_copy(src, dst, in_sem.at[i])
        for i, (src, dst) in enumerate((
            (rows_hbm, rows_ref), (cols_hbm, cols_ref), (cnt_hbm, cnt_ref), (mask_hbm, mask_ref),
        ))
    ] + [
        pltpu.make_async_copy(blocks_ref.at[k], blk.at[k], blk_sem.at[k])
        for k in (*range(BAND, SLOTS), *range(BAND))
    ]
    for c in loads:
        c.start()

    barrier = pltpu.get_barrier_semaphore()
    peers = (
        [x_peer(o, h) for o in range(1, 4) for h in range(2)]
        + [z_peer(o) for o in range(1, 8)]
        + [yc_peer(o) for o in range(1, 8)]
        + [step_peer(1), step_peer(7)]
    )
    for dev in peers:
        pl.semaphore_signal(barrier, inc=1, device_id=dev, device_id_type=MESH)
    for c in loads[:4]:
        c.wait()

    live = cnt_ref[0]
    row_l = [lax.rem(rows_ref[k], RB) for k in range(SLOTS)]
    col_l = [cols_ref[k] - row * RB for k in range(BAND)]
    here = [(c >= 0) & (c < RB) for c in col_l]
    lane = lax.broadcasted_iota(jnp.int32, (8, 128), 1)
    iota8 = lax.broadcasted_iota(jnp.int32, (8, BS), 0)
    iota16 = lax.broadcasted_iota(jnp.int32, (RB, BS), 0)
    iota24 = lax.broadcasted_iota(jnp.int32, (RB + 8, BS), 0)

    idv = jnp.zeros((8, 128), jnp.int32)
    for k in range(IR_MAX):
        code = jnp.where(k < live, cols_ref[BAND + k] + 1, 0)
        idv = jnp.where(lane == yc * 8 + k, code, idv)
    ids[yc] = idv
    for q in range(4):
        keep[:, q * 128:(q + 1) * 128] = mask_ref[pl.ds(q, RB, stride=4), :].astype(F32)
    tbuf[0] = jnp.full((RB, BS), 4.0, F32)

    def total_of(v):
        return jnp.sum(jnp.sum(v, axis=1, keepdims=True), axis=0, keepdims=True)

    sub = lax.broadcasted_iota(jnp.int32, (8, 128), 0)
    stat[...] = jnp.where(sub == 0, total_of(keep[...]), 0.0)

    def weights(s):
        u = jnp.where(keep[...] > 0, 4.0 / tbuf[s], 0.0)
        ubuf[s] = u
        tab[s, own] = u
        uloc[0:RB] = u

    def inter_columns(s):
        m = full_max(uloc[0:RB])
        inv = 1.0 / m
        acc = None
        for k in range(IR_MAX):
            vec = uloc[pl.ds(row_l[BAND + k], 1), :] * inv
            target = jnp.where(k < live, k, -1)
            lhs = split2(jnp.where(iota8 == target, vec, 0.0))
            part = jnp.dot(lhs, blk[BAND + k], preferred_element_type=F32)
            acc = part if acc is None else acc + part
        cparts[s, eight(yc)] = (acc[:8] + acc[8:]) * m

    def band_columns(s):
        m = full_max(uloc[0:RB])
        inv = 1.0 / m
        acc = None
        for k in range(BAND):
            vec = uloc[pl.ds(row_l[k], 1), :] * inv
            target = jnp.where(here[k], col_l[k], RB)
            lhs = split2(jnp.where(iota24 == target, vec, 0.0))
            part = jnp.dot(lhs, blk[k], preferred_element_type=F32)
            acc = part if acc is None else acc + part
        acc = (acc[:RB + 8] + acc[RB + 8:]) * m
        colband[...] = acc[:RB]
        pprev[s] = acc[RB:]

    weights(0)
    for c in loads[4:4 + IR_MAX]:
        c.wait()
    inter_columns(0)
    for c in loads[4 + IR_MAX:]:
        c.wait()
    band_columns(0)

    pl.semaphore_wait(barrier, len(peers))
    id_copies = [
        copy(ids.at[yc], ids.at[yc], ids_ss.at[o - 1], ids_rs.at[o - 1], yc_peer(o))
        for o in YC_OFFSETS
    ]
    for c in (*tab_copies(0), up_copy(0), *id_copies, *cp_copies(0), pp_copy(0)):
        c.start()

    def sweep(s, carry):
        up_copy(s).wait_recv()
        uloc[RB:RB + 8] = uprev[s]
        m = full_max(uloc[...])
        inv = 1.0 / m
        acc = None
        for k in range(BAND):
            vec = uloc[pl.ds(jnp.where(here[k], col_l[k], RB + 7), 1), :] * inv
            lhs = split2(jnp.where(iota16 == row_l[k], vec, 0.0))
            part = lax.dot_general(
                lhs, blk[k], (((1,), (1,)), ((), ())), preferred_element_type=F32
            )
            acc = part if acc is None else acc + part
        rowband[...] = (acc[:RB] + acc[RB:]) * m

        @pl.when(s == 0)
        def _():
            for c in id_copies:
                c.wait()
            code = ids[0]
            for p in range(1, 8):
                code = code + ids[p]
            code = code[0:1]
            cc = jnp.maximum(code - 1, 0)
            want = jnp.where(
                (code > 0) & (((cc // 16) % 8) == yc), (cc // 128) * 16 + cc % 16, -1
            )
            full = jnp.where(
                lax.broadcasted_iota(jnp.int32, (128, 128), 0) == want, 1.0, 0.0
            )
            pick[...] = full[:SEL, :SEL].astype(BF16)
            pickt[...] = full.T[:SEL, :SEL].astype(BF16)

        for c in tab_copies(s):
            c.wait_recv()
        selm[s] = exact_pick(pickt[...], tab[s])
        for c in sel_copies(s):
            c.start()

        for c in cp_copies(s):
            c.wait_recv()
        dense[s] = exact_pick(pick[...], cparts[s])
        for c in dz_copies(s):
            c.start()

        share = total_of(dense[s] * tab[s]) + total_of(uloc[0:RB] * rowband[...])
        stat[...] = jnp.where(sub == s + 1, share, stat[...])

        @pl.when(s == SWEEPS - 1)
        def _():
            stz[z] = stat[...]
            for o in range(1, 8):
                copy(stz.at[z], stz.at[z], sz_ss.at[o - 1], sz_rs.at[o - 1], z_peer(o)).start()

        for c in sel_copies(s):
            c.wait_recv()
        ucol = selm[s, eight(yc)]
        for o in range(1, 8):
            ucol = ucol + rsel[s, lax.rem(yc + o, 8)]
        m2 = full_max(ucol)
        ucol = ucol * (1.0 / m2)
        acc = None
        for k in range(IR_MAX):
            target = jnp.where(k < live, row_l[BAND + k], -1)
            lhs = split2(jnp.where(iota16 == target, ucol[k:k + 1], 0.0))
            part = lax.dot_general(
                lhs, blk[BAND + k], (((1,), (1,)), ((), ())), preferred_element_type=F32
            )
            acc = part if acc is None else acc + part
        total = (acc[:RB] + acc[RB:]) * m2 + rowband[...] + colband[...] + dense[s, own]

        pp_copy(s).wait_recv()
        total = total + jnp.where(iota16 == RB - 1, prevp[s, 0:1], 0.0)
        for c in dz_copies(s):
            c.wait_recv()
        total = total + rz[s, 0] + rz[s, 1] + rz[s, 2]

        xp[s, col] = total
        for c in x_copies(s):
            c.start()

        @pl.when(s == SWEEPS - 1)
        def _():
            for o in range(1, 8):
                copy(stz.at[z], stz.at[z], sz_ss.at[o - 1], sz_rs.at[o - 1], z_peer(o)).wait()
            v = stz[0]
            for p in range(1, 8):
                v = v + stz[p]
            styc[yc] = v
            c_sy = [
                copy(styc.at[yc], styc.at[yc], sy_ss.at[o - 1], sy_rs.at[o - 1], yc_peer(o))
                for o in YC_OFFSETS
            ]
            for c in c_sy:
                c.start()
            for c in c_sy:
                c.wait()
            v = styc[0]
            for p in range(1, 8):
                v = v + styc[p]
            stx[x] = v
            for o in range(1, 4):
                copy(stx.at[x], stx.at[x], sx_ss.at[o - 1], sx_rs.at[o - 1], x_peer(o, 0)).start()

        for c in (*tab_copies(s), up_copy(s), *cp_copies(s), pp_copy(s),
                  *sel_copies(s), *dz_copies(s)):
            c.wait_send()
        for c in x_copies(s):
            c.wait()
        t = xp[s, 0]
        for p in range(1, 8):
            t = t + xp[s, p]
        tbuf[s + 1] = t

        @pl.when(s < SWEEPS - 1)
        def _():
            n = s + 1
            weights(n)
            for c in (*tab_copies(n), up_copy(n)):
                c.start()
            inter_columns(n)
            for c in cp_copies(n):
                c.start()
            band_columns(n)
            pp_copy(n).start()

        return carry

    lax.fori_loop(0, SWEEPS, sweep, 0)

    for o in range(1, 4):
        copy(stx.at[x], stx.at[x], sx_ss.at[o - 1], sx_rs.at[o - 1], x_peer(o, 0)).wait()
    v = (stx[0] + stx[1]) + (stx[2] + stx[3])
    count = v[0:1, 0:1] * 0.125
    mean1 = v[1:2, 0:1] * 2.0 / count
    mean2 = v[2:3, 0:1] * 2.0 / count
    mean3 = v[3:4, 0:1] * 2.0 / count
    scale = mean1 * mean2 * 0.0625 * mean3
    b3 = tbuf[SWEEPS]
    bias = jnp.where(keep[...] > 0, b3 / scale, 1.0)
    balance = b3 * ubuf[SWEEPS - 1] / mean3
    for q in range(4):
        bias_ref[pl.ds(q, RB, stride=4), :] = bias[:, q * 128:(q + 1) * 128]
        bal_ref[pl.ds(q, RB, stride=4), :] = balance[:, q * 128:(q + 1) * 128]


def body(blocks, block_rows, block_cols, inter_counts, keep_mask):
    seg = keep_mask.shape[0]
    vm = pl.BlockSpec(memory_space=pltpu.VMEM)
    hbm = pl.BlockSpec(memory_space=pl.ANY)
    S = SWEEPS
    dma = pltpu.SemaphoreType.DMA
    i32 = jnp.int32
    out = jax.ShapeDtypeStruct((seg // 128, 128), F32)
    bias, balance = pl.pallas_call(
        kernel,
        out_shape=(out, out),
        in_specs=[hbm] * 5,
        out_specs=(vm, vm),
        scratch_shapes=[
            pltpu.SMEM((SLOTS,), i32),
            pltpu.SMEM((SLOTS,), i32),
            pltpu.SMEM((1,), i32),
            pltpu.VMEM((seg // 128, 128), i32),
            pltpu.VMEM((SLOTS, BS, BS), BF16),
            pltpu.VMEM((RB, BS), F32),
            pltpu.VMEM((S + 1, RB, BS), F32),
            pltpu.VMEM((S, RB, BS), F32),
            pltpu.VMEM((RB + 8, BS), F32),
            pltpu.VMEM((8, 8, 128), i32),
            pltpu.VMEM((SEL, SEL), BF16),
            pltpu.VMEM((SEL, SEL), BF16),
            pltpu.VMEM((8, 128), F32),
            pltpu.VMEM((RB, BS), F32),
            pltpu.VMEM((RB, BS), F32),
            pltpu.VMEM((S, SEL, BS), F32),
            pltpu.VMEM((S, SEL, BS), F32),
            pltpu.VMEM((S, 8, 8, BS), F32),
            pltpu.VMEM((S, 8, BS), F32),
            pltpu.VMEM((S, SEL, BS), F32),
            pltpu.VMEM((S, 8, BS), F32),
            pltpu.VMEM((S, 8, BS), F32),
            pltpu.VMEM((S, SEL, BS), F32),
            pltpu.VMEM((S, 3, RB, BS), F32),
            pltpu.VMEM((S, 8, RB, BS), F32),
            pltpu.VMEM((8, 8, 128), F32),
            pltpu.VMEM((8, 8, 128), F32),
            pltpu.VMEM((4, 8, 128), F32),
            dma((4,)),
            dma((SLOTS,)),
            dma((7,)), dma((7,)),
            dma((S, 3)), dma((S, 3)),
            dma((S, 7)), dma((S, 7)),
            dma((S,)), dma((S,)),
            dma((S, 7)), dma((S, 7)),
            dma((S,)), dma((S,)),
            dma((S, 3)), dma((S, 3)),
            dma((S, 7)), dma((S, 7)),
            dma((7,)), dma((7,)),
            dma((7,)), dma((7,)),
            dma((3,)), dma((3,)),
        ],
        compiler_params=pltpu.CompilerParams(
            collective_id=0, has_side_effects=True, vmem_limit_bytes=48 * 2**20
        ),
        name="balance",
    )(block_rows, block_cols, inter_counts, keep_mask.reshape(seg // 128, 128), blocks)
    return bias.reshape(seg), balance.reshape(seg)


def solution(mesh):
    return jax.shard_map(
        body,
        mesh=mesh,
        in_specs=(
            P(("row", "col"), None, None),
            P(("row", "col")),
            P(("row", "col")),
            P(("row", "col")),
            P("row"),
        ),
        out_specs=(P("row"), P("row")),
        check_vma=False,
    )
```

```python
import jax
import jax.numpy as jnp
from jax import lax
from jax.experimental import pallas as pl
from jax.experimental.pallas import tpu as pltpu
from jax.sharding import PartitionSpec as P

IR_MAX = 8
SWEEPS = 3
RB = 16
BS = 512
SLOTS = 12
BAND = SLOTS - IR_MAX
SEL = 64

F32 = jnp.float32
BF16 = jnp.bfloat16
MESH = pl.DeviceIdType.MESH
YC_OFFSETS = (4, 5, 3, 2, 6, 1, 7)
X_OFFSETS = (2, 1, 3)


def split2(v):
    hi = v.astype(BF16)
    lo = (v - hi.astype(F32)).astype(BF16)
    return jnp.concatenate([hi, lo], axis=0)


def exact_pick(pick, v):
    out = None
    for _ in range(3):
        term = v.astype(BF16)
        v = v - term.astype(F32)
        part = jnp.dot(pick, term, preferred_element_type=F32)
        out = part if out is None else out + part
    return out


def full_max(v):
    m = jnp.max(jnp.max(v, axis=1, keepdims=True), axis=0, keepdims=True)
    return jnp.where(m > 0, m, 1.0)


def kernel(
    rows_hbm, cols_hbm, cnt_hbm, mask_hbm, blocks_ref,
    bias_ref, bal_ref,
    rows_ref, cols_ref, cnt_ref, mask_ref,
    blk, keep, tbuf, ubuf, uloc, ids, pick, pickt, stat, rowband, colband,
    tab, selm, rsel, ulast, uprev, cparts, pprev, prevp, dense, rz, xp, zp, stz, styc, stx,
    in_sem, blk_sem, ids_ss, ids_rs, tab_ss, tab_rs, sel_ss, sel_rs, up_ss, up_rs,
    cp_ss, cp_rs, pp_ss, pp_rs, dz_ss, dz_rs, x_ss, x_rs, zh_ss, zh_rs,
    sz_ss, sz_rs, sy_ss, sy_rs, sx_ss, sx_rs,
):
    row = lax.axis_index("row")
    col = lax.axis_index("col")
    zl = row // 8
    yc = lax.rem(row, 8)
    x = col // 2
    zh = lax.rem(col, 2)
    z = zh * 4 + zl
    z_offsets = (jnp.where(lax.rem(row, 2) == 0, 2, 6), 1, 7)

    def z_peer(o):
        q = lax.rem(z + o, 8)
        return (lax.rem(q, 4) * 8 + yc, x * 2 + q // 4)

    def yc_peer(o):
        return (zl * 8 + lax.rem(yc + o, 8), col)

    def x_peer(o):
        return (row, lax.rem(x + o, 4) * 2 + zh)

    def step_peer(o):
        wrap = 7 if o == 1 else 0
        q = jnp.where(yc == wrap, lax.rem(z + o, 8), z)
        return (lax.rem(q, 4) * 8 + lax.rem(yc + o, 8), x * 2 + q // 4)

    def copy(src, dst, ss, rs, dev):
        return pltpu.make_async_remote_copy(
            src_ref=src, dst_ref=dst, send_sem=ss, recv_sem=rs,
            device_id=dev, device_id_type=MESH,
        )

    def seg(i):
        return pl.ds(pl.multiple_of(i * RB, RB), RB)

    def eight(i):
        return pl.ds(pl.multiple_of(i * 8, 8), 8)

    own = seg(zl)

    def tab_copies(s):
        return [
            copy(tab.at[s, own], tab.at[s, own], tab_ss.at[s, i], tab_rs.at[s, i], z_peer(o))
            for i, o in enumerate(z_offsets)
        ]

    def up_copy(s):
        return copy(
            ulast.at[s], uprev.at[s], up_ss.at[s], up_rs.at[s], step_peer(1),
        )

    def cp_copies(s):
        return [
            copy(cparts.at[s, eight(yc)], cparts.at[s, eight(yc)],
                 cp_ss.at[s, o - 1], cp_rs.at[s, o - 1], yc_peer(o))
            for o in YC_OFFSETS
        ]

    def pp_copy(s):
        return copy(pprev.at[s], prevp.at[s], pp_ss.at[s], pp_rs.at[s], step_peer(7))

    def sel_copies(s):
        return [
            copy(selm.at[s, eight(lax.rem(yc + o, 8))], rsel.at[s, yc],
                 sel_ss.at[s, o - 1], sel_rs.at[s, o - 1], yc_peer(o))
            for o in YC_OFFSETS
        ]

    def dz_copies(s):
        return [
            copy(dense.at[s, seg(lax.rem(zl + o, 4))], rz.at[s, i],
                 dz_ss.at[s, i], dz_rs.at[s, i], z_peer(o))
            for i, o in enumerate(z_offsets)
        ]

    def x_copies(s, h):
        return [
            copy(xp.at[s, h, x], xp.at[s, h, x], x_ss.at[s, h, o - 1],
                 x_rs.at[s, h, o - 1], x_peer(o))
            for o in X_OFFSETS
        ]

    def zh_copy(s, h):
        return copy(zp.at[s, h, 0], zp.at[s, h, 1], zh_ss.at[s, h], zh_rs.at[s, h], z_peer(4))

    def x_sum(s, h):
        return (xp[s, h, 0] + xp[s, h, 1]) + (xp[s, h, 2] + xp[s, h, 3])

    loads = [
        pltpu.make_async_copy(src, dst, in_sem.at[i])
        for i, (src, dst) in enumerate((
            (rows_hbm, rows_ref), (cols_hbm, cols_ref), (cnt_hbm, cnt_ref), (mask_hbm, mask_ref),
        ))
    ] + [
        pltpu.make_async_copy(blocks_ref.at[k], blk.at[k], blk_sem.at[k])
        for k in (*range(BAND, SLOTS), *range(BAND))
    ]
    for c in loads:
        c.start()

    barrier = pltpu.get_barrier_semaphore()
    peers = (
        [x_peer(o) for o in range(1, 4)]
        + [z_peer(o) for o in range(1, 8)]
        + [yc_peer(o) for o in range(1, 8)]
        + [step_peer(1), step_peer(7)]
    )
    for dev in peers:
        pl.semaphore_signal(barrier, inc=1, device_id=dev, device_id_type=MESH)
    for c in loads[:4]:
        c.wait()

    live = cnt_ref[0]
    row_l = [lax.rem(rows_ref[k], RB) for k in range(SLOTS)]
    col_l = [cols_ref[k] - row * RB for k in range(BAND)]
    here = [(c >= 0) & (c < RB) for c in col_l]
    lane = lax.broadcasted_iota(jnp.int32, (8, 128), 1)
    iota8 = lax.broadcasted_iota(jnp.int32, (8, BS), 0)
    iota16 = lax.broadcasted_iota(jnp.int32, (RB, BS), 0)
    iota24 = lax.broadcasted_iota(jnp.int32, (RB + 8, BS), 0)

    idv = jnp.zeros((8, 128), jnp.int32)
    for k in range(IR_MAX):
        code = jnp.where(k < live, cols_ref[BAND + k] + 1, 0)
        idv = jnp.where(lane == yc * 8 + k, code, idv)
    ids[yc] = idv
    for q in range(4):
        keep[:, q * 128:(q + 1) * 128] = mask_ref[pl.ds(q, RB, stride=4), :].astype(F32)
    tbuf[0] = jnp.full((RB, BS), 4.0, F32)
    uloc[...] = jnp.zeros_like(uloc)

    def total_of(v):
        return jnp.sum(jnp.sum(v, axis=1, keepdims=True), axis=0, keepdims=True)

    sub = lax.broadcasted_iota(jnp.int32, (8, 128), 0)
    stat[...] = jnp.where(sub == 0, total_of(keep[...]), 0.0)

    def weights(s):
        u = jnp.where(keep[...] > 0, 4.0 / tbuf[s], 0.0)
        ubuf[s] = u
        tab[s, own] = u
        uloc[0:RB] = u
        ulast[s] = u[RB - 1:]

    def inter_columns(s):
        m = full_max(uloc[0:RB])
        inv = 1.0 / m
        acc = None
        for k in range(IR_MAX):
            vec = uloc[pl.ds(row_l[BAND + k], 1), :] * inv
            target = jnp.where(k < live, k, -1)
            lhs = split2(jnp.where(iota8 == target, vec, 0.0))
            part = jnp.dot(lhs, blk[BAND + k], preferred_element_type=F32)
            acc = part if acc is None else acc + part
        cparts[s, eight(yc)] = (acc[:8] + acc[8:]) * m

    def band_columns(s):
        m = full_max(uloc[0:RB])
        inv = 1.0 / m
        acc = None
        for k in range(BAND):
            vec = uloc[pl.ds(row_l[k], 1), :] * inv
            target = jnp.where(here[k], col_l[k], RB)
            lhs = split2(jnp.where(iota24 == target, vec, 0.0))
            part = jnp.dot(lhs, blk[k], preferred_element_type=F32)
            acc = part if acc is None else acc + part
        acc = (acc[:RB + 8] + acc[RB + 8:]) * m
        colband[...] = acc[:RB]
        pprev[s] = acc[RB:RB + 1]

    def add_share(s):
        share = total_of(dense[s] * tab[s]) + total_of(uloc[0:RB] * rowband[...])
        stat[...] = jnp.where(sub == s + 1, share, stat[...])

    def first_columns():
        for c in loads[4:4 + IR_MAX]:
            c.wait()
        inter_columns(0)

    early = z < 4
    weights(0)

    @pl.when(early)
    def _():
        first_columns()

    pl.semaphore_wait(barrier, len(peers))
    id_copies = [
        copy(ids.at[yc], ids.at[yc], ids_ss.at[o - 1], ids_rs.at[o - 1], yc_peer(o))
        for o in YC_OFFSETS
    ]
    for c in (*tab_copies(0), up_copy(0), *id_copies):
        c.start()

    @pl.when(jnp.logical_not(early))
    def _():
        first_columns()

    for c in cp_copies(0):
        c.start()
    for c in loads[4 + IR_MAX:]:
        c.wait()
    band_columns(0)
    pp_copy(0).start()

    def sweep(s, carry):
        up_copy(s).wait_recv()
        uloc[RB:RB + 1] = uprev[s]
        m = full_max(uloc[...])
        inv = 1.0 / m
        acc = None
        for k in range(BAND):
            vec = uloc[pl.ds(jnp.where(here[k], col_l[k], RB), 1), :] * inv
            lhs = split2(jnp.where(iota16 == row_l[k], vec, 0.0))
            part = lax.dot_general(
                lhs, blk[k], (((1,), (1,)), ((), ())), preferred_element_type=F32
            )
            acc = part if acc is None else acc + part
        rowband[...] = (acc[:RB] + acc[RB:]) * m

        @pl.when(s == 0)
        def _():
            for c in id_copies:
                c.wait()
            code = ids[0]
            for p in range(1, 8):
                code = code + ids[p]
            code = code[0:1]
            cc = jnp.maximum(code - 1, 0)
            want = jnp.where(
                (code > 0) & (((cc // 16) % 8) == yc), (cc // 128) * 16 + cc % 16, -1
            )
            full = jnp.where(
                lax.broadcasted_iota(jnp.int32, (128, 128), 0) == want, 1.0, 0.0
            )
            pick[...] = full[:SEL, :SEL].astype(BF16)
            pickt[...] = full.T[:SEL, :SEL].astype(BF16)

        for c in tab_copies(s):
            c.wait_recv()
        selm[s] = exact_pick(pickt[...], tab[s])
        for c in sel_copies(s):
            c.start()

        for c in cp_copies(s):
            c.wait_recv()
        dense[s] = exact_pick(pick[...], cparts[s])
        for c in dz_copies(s):
            c.start()

        @pl.when(s == SWEEPS - 1)
        def _():
            add_share(s)
            stz[z] = stat[...]
            for o in range(1, 8):
                copy(stz.at[z], stz.at[z], sz_ss.at[o - 1], sz_rs.at[o - 1], z_peer(o)).start()

        for c in sel_copies(s):
            c.wait_recv()
        ucol = selm[s, eight(yc)]
        for o in range(1, 8):
            ucol = ucol + rsel[s, lax.rem(yc + o, 8)]
        m2 = full_max(ucol)
        ucol = ucol * (1.0 / m2)
        acc = None
        for k in range(IR_MAX):
            target = jnp.where(k < live, row_l[BAND + k], -1)
            lhs = split2(jnp.where(iota16 == target, ucol[k:k + 1], 0.0))
            part = lax.dot_general(
                lhs, blk[BAND + k], (((1,), (1,)), ((), ())), preferred_element_type=F32
            )
            acc = part if acc is None else acc + part
        total = (acc[:RB] + acc[RB:]) * m2 + rowband[...] + colband[...] + dense[s, own]

        pp_copy(s).wait_recv()
        total = total + jnp.where(iota16 == RB - 1, prevp[s], 0.0)
        for c in dz_copies(s):
            c.wait_recv()
        total = total + rz[s, 0] + rz[s, 1] + rz[s, 2]

        half = BS // 2
        zp[s, 1, 0] = total[:, half:]
        zh_copy(s, 1).start()
        xp[s, 0, x] = total[:, :half]
        for c in x_copies(s, 0):
            c.start()

        @pl.when(s < SWEEPS - 1)
        def _():
            add_share(s)

        for c in (*tab_copies(s), up_copy(s), *cp_copies(s), pp_copy(s),
                  *sel_copies(s), *dz_copies(s)):
            c.wait_send()

        for c in x_copies(s, 0):
            c.wait_recv()
        zp[s, 0, 0] = x_sum(s, 0)
        zh_copy(s, 0).start()
        zh_copy(s, 1).wait_recv()
        xp[s, 1, x] = zp[s, 1, 0] + zp[s, 1, 1]
        for c in x_copies(s, 1):
            c.start()

        @pl.when(s == SWEEPS - 1)
        def _():
            for o in range(1, 8):
                copy(stz.at[z], stz.at[z], sz_ss.at[o - 1], sz_rs.at[o - 1], z_peer(o)).wait()
            v = stz[0]
            for p in range(1, 8):
                v = v + stz[p]
            styc[yc] = v
            c_sy = [
                copy(styc.at[yc], styc.at[yc], sy_ss.at[o - 1], sy_rs.at[o - 1], yc_peer(o))
                for o in YC_OFFSETS
            ]
            for c in c_sy:
                c.start()
            for c in c_sy:
                c.wait()
            v = styc[0]
            for p in range(1, 8):
                v = v + styc[p]
            stx[x] = v
            for o in range(1, 4):
                copy(stx.at[x], stx.at[x], sx_ss.at[o - 1], sx_rs.at[o - 1], x_peer(o)).start()

        for h in range(2):
            for c in (zh_copy(s, h), *x_copies(s, h)):
                c.wait_send()
        for c in x_copies(s, 1):
            c.wait_recv()
        tbuf[s + 1, :, half:] = x_sum(s, 1)
        zh_copy(s, 0).wait_recv()
        tbuf[s + 1, :, :half] = zp[s, 0, 0] + zp[s, 0, 1]

        @pl.when(s < SWEEPS - 1)
        def _():
            n = s + 1
            weights(n)
            for c in (*tab_copies(n), up_copy(n)):
                c.start()
            inter_columns(n)
            for c in cp_copies(n):
                c.start()
            band_columns(n)
            pp_copy(n).start()

        return carry

    lax.fori_loop(0, SWEEPS, sweep, 0)

    for o in range(1, 4):
        copy(stx.at[x], stx.at[x], sx_ss.at[o - 1], sx_rs.at[o - 1], x_peer(o)).wait()
    v = (stx[0] + stx[1]) + (stx[2] + stx[3])
    count = v[0:1, 0:1] * 0.125
    mean1 = v[1:2, 0:1] * 2.0 / count
    mean2 = v[2:3, 0:1] * 2.0 / count
    mean3 = v[3:4, 0:1] * 2.0 / count
    scale = mean1 * mean2 * 0.0625 * mean3
    b3 = tbuf[SWEEPS]
    bias = jnp.where(keep[...] > 0, b3 / scale, 1.0)
    balance = b3 * ubuf[SWEEPS - 1] / mean3
    for q in range(4):
        bias_ref[pl.ds(q, RB, stride=4), :] = bias[:, q * 128:(q + 1) * 128]
        bal_ref[pl.ds(q, RB, stride=4), :] = balance[:, q * 128:(q + 1) * 128]


def body(blocks, block_rows, block_cols, inter_counts, keep_mask):
    seg = keep_mask.shape[0]
    vm = pl.BlockSpec(memory_space=pltpu.VMEM)
    hbm = pl.BlockSpec(memory_space=pltpu.HBM)
    S = SWEEPS
    dma = pltpu.SemaphoreType.DMA
    i32 = jnp.int32
    out = jax.ShapeDtypeStruct((seg // 128, 128), F32)
    bias, balance = pl.pallas_call(
        kernel,
        out_shape=(out, out),
        in_specs=[hbm] * 5,
        out_specs=(vm, vm),
        scratch_shapes=[
            pltpu.SMEM((SLOTS,), i32),
            pltpu.SMEM((SLOTS,), i32),
            pltpu.SMEM((1,), i32),
            pltpu.VMEM((seg // 128, 128), i32),
            pltpu.VMEM((SLOTS, BS, BS), BF16),
            pltpu.VMEM((RB, BS), F32),
            pltpu.VMEM((S + 1, RB, BS), F32),
            pltpu.VMEM((S, RB, BS), F32),
            pltpu.VMEM((RB + 8, BS), F32),
            pltpu.VMEM((8, 8, 128), i32),
            pltpu.VMEM((SEL, SEL), BF16),
            pltpu.VMEM((SEL, SEL), BF16),
            pltpu.VMEM((8, 128), F32),
            pltpu.VMEM((RB, BS), F32),
            pltpu.VMEM((RB, BS), F32),
            pltpu.VMEM((S, SEL, BS), F32),
            pltpu.VMEM((S, SEL, BS), F32),
            pltpu.VMEM((S, 8, 8, BS), F32),
            pltpu.VMEM((S, 1, BS), F32),
            pltpu.VMEM((S, 1, BS), F32),
            pltpu.VMEM((S, SEL, BS), F32),
            pltpu.VMEM((S, 1, BS), F32),
            pltpu.VMEM((S, 1, BS), F32),
            pltpu.VMEM((S, SEL, BS), F32),
            pltpu.VMEM((S, 3, RB, BS), F32),
            pltpu.VMEM((S, 2, 4, RB, BS // 2), F32),
            pltpu.VMEM((S, 2, 2, RB, BS // 2), F32),
            pltpu.VMEM((8, 8, 128), F32),
            pltpu.VMEM((8, 8, 128), F32),
            pltpu.VMEM((4, 8, 128), F32),
            dma((4,)),
            dma((SLOTS,)),
            dma((7,)), dma((7,)),
            dma((S, 3)), dma((S, 3)),
            dma((S, 7)), dma((S, 7)),
            dma((S,)), dma((S,)),
            dma((S, 7)), dma((S, 7)),
            dma((S,)), dma((S,)),
            dma((S, 3)), dma((S, 3)),
            dma((S, 2, 3)), dma((S, 2, 3)),
            dma((S, 2)), dma((S, 2)),
            dma((7,)), dma((7,)),
            dma((7,)), dma((7,)),
            dma((3,)), dma((3,)),
        ],
        compiler_params=pltpu.CompilerParams(
            collective_id=0, has_side_effects=True, vmem_limit_bytes=58 * 2**20
        ),
        name="balance",
    )(block_rows, block_cols, inter_counts, keep_mask.reshape(seg // 128, 128), blocks)
    return bias.reshape(seg), balance.reshape(seg)


def solution(mesh):
    return jax.shard_map(
        body,
        mesh=mesh,
        in_specs=(
            P(("row", "col"), None, None),
            P(("row", "col")),
            P(("row", "col")),
            P(("row", "col")),
            P("row"),
        ),
        out_specs=(P("row"), P("row")),
        check_vma=False,
    )
```

```python
import jax
import jax.numpy as jnp
from jax import lax
from jax.experimental import pallas as pl
from jax.experimental.pallas import tpu as pltpu
from jax.sharding import PartitionSpec as P

IR_MAX = 8
SWEEPS = 3
RB = 16
BS = 512
SLOTS = 12
BAND = SLOTS - IR_MAX
SEL = 64
VMEM_LIMIT = 58 * 2**20

F32 = jnp.float32
BF16 = jnp.bfloat16
MESH = pl.DeviceIdType.MESH
RING = (2, 1, 3)


def split2(v):
    hi = v.astype(BF16)
    lo = (v - hi.astype(F32)).astype(BF16)
    return jnp.concatenate([hi, lo], axis=0)


def exact_pick(pick, v):
    out = None
    for _ in range(3):
        term = v.astype(BF16)
        v = v - term.astype(F32)
        part = jnp.dot(pick, term, preferred_element_type=F32)
        out = part if out is None else out + part
    return out


def full_max(v):
    m = jnp.max(jnp.max(v, axis=1, keepdims=True), axis=0, keepdims=True)
    return jnp.where(m > 0, m, 1.0)


def kernel(
    rows_hbm, cols_hbm, cnt_hbm, mask_hbm, blocks_ref,
    bias_ref, bal_ref,
    rows_ref, cols_ref, cnt_ref, mask_ref,
    blk, keep, tbuf, ubuf, uloc, ids, pick, pickt, stat, rowband, colband,
    tab, selm, rsel, ulast, uprev, cparts, pprev, prevp, dense, rz,
    xa, za, ta, zb, xb, tb, wstat, stz, sty, stx, fin,
    in_sem, blk_sem, ids_ss, ids_rs, tab_ss, tab_rs, sel_ss, sel_rs, up_ss, up_rs,
    cp_ss, cp_rs, pp_ss, pp_rs, dz_ss, dz_rs, xa_ss, xa_rs, za_ss, za_rs,
    zb_ss, zb_rs, xb_ss, xb_rs, ws_ss, ws_rs,
    sz_ss, sz_rs, sy_ss, sy_rs, sx_ss, sx_rs, fin_ss, fin_rs,
):
    row = lax.axis_index("row")
    col = lax.axis_index("col")
    zl = row // 8
    yc = lax.rem(row, 8)
    y = yc // 2
    core = lax.rem(row, 2)
    x = col // 2
    zh = lax.rem(col, 2)
    z = zh * 4 + zl
    half = BS // 2
    hub = core == 1
    worker = core == 0
    inner = jnp.where(zl < 2, 2, 6)
    two = (inner, 8 - inner)

    def chip(xx, yy, zz, cc):
        return (lax.rem(zz, 4) * 8 + yy * 2 + cc, xx * 2 + zz // 4)

    def z_peer(o, c):
        return chip(x, y, lax.rem(z + o, 8), c)

    def y_peer(o, c):
        return chip(x, lax.rem(y + o, 4), z, c)

    def x_peer(o, c):
        return chip(lax.rem(x + o, 4), y, z, c)

    def sibling(c):
        return chip(x, y, z, c)

    def step_peer(o):
        wrap = 7 if o == 1 else 0
        q = jnp.where(yc == wrap, lax.rem(z + o, 8), z)
        return (lax.rem(q, 4) * 8 + lax.rem(yc + o, 8), x * 2 + q // 4)

    def copy(src, dst, ss, rs, dev):
        return pltpu.make_async_remote_copy(
            src_ref=src, dst_ref=dst, send_sem=ss, recv_sem=rs,
            device_id=dev, device_id_type=MESH,
        )

    def seg(q, c):
        return pl.ds(pl.multiple_of(q * 2 * RB + c * RB, RB), RB)

    def eight(i):
        return pl.ds(pl.multiple_of(i * 8, 8), 8)

    own = seg(zl, core)
    mine = eight(yc)

    def tab_copies(s, c):
        out = [
            copy(tab.at[s, own], tab.at[s, own], tab_ss.at[s, i], tab_rs.at[s, i, c], z_peer(o, 1))
            for i, o in enumerate((two[c], 1, 7))
        ]
        if c == 0:
            out.append(copy(tab.at[s, own], tab.at[s, own], tab_ss.at[s, 3], tab_rs.at[s, 3, 0], sibling(1)))
        return out

    def ids_copies(c):
        out = [copy(ids.at[yc], ids.at[yc], ids_ss.at[o - 1], ids_rs.at[o - 1, c], y_peer(o, 1)) for o in RING]
        if c == 0:
            out.append(copy(ids.at[yc], ids.at[yc], ids_ss.at[3], ids_rs.at[3, 0], sibling(1)))
        return out

    def cp_copies(s, c):
        out = [
            copy(cparts.at[s, mine], cparts.at[s, mine], cp_ss.at[s, o - 1], cp_rs.at[s, o - 1, c], y_peer(o, 1))
            for o in RING
        ]
        if c == 0:
            out.append(copy(cparts.at[s, mine], cparts.at[s, mine], cp_ss.at[s, 3], cp_rs.at[s, 3, 0], sibling(1)))
        return out

    def up_copy(s):
        return copy(ulast.at[s], uprev.at[s], up_ss.at[s], up_rs.at[s], step_peer(1))

    def pp_copy(s):
        return copy(pprev.at[s], prevp.at[s], pp_ss.at[s], pp_rs.at[s], step_peer(7))

    def sel_copies(s):
        out = [
            copy(selm.at[s, eight(lax.rem(y + o, 4) * 2 + c)], rsel.at[s, y],
                 sel_ss.at[s, o - 1, c], sel_rs.at[s, o - 1], y_peer(o, c))
            for o in RING for c in (0, 1)
        ]
        return out + [copy(selm.at[s, eight(y * 2)], rsel.at[s, y], sel_ss.at[s, 3, 0], sel_rs.at[s, 3], sibling(0))]

    def dz_copies(s):
        out = [
            copy(dense.at[s, seg(lax.rem(zl + o, 4), c)], rz.at[s, i],
                 dz_ss.at[s, i, c], dz_rs.at[s, i], z_peer(o, c))
            for c in (0, 1) for i, o in enumerate((two[c], 1, 7))
        ]
        return out + [copy(dense.at[s, seg(zl, 0)], rz.at[s, 3], dz_ss.at[s, 3, 0], dz_rs.at[s, 3], sibling(0))]

    def xa_copies(s, c):
        out = [
            copy(xa.at[s, c, x], xa.at[s, c, x], xa_ss.at[s, o - 1], xa_rs.at[s, o - 1, c], x_peer(o, 1))
            for o in RING
        ]
        if c == 0:
            out.append(copy(xa.at[s, 0, x], xa.at[s, 0, x], xa_ss.at[s, 3], xa_rs.at[s, 3, 0], sibling(1)))
        return out

    def za_copies(s):
        return [
            copy(za.at[s], ta.at[s, 1], za_ss.at[s, 0], za_rs.at[s, 1], z_peer(4, 0)),
            copy(ta.at[s, 0], ta.at[s, 1], za_ss.at[s, 1], za_rs.at[s, 1], z_peer(4, 1)),
            copy(za.at[s], ta.at[s, 0], za_ss.at[s, 2], za_rs.at[s, 0], sibling(0)),
        ]

    def zb_copies(s, c):
        out = [copy(zb.at[s, c, 0], zb.at[s, c, 1], zb_ss.at[s, 0], zb_rs.at[s, 0, c], z_peer(4, 1))]
        if c == 0:
            out.append(copy(zb.at[s, 0, 0], zb.at[s, 0, 0], zb_ss.at[s, 1], zb_rs.at[s, 1, 0], sibling(1)))
        return out

    def xb_copies(s):
        out = []
        for o in RING:
            out.append(copy(xb.at[s], tb.at[s, x], xb_ss.at[s, o - 1, 0], xb_rs.at[s, o - 1], x_peer(o, 0)))
            out.append(copy(tb.at[s, x], tb.at[s, x], xb_ss.at[s, o - 1, 1], xb_rs.at[s, o - 1], x_peer(o, 1)))
        return out + [copy(xb.at[s], tb.at[s, x], xb_ss.at[s, 3, 0], xb_rs.at[s, 3], sibling(0))]

    def start(copies):
        for c in copies:
            c.start()

    def sent(copies):
        for c in copies:
            c.wait_send()

    def arrived(sems, like):
        for r in sems:
            pltpu.make_async_copy(like, like, r).wait()

    def by_core(f):
        pl.when(worker)(lambda: f(0))
        pl.when(hub)(lambda: f(1))

    both = [(i, c) for i in range(3) for c in (0, 1)] + [(3, 0)]

    loads = [
        pltpu.make_async_copy(src, dst, in_sem.at[i])
        for i, (src, dst) in enumerate((
            (rows_hbm, rows_ref), (cols_hbm, cols_ref), (cnt_hbm, cnt_ref), (mask_hbm, mask_ref),
        ))
    ] + [
        pltpu.make_async_copy(blocks_ref.at[k], blk.at[k], blk_sem.at[k])
        for k in (*range(BAND, SLOTS), *range(BAND))
    ]
    start(loads)

    barrier = pltpu.get_barrier_semaphore()

    def greet(c):
        if c == 0:
            peers = (
                [sibling(1), step_peer(7)] + [x_peer(o, 1) for o in range(1, 4)]
                + [y_peer(o, 1) for o in range(1, 4)] + [z_peer(o, 1) for o in (1, 2, 4, 6, 7)]
            )
        else:
            peers = (
                [sibling(0), step_peer(1)] + [z_peer(o, 1) for o in range(1, 8)]
                + [x_peer(o, d) for o in range(1, 4) for d in (0, 1)]
                + [y_peer(o, d) for o in range(1, 4) for d in (0, 1)]
                + [z_peer(o, 0) for o in (1, 2, 4, 6, 7)]
            )
        return peers

    def signal_peers(c):
        for dev in greet(c):
            pl.semaphore_signal(barrier, inc=1, device_id=dev, device_id_type=MESH)

    by_core(signal_peers)
    for c in loads[:4]:
        c.wait()

    live = cnt_ref[0]
    row_l = [lax.rem(rows_ref[k], RB) for k in range(SLOTS)]
    col_l = [cols_ref[k] - row * RB for k in range(BAND)]
    here = [(c >= 0) & (c < RB) for c in col_l]
    lane = lax.broadcasted_iota(jnp.int32, (8, 128), 1)
    iota8 = lax.broadcasted_iota(jnp.int32, (8, BS), 0)
    iota16 = lax.broadcasted_iota(jnp.int32, (RB, BS), 0)
    iota24 = lax.broadcasted_iota(jnp.int32, (RB + 8, BS), 0)

    idv = jnp.zeros((8, 128), jnp.int32)
    for k in range(IR_MAX):
        code = jnp.where(k < live, cols_ref[BAND + k] + 1, 0)
        idv = jnp.where(lane == yc * 8 + k, code, idv)
    ids[yc] = idv
    for q in range(4):
        keep[:, q * 128:(q + 1) * 128] = mask_ref[pl.ds(q, RB, stride=4), :].astype(F32)
    tbuf[0] = jnp.full((RB, BS), 4.0, F32)
    uloc[...] = jnp.zeros_like(uloc)

    def total_of(v):
        return jnp.sum(jnp.sum(v, axis=1, keepdims=True), axis=0, keepdims=True)

    sub = lax.broadcasted_iota(jnp.int32, (8, 128), 0)
    stat[...] = jnp.where(sub == 0, total_of(keep[...]), 0.0)

    def add_share(s, v):
        stat[...] += jnp.where(sub == s + 1, total_of(v), 0.0)

    def weights(s):
        u = jnp.where(keep[...] > 0, 4.0 / tbuf[s], 0.0)
        ubuf[s] = u
        tab[s, own] = u
        uloc[0:RB] = u
        ulast[s] = u[RB - 1:]

    def inter_columns(s):
        m = full_max(uloc[0:RB])
        inv = 1.0 / m
        acc = None
        for k in range(IR_MAX):
            vec = uloc[pl.ds(row_l[BAND + k], 1), :] * inv
            target = jnp.where(k < live, k, -1)
            lhs = split2(jnp.where(iota8 == target, vec, 0.0))
            part = jnp.dot(lhs, blk[BAND + k], preferred_element_type=F32)
            acc = part if acc is None else acc + part
        cparts[s, mine] = (acc[:8] + acc[8:]) * m

    def band_columns(s):
        m = full_max(uloc[0:RB])
        inv = 1.0 / m
        acc = None
        for k in range(BAND):
            vec = uloc[pl.ds(row_l[k], 1), :] * inv
            target = jnp.where(here[k], col_l[k], RB)
            lhs = split2(jnp.where(iota24 == target, vec, 0.0))
            part = jnp.dot(lhs, blk[k], preferred_element_type=F32)
            acc = part if acc is None else acc + part
        acc = (acc[:RB + 8] + acc[RB + 8:]) * m
        colband[...] = acc[:RB]
        pprev[s] = acc[RB:RB + 1]

    def first_columns():
        for c in loads[4:4 + IR_MAX]:
            c.wait()
        inter_columns(0)

    early = z < 4
    weights(0)

    @pl.when(early)
    def _():
        first_columns()

    def open_up(c):
        pl.semaphore_wait(barrier, len(greet(c)))
        start(tab_copies(0, c))
        up_copy(0).start()
        start(ids_copies(c))

    by_core(open_up)

    @pl.when(jnp.logical_not(early))
    def _():
        first_columns()

    by_core(lambda c: start(cp_copies(0, c)))
    for c in loads[4 + IR_MAX:]:
        c.wait()
    band_columns(0)
    pp_copy(0).start()

    def sweep(s, carry):
        last = s == SWEEPS - 1

        up_copy(s).wait_recv()
        uloc[RB:RB + 1] = uprev[s]
        m = full_max(uloc[...])
        inv = 1.0 / m
        acc = None
        for k in range(BAND):
            vec = uloc[pl.ds(jnp.where(here[k], col_l[k], RB), 1), :] * inv
            lhs = split2(jnp.where(iota16 == row_l[k], vec, 0.0))
            part = lax.dot_general(
                lhs, blk[k], (((1,), (1,)), ((), ())), preferred_element_type=F32
            )
            acc = part if acc is None else acc + part
        rowband[...] = (acc[:RB] + acc[RB:]) * m

        @pl.when(worker)
        def _():
            add_share(s, uloc[0:RB] * rowband[...])

            @pl.when(last)
            def _():
                copy(stat, wstat, ws_ss, ws_rs, sibling(1)).start()

        @pl.when(hub)
        def _():
            @pl.when(s == 0)
            def _():
                arrived([ids_rs.at[i, c] for i, c in both], ids.at[0])
                code = ids[0]
                for p in range(1, 8):
                    code = code + ids[p]
                code = code[0:1]
                cc = jnp.maximum(code - 1, 0)
                want = jnp.where(
                    (code > 0) & (((cc // 32) % 4) == y), (cc // 128) * 32 + cc % 32, -1
                )
                full = jnp.where(
                    lax.broadcasted_iota(jnp.int32, (128, 128), 0) == want, 1.0, 0.0
                )
                pick[...] = full[:, :SEL].astype(BF16)
                pickt[...] = full.T[:SEL].astype(BF16)

            arrived([tab_rs.at[s, i, c] for i, c in both], tab.at[s, own])
            selm[s] = exact_pick(pickt[...], tab[s])
            start(sel_copies(s))
            rsel[s, y] = selm[s, mine]

            arrived([cp_rs.at[s, i, c] for i, c in both], cparts.at[s, mine])
            dense[s] = exact_pick(pick[...], cparts[s])
            start(dz_copies(s))
            rz[s, 3] = dense[s, own]

            @pl.when(last)
            def _():
                arrived([ws_rs], wstat)
                add_share(s, dense[s] * tab[s])
                add_share(s, uloc[0:RB] * rowband[...])
                stz[z] = stat[...] + wstat[...]
                for o in range(1, 8):
                    copy(stz.at[z], stz.at[z], sz_ss.at[o - 1], sz_rs.at[o - 1], z_peer(o, 1)).start()

        arrived([sel_rs.at[s, i] for i in range(3)], rsel.at[s, 0])
        pl.when(worker)(lambda: arrived([sel_rs.at[s, 3]], rsel.at[s, 0]))
        ucol = (rsel[s, 0] + rsel[s, 1]) + (rsel[s, 2] + rsel[s, 3])
        m2 = full_max(ucol)
        ucol = ucol * (1.0 / m2)
        acc = None
        for k in range(IR_MAX):
            target = jnp.where(k < live, row_l[BAND + k], -1)
            lhs = split2(jnp.where(iota16 == target, ucol[k:k + 1], 0.0))
            part = lax.dot_general(
                lhs, blk[BAND + k], (((1,), (1,)), ((), ())), preferred_element_type=F32
            )
            acc = part if acc is None else acc + part
        total = (acc[:RB] + acc[RB:]) * m2 + rowband[...] + colband[...]

        pp_copy(s).wait_recv()
        total = total + jnp.where(iota16 == RB - 1, prevp[s], 0.0)
        arrived([dz_rs.at[s, i] for i in range(3)], rz.at[s, 0])
        pl.when(worker)(lambda: arrived([dz_rs.at[s, 3]], rz.at[s, 0]))
        total = total + ((rz[s, 0] + rz[s, 1]) + (rz[s, 2] + rz[s, 3]))

        zb[s, core, 0] = total[:, half:]
        by_core(lambda c: start(zb_copies(s, c)))
        xa[s, core, x] = total[:, :half]
        by_core(lambda c: start(xa_copies(s, c)))

        @pl.when(worker)
        def _():
            sent([*tab_copies(s, 0), up_copy(s), *cp_copies(s, 0), pp_copy(s)])

        @pl.when(hub)
        def _():
            @pl.when(jnp.logical_not(last))
            def _():
                add_share(s, dense[s] * tab[s])
                add_share(s, uloc[0:RB] * rowband[...])

            @pl.when(last)
            def _():
                for o in range(1, 8):
                    copy(stz.at[z], stz.at[z], sz_ss.at[o - 1], sz_rs.at[o - 1], z_peer(o, 1)).wait()
                v = stz[0]
                for p in range(1, 8):
                    v = v + stz[p]
                sty[y] = v
                for o in RING:
                    copy(sty.at[y], sty.at[y], sy_ss.at[o - 1], sy_rs.at[o - 1], y_peer(o, 1)).start()

            sent([*tab_copies(s, 1), up_copy(s), *cp_copies(s, 1), pp_copy(s), *sel_copies(s), *dz_copies(s)])

            arrived([xa_rs.at[s, i, c] for i, c in both], xa.at[s, 0, 0])
            za[s] = (xa[s, 0, 0] + xa[s, 0, 1]) + (xa[s, 0, 2] + xa[s, 0, 3])
            ta[s, 0] = (xa[s, 1, 0] + xa[s, 1, 1]) + (xa[s, 1, 2] + xa[s, 1, 3])
            start(za_copies(s))
            arrived([zb_rs.at[s, 0, 0], zb_rs.at[s, 0, 1], zb_rs.at[s, 1, 0]], zb.at[s, 0, 0])
            xb[s] = zb[s, 0, 0] + zb[s, 0, 1]
            tb[s, x] = zb[s, 1, 0] + zb[s, 1, 1]
            start(xb_copies(s))

            @pl.when(last)
            def _():
                for o in RING:
                    copy(sty.at[y], sty.at[y], sy_ss.at[o - 1], sy_rs.at[o - 1], y_peer(o, 1)).wait()
                stx[x] = (sty[0] + sty[1]) + (sty[2] + sty[3])
                for o in RING:
                    copy(stx.at[x], stx.at[x], sx_ss.at[o - 1], sx_rs.at[o - 1], x_peer(o, 1)).start()

            sent([*za_copies(s), *xb_copies(s)])

        by_core(lambda c: sent([*xa_copies(s, c), *zb_copies(s, c)]))
        arrived([xb_rs.at[s, i] for i in range(3)], tb.at[s, 0])
        pl.when(worker)(lambda: arrived([xb_rs.at[s, 3], za_rs.at[s, 0]], tb.at[s, 0]))
        arrived([za_rs.at[s, 1]], tb.at[s, 0])
        tbuf[s + 1, :, :half] = ta[s, 0] + ta[s, 1]
        tbuf[s + 1, :, half:] = (tb[s, 0] + tb[s, 1]) + (tb[s, 2] + tb[s, 3])

        @pl.when(s < SWEEPS - 1)
        def _():
            n = s + 1
            weights(n)
            by_core(lambda c: start(tab_copies(n, c)))
            up_copy(n).start()
            inter_columns(n)
            by_core(lambda c: start(cp_copies(n, c)))
            band_columns(n)
            pp_copy(n).start()

        return carry

    lax.fori_loop(0, SWEEPS, sweep, 0)

    @pl.when(hub)
    def _():
        for o in RING:
            copy(stx.at[x], stx.at[x], sx_ss.at[o - 1], sx_rs.at[o - 1], x_peer(o, 1)).wait()
        fin[...] = (stx[0] + stx[1]) + (stx[2] + stx[3])
        c = copy(fin, fin, fin_ss, fin_rs, sibling(0))
        c.start()
        c.wait_send()
        sent(ids_copies(1))

    @pl.when(worker)
    def _():
        sent([copy(stat, wstat, ws_ss, ws_rs, sibling(1)), *ids_copies(0)])
        arrived([fin_rs], fin)

    v = fin[...]
    count = v[0:1, 0:1] * 0.125
    mean1 = v[1:2, 0:1] * 2.0 / count
    mean2 = v[2:3, 0:1] * 2.0 / count
    mean3 = v[3:4, 0:1] * 2.0 / count
    scale = mean1 * mean2 * 0.0625 * mean3
    b3 = tbuf[SWEEPS]
    bias = jnp.where(keep[...] > 0, b3 / scale, 1.0)
    balance = b3 * ubuf[SWEEPS - 1] / mean3
    for q in range(4):
        bias_ref[pl.ds(q, RB, stride=4), :] = bias[:, q * 128:(q + 1) * 128]
        bal_ref[pl.ds(q, RB, stride=4), :] = balance[:, q * 128:(q + 1) * 128]


def body(blocks, block_rows, block_cols, inter_counts, keep_mask):
    seg = keep_mask.shape[0]
    vm = pl.BlockSpec(memory_space=pltpu.VMEM)
    hbm = pl.BlockSpec(memory_space=pl.ANY)
    S = SWEEPS
    H = BS // 2
    dma = pltpu.SemaphoreType.DMA
    i32 = jnp.int32
    out = jax.ShapeDtypeStruct((seg // 128, 128), F32)

    def vf(*shape):
        return pltpu.VMEM(shape, F32)

    bias, balance = pl.pallas_call(
        kernel,
        out_shape=(out, out),
        in_specs=[hbm] * 5,
        out_specs=(vm, vm),
        scratch_shapes=[
            pltpu.SMEM((SLOTS,), i32),
            pltpu.SMEM((SLOTS,), i32),
            pltpu.SMEM((1,), i32),
            pltpu.VMEM((seg // 128, 128), i32),
            pltpu.VMEM((SLOTS, BS, BS), BF16),
            vf(RB, BS),
            vf(S + 1, RB, BS),
            vf(S, RB, BS),
            vf(RB + 8, BS),
            pltpu.VMEM((8, 8, 128), i32),
            pltpu.VMEM((128, SEL), BF16),
            pltpu.VMEM((SEL, 128), BF16),
            vf(8, 128),
            vf(RB, BS),
            vf(RB, BS),
            vf(S, 128, BS),
            vf(S, SEL, BS),
            vf(S, 4, 8, BS),
            vf(S, 1, BS),
            vf(S, 1, BS),
            vf(S, SEL, BS),
            vf(S, 1, BS),
            vf(S, 1, BS),
            vf(S, 128, BS),
            vf(S, 4, RB, BS),
            vf(S, 2, 4, RB, H),
            vf(S, RB, H),
            vf(S, 2, RB, H),
            vf(S, 2, 2, RB, H),
            vf(S, RB, H),
            vf(S, 4, RB, H),
            vf(8, 128),
            vf(8, 8, 128),
            vf(4, 8, 128),
            vf(4, 8, 128),
            vf(8, 128),
            dma((4,)),
            dma((SLOTS,)),
            dma((4,)), dma((4, 2)),
            dma((S, 4)), dma((S, 4, 2)),
            dma((S, 4, 2)), dma((S, 4)),
            dma((S,)), dma((S,)),
            dma((S, 4)), dma((S, 4, 2)),
            dma((S,)), dma((S,)),
            dma((S, 4, 2)), dma((S, 4)),
            dma((S, 4)), dma((S, 4, 2)),
            dma((S, 3)), dma((S, 2)),
            dma((S, 2)), dma((S, 2, 2)),
            dma((S, 4, 2)), dma((S, 4)),
            dma, dma,
            dma((7,)), dma((7,)),
            dma((3,)), dma((3,)),
            dma((3,)), dma((3,)),
            dma, dma,
        ],
        compiler_params=pltpu.CompilerParams(
            collective_id=0, has_side_effects=True, vmem_limit_bytes=VMEM_LIMIT
        ),
        name="balance",
    )(block_rows, block_cols, inter_counts, keep_mask.reshape(seg // 128, 128), blocks)
    return bias.reshape(seg), balance.reshape(seg)


def solution(mesh):
    return jax.shard_map(
        body,
        mesh=mesh,
        in_specs=(
            P(("row", "col"), None, None),
            P(("row", "col")),
            P(("row", "col")),
            P(("row", "col")),
            P("row"),
        ),
        out_specs=(P("row"), P("row")),
        check_vma=False,
    )
```

```python
import jax
import jax.numpy as jnp
from jax import lax
from jax.experimental import pallas as pl
from jax.experimental.pallas import tpu as pltpu
from jax.sharding import PartitionSpec as P

IR_MAX = 8
SWEEPS = 3
RB = 16
BS = 512
SLOTS = 12
BAND = SLOTS - IR_MAX
SEL = 64
VMEM_LIMIT = 58 * 2**20

F32 = jnp.float32
BF16 = jnp.bfloat16
MESH = pl.DeviceIdType.MESH
RING = (2, 1, 3)


def split2(v):
    hi = v.astype(BF16)
    lo = (v - hi.astype(F32)).astype(BF16)
    return jnp.concatenate([hi, lo], axis=0)


def two_term_pick(pick, v):
    hi = v.astype(BF16)
    lo = (v - hi.astype(F32)).astype(BF16)
    return jnp.dot(pick, hi, preferred_element_type=F32) + jnp.dot(pick, lo, preferred_element_type=F32)


def full_max(v):
    m = jnp.max(jnp.max(v, axis=1, keepdims=True), axis=0, keepdims=True)
    return jnp.where(m > 0, m, 1.0)


def kernel(
    rows_hbm, cols_hbm, cnt_hbm, mask_hbm, blocks_ref,
    out_ref,
    rows_ref, cols_ref, cnt_ref, mask_ref,
    blk, blkt, keep, tbuf, ubuf, uloc, ids, pick, pickt, stat, rowband, colband,
    tab, selm, rsel, ulast, uprev, cparts, pprev, prevp, dense, rz,
    xa, za, ta, zb, xb, tb, wstat, stz, sty, stx,
    in_sem, blk_sem, ids_ss, ids_rs, tab_ss, tab_rs, sel_ss, sel_rs, up_ss, up_rs,
    cp_ss, cp_rs, pp_ss, pp_rs, dz_ss, dz_rs, xa_ss, xa_rs, za_ss, za_rs,
    zb_ss, zb_rs, xb_ss, xb_rs, ws_ss, ws_rs,
    sz_ss, sz_rs, sy_ss, sy_rs, sx_ss, sx_rs,
):
    row = lax.axis_index("row")
    col = lax.axis_index("col")
    zl = row // 8
    yc = lax.rem(row, 8)
    y = yc // 2
    core = lax.rem(row, 2)
    x = col // 2
    zh = lax.rem(col, 2)
    z = zh * 4 + zl
    half = BS // 2
    hub = core == 1
    worker = core == 0
    inner = jnp.where(zl < 2, 2, 6)
    two = (inner, 8 - inner)

    def chip(xx, yy, zz, cc):
        return (lax.rem(zz, 4) * 8 + yy * 2 + cc, xx * 2 + zz // 4)

    def z_peer(o, c):
        return chip(x, y, lax.rem(z + o, 8), c)

    def y_peer(o, c):
        return chip(x, lax.rem(y + o, 4), z, c)

    def x_peer(o, c):
        return chip(lax.rem(x + o, 4), y, z, c)

    def sibling(c):
        return chip(x, y, z, c)

    def step_peer(o):
        wrap = 7 if o == 1 else 0
        q = jnp.where(yc == wrap, lax.rem(z + o, 8), z)
        return (lax.rem(q, 4) * 8 + lax.rem(yc + o, 8), x * 2 + q // 4)

    def copy(src, dst, ss, rs, dev):
        return pltpu.make_async_remote_copy(
            src_ref=src, dst_ref=dst, send_sem=ss, recv_sem=rs,
            device_id=dev, device_id_type=MESH,
        )

    def seg(q, c):
        return pl.ds(pl.multiple_of(q * 2 * RB + c * RB, RB), RB)

    def eight(i):
        return pl.ds(pl.multiple_of(i * 8, 8), 8)

    own = seg(zl, core)
    mine = eight(yc)

    def tab_copies(s, c):
        out = [
            copy(tab.at[s, own], tab.at[s, own], tab_ss.at[s, i], tab_rs.at[s, i, c], z_peer(o, 1))
            for i, o in enumerate((two[c], 1, 7))
        ]
        if c == 0:
            out.append(copy(tab.at[s, own], tab.at[s, own], tab_ss.at[s, 3], tab_rs.at[s, 3, 0], sibling(1)))
        return out

    def ids_copies(c):
        out = [copy(ids.at[yc], ids.at[yc], ids_ss.at[o - 1], ids_rs.at[o - 1, c], y_peer(o, 1)) for o in RING]
        if c == 0:
            out.append(copy(ids.at[yc], ids.at[yc], ids_ss.at[3], ids_rs.at[3, 0], sibling(1)))
        return out

    def cp_copies(s, c):
        out = [
            copy(cparts.at[s, mine], cparts.at[s, mine], cp_ss.at[s, o - 1], cp_rs.at[s, o - 1, c], y_peer(o, 1))
            for o in RING
        ]
        if c == 0:
            out.append(copy(cparts.at[s, mine], cparts.at[s, mine], cp_ss.at[s, 3], cp_rs.at[s, 3, 0], sibling(1)))
        return out

    def up_copy(s):
        return copy(ulast.at[s], uprev.at[s], up_ss.at[s], up_rs.at[s], step_peer(1))

    def pp_copy(s):
        return copy(pprev.at[s], prevp.at[s], pp_ss.at[s], pp_rs.at[s], step_peer(7))

    def sel_copies(s):
        out = [
            copy(selm.at[s, eight(lax.rem(y + o, 4) * 2 + c)], rsel.at[s, y],
                 sel_ss.at[s, o - 1, c], sel_rs.at[s, o - 1], y_peer(o, c))
            for o in RING for c in (0, 1)
        ]
        return out + [copy(selm.at[s, eight(y * 2)], rsel.at[s, y], sel_ss.at[s, 3, 0], sel_rs.at[s, 3], sibling(0))]

    def dz_copies(s):
        out = [
            copy(dense.at[s, seg(lax.rem(zl + o, 4), c)], rz.at[s, i],
                 dz_ss.at[s, i, c], dz_rs.at[s, i], z_peer(o, c))
            for c in (0, 1) for i, o in enumerate((two[c], 1, 7))
        ]
        return out + [copy(dense.at[s, seg(zl, 0)], rz.at[s, 3], dz_ss.at[s, 3, 0], dz_rs.at[s, 3], sibling(0))]

    def xa_copies(s, c):
        out = [
            copy(xa.at[s, c, x], xa.at[s, c, x], xa_ss.at[s, o - 1], xa_rs.at[s, o - 1, c], x_peer(o, 1))
            for o in RING
        ]
        if c == 0:
            out.append(copy(xa.at[s, 0, x], xa.at[s, 0, x], xa_ss.at[s, 3], xa_rs.at[s, 3, 0], sibling(1)))
        return out

    def za_copies(s):
        return [
            copy(za.at[s], ta.at[s, 1], za_ss.at[s, 0], za_rs.at[s, 1], z_peer(4, 0)),
            copy(ta.at[s, 0], ta.at[s, 1], za_ss.at[s, 1], za_rs.at[s, 1], z_peer(4, 1)),
            copy(za.at[s], ta.at[s, 0], za_ss.at[s, 2], za_rs.at[s, 0], sibling(0)),
        ]

    def zb_copies(s, c):
        out = [copy(zb.at[s, c, 0], zb.at[s, c, 1], zb_ss.at[s, 0], zb_rs.at[s, 0, c], z_peer(4, 1))]
        if c == 0:
            out.append(copy(zb.at[s, 0, 0], zb.at[s, 0, 0], zb_ss.at[s, 1], zb_rs.at[s, 1, 0], sibling(1)))
        return out

    def xb_copies(s):
        out = []
        for o in RING:
            out.append(copy(xb.at[s], tb.at[s, x], xb_ss.at[s, o - 1, 0], xb_rs.at[s, o - 1], x_peer(o, 0)))
            out.append(copy(tb.at[s, x], tb.at[s, x], xb_ss.at[s, o - 1, 1], xb_rs.at[s, o - 1], x_peer(o, 1)))
        return out + [copy(xb.at[s], tb.at[s, x], xb_ss.at[s, 3, 0], xb_rs.at[s, 3], sibling(0))]

    def sx_copies():
        out = [
            copy(stx.at[x], stx.at[x], sx_ss.at[o - 1, c], sx_rs.at[o - 1], x_peer(o, c))
            for o in RING for c in (0, 1)
        ]
        return out + [copy(stx.at[x], stx.at[x], sx_ss.at[3, 0], sx_rs.at[3], sibling(0))]

    def start(copies):
        for c in copies:
            c.start()

    def sent(copies):
        for c in copies:
            c.wait_send()

    def arrived(sems, like):
        for r in sems:
            pltpu.make_async_copy(like, like, r).wait()

    def by_core(f):
        pl.when(worker)(lambda: f(0))
        pl.when(hub)(lambda: f(1))

    both = [(i, c) for i in range(3) for c in (0, 1)] + [(3, 0)]

    loads = [
        pltpu.make_async_copy(src, dst, in_sem.at[i])
        for i, (src, dst) in enumerate((
            (rows_hbm, rows_ref), (cols_hbm, cols_ref), (cnt_hbm, cnt_ref), (mask_hbm, mask_ref),
        ))
    ] + [
        pltpu.make_async_copy(blocks_ref.at[k], blk.at[k], blk_sem.at[k])
        for k in (*range(BAND, SLOTS), *range(BAND))
    ]
    start(loads)

    barrier = pltpu.get_barrier_semaphore()

    def greet(c):
        if c == 0:
            peers = (
                [sibling(1), step_peer(7)] + [x_peer(o, 1) for o in range(1, 4)]
                + [y_peer(o, 1) for o in range(1, 4)] + [z_peer(o, 1) for o in (1, 2, 4, 6, 7)]
            )
        else:
            peers = (
                [sibling(0), step_peer(1)] + [z_peer(o, 1) for o in range(1, 8)]
                + [x_peer(o, d) for o in range(1, 4) for d in (0, 1)]
                + [y_peer(o, d) for o in range(1, 4) for d in (0, 1)]
                + [z_peer(o, 0) for o in (1, 2, 4, 6, 7)]
            )
        return peers

    def signal_peers(c):
        for dev in greet(c):
            pl.semaphore_signal(barrier, inc=1, device_id=dev, device_id_type=MESH)

    by_core(signal_peers)
    for c in loads[:4]:
        c.wait()

    live = cnt_ref[0]
    row_l = [lax.rem(rows_ref[k], RB) for k in range(SLOTS)]
    col_l = [cols_ref[k] - row * RB for k in range(BAND)]
    here = [(c >= 0) & (c < RB) for c in col_l]
    lane = lax.broadcasted_iota(jnp.int32, (8, 128), 1)
    iota8 = lax.broadcasted_iota(jnp.int32, (8, BS), 0)
    iota16 = lax.broadcasted_iota(jnp.int32, (RB, BS), 0)
    iota24 = lax.broadcasted_iota(jnp.int32, (RB + 8, BS), 0)

    idv = jnp.zeros((8, 128), jnp.int32)
    for k in range(IR_MAX):
        code = jnp.where(k < live, cols_ref[BAND + k] + 1, 0)
        idv = jnp.where(lane == yc * 8 + k, code, idv)
    ids[yc] = idv
    for q in range(4):
        keep[:, q * 128:(q + 1) * 128] = mask_ref[pl.ds(q, RB, stride=4), :].astype(F32)
    tbuf[0] = jnp.full((RB, BS), 4.0, F32)
    uloc[...] = jnp.zeros_like(uloc)

    def total_of(v):
        return jnp.sum(jnp.sum(v, axis=1, keepdims=True), axis=0, keepdims=True)

    sub = lax.broadcasted_iota(jnp.int32, (8, 128), 0)
    stat[...] = jnp.where(sub == 0, total_of(keep[...]), 0.0)

    def add_share(s, v):
        stat[...] += jnp.where(sub == s + 1, total_of(v), 0.0)

    def weights(s):
        u = jnp.where(keep[...] > 0, 4.0 / tbuf[s], 0.0)
        ubuf[s] = u
        tab[s, own] = u
        uloc[0:RB] = u
        ulast[s] = u[RB - 1:]

    def inter_columns(s):
        m = full_max(uloc[0:RB])
        inv = 1.0 / m
        acc = None
        for k in range(IR_MAX):
            vec = uloc[pl.ds(row_l[BAND + k], 1), :] * inv
            target = jnp.where(k < live, k, -1)
            lhs = split2(jnp.where(iota8 == target, vec, 0.0))
            part = jnp.dot(lhs, blk[BAND + k], preferred_element_type=F32)
            acc = part if acc is None else acc + part
        cparts[s, mine] = (acc[:8] + acc[8:]) * m

    def band_columns(s):
        m = full_max(uloc[0:RB])
        inv = 1.0 / m
        acc = None
        for k in range(BAND):
            vec = uloc[pl.ds(row_l[k], 1), :] * inv
            target = jnp.where(here[k], col_l[k], RB)
            lhs = split2(jnp.where(iota24 == target, vec, 0.0))
            part = jnp.dot(lhs, blk[k], preferred_element_type=F32)
            acc = part if acc is None else acc + part
        acc = (acc[:RB + 8] + acc[RB + 8:]) * m
        colband[...] = acc[:RB]
        pprev[s] = acc[RB:RB + 1]

    def first_columns():
        for c in loads[4:4 + IR_MAX]:
            c.wait()
        inter_columns(0)

    def transpose_inter():
        def one(k, carry):
            blkt[k] = blk[BAND + k].T
            return carry

        lax.fori_loop(0, IR_MAX, one, 0)

    early = z < 4
    weights(0)

    @pl.when(early)
    def _():
        first_columns()
        transpose_inter()

    def open_up(c):
        pl.semaphore_wait(barrier, len(greet(c)))
        start(tab_copies(0, c))
        up_copy(0).start()
        start(ids_copies(c))

    by_core(open_up)

    @pl.when(jnp.logical_not(early))
    def _():
        first_columns()

    by_core(lambda c: start(cp_copies(0, c)))
    for c in loads[4 + IR_MAX:]:
        c.wait()
    band_columns(0)
    pp_copy(0).start()

    @pl.when(jnp.logical_not(early))
    def _():
        transpose_inter()

    def sweep(s, carry):
        last = s == SWEEPS - 1

        up_copy(s).wait_recv()
        uloc[RB:RB + 1] = uprev[s]
        m = full_max(uloc[...])
        inv = 1.0 / m
        acc = None
        for k in range(BAND):
            vec = uloc[pl.ds(jnp.where(here[k], col_l[k], RB), 1), :] * inv
            lhs = split2(jnp.where(iota16 == row_l[k], vec, 0.0))
            part = lax.dot_general(
                lhs, blk[k], (((1,), (1,)), ((), ())), preferred_element_type=F32
            )
            acc = part if acc is None else acc + part
        rowband[...] = (acc[:RB] + acc[RB:]) * m

        @pl.when(worker)
        def _():
            add_share(s, uloc[0:RB] * rowband[...])

            @pl.when(last)
            def _():
                copy(stat, wstat, ws_ss, ws_rs, sibling(1)).start()

        @pl.when(hub)
        def _():
            @pl.when(s == 0)
            def _():
                arrived([ids_rs.at[i, c] for i, c in both], ids.at[0])
                code = ids[0]
                for p in range(1, 8):
                    code = code + ids[p]
                code = code[0:1]
                cc = jnp.maximum(code - 1, 0)
                want = jnp.where(
                    (code > 0) & (((cc // 32) % 4) == y), (cc // 128) * 32 + cc % 32, -1
                )
                full = jnp.where(
                    lax.broadcasted_iota(jnp.int32, (128, 128), 0) == want, 1.0, 0.0
                )
                pick[...] = full[:, :SEL].astype(BF16)
                pickt[...] = full.T[:SEL].astype(BF16)

            arrived([tab_rs.at[s, i, c] for i, c in both], tab.at[s, own])
            selm[s] = two_term_pick(pickt[...], tab[s])
            start(sel_copies(s))
            rsel[s, y] = selm[s, mine]

            arrived([cp_rs.at[s, i, c] for i, c in both], cparts.at[s, mine])
            dense[s] = two_term_pick(pick[...], cparts[s])
            start(dz_copies(s))
            rz[s, 3] = dense[s, own]

            @pl.when(last)
            def _():
                arrived([ws_rs], wstat)
                add_share(s, dense[s] * tab[s])
                add_share(s, uloc[0:RB] * rowband[...])
                stz[z] = stat[...] + wstat[...]
                for o in range(1, 8):
                    copy(stz.at[z], stz.at[z], sz_ss.at[o - 1], sz_rs.at[o - 1], z_peer(o, 1)).start()

        arrived([sel_rs.at[s, i] for i in range(3)], rsel.at[s, 0])
        pl.when(worker)(lambda: arrived([sel_rs.at[s, 3]], rsel.at[s, 0]))
        ucol = (rsel[s, 0] + rsel[s, 1]) + (rsel[s, 2] + rsel[s, 3])
        m2 = full_max(ucol)
        ucol = ucol * (1.0 / m2)
        acc = None
        for k in range(IR_MAX):
            target = jnp.where(k < live, row_l[BAND + k], -1)
            lhs = split2(jnp.where(iota16 == target, ucol[k:k + 1], 0.0))
            part = jnp.dot(lhs, blkt[k], preferred_element_type=F32)
            acc = part if acc is None else acc + part
        total = (acc[:RB] + acc[RB:]) * m2 + rowband[...] + colband[...]

        pp_copy(s).wait_recv()
        total = total + jnp.where(iota16 == RB - 1, prevp[s], 0.0)
        arrived([dz_rs.at[s, i] for i in range(3)], rz.at[s, 0])
        pl.when(worker)(lambda: arrived([dz_rs.at[s, 3]], rz.at[s, 0]))
        total = total + ((rz[s, 0] + rz[s, 1]) + (rz[s, 2] + rz[s, 3]))

        zb[s, core, 0] = total[:, half:]
        by_core(lambda c: start(zb_copies(s, c)))
        xa[s, core, x] = total[:, :half]
        by_core(lambda c: start(xa_copies(s, c)))

        @pl.when(worker)
        def _():
            sent([*tab_copies(s, 0), up_copy(s), *cp_copies(s, 0), pp_copy(s)])

        @pl.when(hub)
        def _():
            @pl.when(jnp.logical_not(last))
            def _():
                add_share(s, dense[s] * tab[s])
                add_share(s, uloc[0:RB] * rowband[...])

            @pl.when(last)
            def _():
                for o in range(1, 8):
                    copy(stz.at[z], stz.at[z], sz_ss.at[o - 1], sz_rs.at[o - 1], z_peer(o, 1)).wait()
                v = stz[0]
                for p in range(1, 8):
                    v = v + stz[p]
                sty[y] = v
                for o in RING:
                    copy(sty.at[y], sty.at[y], sy_ss.at[o - 1], sy_rs.at[o - 1], y_peer(o, 1)).start()

            sent([*tab_copies(s, 1), up_copy(s), *cp_copies(s, 1), pp_copy(s), *sel_copies(s), *dz_copies(s)])

            arrived([xa_rs.at[s, i, c] for i, c in both], xa.at[s, 0, 0])
            za[s] = (xa[s, 0, 0] + xa[s, 0, 1]) + (xa[s, 0, 2] + xa[s, 0, 3])
            ta[s, 0] = (xa[s, 1, 0] + xa[s, 1, 1]) + (xa[s, 1, 2] + xa[s, 1, 3])
            start(za_copies(s))
            arrived([zb_rs.at[s, 0, 0], zb_rs.at[s, 0, 1], zb_rs.at[s, 1, 0]], zb.at[s, 0, 0])
            xb[s] = zb[s, 0, 0] + zb[s, 0, 1]
            tb[s, x] = zb[s, 1, 0] + zb[s, 1, 1]
            start(xb_copies(s))

            @pl.when(last)
            def _():
                for o in RING:
                    copy(sty.at[y], sty.at[y], sy_ss.at[o - 1], sy_rs.at[o - 1], y_peer(o, 1)).wait()
                stx[x] = (sty[0] + sty[1]) + (sty[2] + sty[3])
                start(sx_copies())

            sent([*za_copies(s), *xb_copies(s)])

        by_core(lambda c: sent([*xa_copies(s, c), *zb_copies(s, c)]))
        arrived([xb_rs.at[s, i] for i in range(3)], tb.at[s, 0])
        pl.when(worker)(lambda: arrived([xb_rs.at[s, 3], za_rs.at[s, 0]], tb.at[s, 0]))
        arrived([za_rs.at[s, 1]], tb.at[s, 0])
        tbuf[s + 1, :, :half] = ta[s, 0] + ta[s, 1]
        tbuf[s + 1, :, half:] = (tb[s, 0] + tb[s, 1]) + (tb[s, 2] + tb[s, 3])

        @pl.when(s < SWEEPS - 1)
        def _():
            n = s + 1
            weights(n)
            by_core(lambda c: start(tab_copies(n, c)))
            up_copy(n).start()
            inter_columns(n)
            by_core(lambda c: start(cp_copies(n, c)))
            band_columns(n)
            pp_copy(n).start()

        return carry

    lax.fori_loop(0, SWEEPS, sweep, 0)

    arrived([sx_rs.at[i] for i in range(3)], stx.at[0])

    @pl.when(hub)
    def _():
        sent([*ids_copies(1), *sx_copies()])

    @pl.when(worker)
    def _():
        sent([copy(stat, wstat, ws_ss, ws_rs, sibling(1)), *ids_copies(0)])
        arrived([sx_rs.at[3]], stx.at[0])

    v = (stx[0] + stx[1]) + (stx[2] + stx[3])
    count = v[0:1, 0:1] * 0.125
    mean1 = v[1:2, 0:1] * 2.0 / count
    mean2 = v[2:3, 0:1] * 2.0 / count
    mean3 = v[3:4, 0:1] * 2.0 / count
    scale = mean1 * mean2 * 0.0625 * mean3
    b3 = tbuf[SWEEPS]
    bias = jnp.where(keep[...] > 0, b3 / scale, 1.0)
    balance = b3 * ubuf[SWEEPS - 1] / mean3
    for q in range(4):
        out_ref[pl.ds(q, RB, stride=4), :] = bias[:, q * 128:(q + 1) * 128]
        out_ref[pl.ds(4 * RB + q, RB, stride=4), :] = balance[:, q * 128:(q + 1) * 128]


def body(blocks, block_rows, block_cols, inter_counts, keep_mask):
    seg = keep_mask.shape[0]
    vm = pl.BlockSpec(memory_space=pltpu.VMEM)
    hbm = pl.BlockSpec(memory_space=pl.ANY)
    S = SWEEPS
    H = BS // 2
    dma = pltpu.SemaphoreType.DMA
    i32 = jnp.int32
    out = jax.ShapeDtypeStruct((seg // 64, 128), F32)

    def vf(*shape):
        return pltpu.VMEM(shape, F32)

    both = pl.pallas_call(
        kernel,
        out_shape=out,
        in_specs=[hbm] * 5,
        out_specs=vm,
        scratch_shapes=[
            pltpu.SMEM((SLOTS,), i32),
            pltpu.SMEM((SLOTS,), i32),
            pltpu.SMEM((1,), i32),
            pltpu.VMEM((seg // 128, 128), i32),
            pltpu.VMEM((SLOTS, BS, BS), BF16),
            pltpu.VMEM((IR_MAX, BS, BS), BF16),
            vf(RB, BS),
            vf(S + 1, RB, BS),
            vf(S, RB, BS),
            vf(RB + 8, BS),
            pltpu.VMEM((8, 8, 128), i32),
            pltpu.VMEM((128, SEL), BF16),
            pltpu.VMEM((SEL, 128), BF16),
            vf(8, 128),
            vf(RB, BS),
            vf(RB, BS),
            vf(S, 128, BS),
            vf(S, SEL, BS),
            vf(S, 4, 8, BS),
            vf(S, 1, BS),
            vf(S, 1, BS),
            vf(S, SEL, BS),
            vf(S, 1, BS),
            vf(S, 1, BS),
            vf(S, 128, BS),
            vf(S, 4, RB, BS),
            vf(S, 2, 4, RB, H),
            vf(S, RB, H),
            vf(S, 2, RB, H),
            vf(S, 2, 2, RB, H),
            vf(S, RB, H),
            vf(S, 4, RB, H),
            vf(8, 128),
            vf(8, 8, 128),
            vf(4, 8, 128),
            vf(4, 8, 128),
            dma((4,)),
            dma((SLOTS,)),
            dma((4,)), dma((4, 2)),
            dma((S, 4)), dma((S, 4, 2)),
            dma((S, 4, 2)), dma((S, 4)),
            dma((S,)), dma((S,)),
            dma((S, 4)), dma((S, 4, 2)),
            dma((S,)), dma((S,)),
            dma((S, 4, 2)), dma((S, 4)),
            dma((S, 4)), dma((S, 4, 2)),
            dma((S, 3)), dma((S, 2)),
            dma((S, 2)), dma((S, 2, 2)),
            dma((S, 4, 2)), dma((S, 4)),
            dma, dma,
            dma((7,)), dma((7,)),
            dma((3,)), dma((3,)),
            dma((4, 2)), dma((4,)),
        ],
        compiler_params=pltpu.CompilerParams(
            collective_id=0, has_side_effects=True, vmem_limit_bytes=VMEM_LIMIT
        ),
        name="balance",
    )(block_rows, block_cols, inter_counts, keep_mask.reshape(seg // 128, 128), blocks)
    bias, balance = both[:seg // 128], both[seg // 128:]
    return bias.reshape(seg), balance.reshape(seg)


def solution(mesh):
    return jax.shard_map(
        body,
        mesh=mesh,
        in_specs=(
            P(("row", "col"), None, None),
            P(("row", "col")),
            P(("row", "col")),
            P(("row", "col")),
            P("row"),
        ),
        out_specs=(P("row"), P("row")),
        check_vma=False,
    )
```

```python
import jax
import jax.numpy as jnp
from jax import lax
from jax.experimental import pallas as pl
from jax.experimental.pallas import tpu as pltpu
from jax.sharding import PartitionSpec as P

IR_MAX = 8
SWEEPS = 3
RB = 16
BS = 512
SLOTS = 12
BAND = SLOTS - IR_MAX
SEL = 64
VMEM_LIMIT = 58 * 2**20

F32 = jnp.float32
BF16 = jnp.bfloat16
MESH = pl.DeviceIdType.MESH
RING = (2, 1, 3)


def split2(v):
    hi = v.astype(BF16)
    lo = (v - hi.astype(F32)).astype(BF16)
    return jnp.concatenate([hi, lo], axis=0)


def two_term_pick(pick, v):
    hi = v.astype(BF16)
    lo = (v - hi.astype(F32)).astype(BF16)
    return jnp.dot(pick, hi, preferred_element_type=F32) + jnp.dot(pick, lo, preferred_element_type=F32)


def full_max(v):
    m = jnp.max(jnp.max(v, axis=1, keepdims=True), axis=0, keepdims=True)
    return jnp.where(m > 0, m, 1.0)


def kernel(
    rows_hbm, cols_hbm, cnt_hbm, mask_hbm, blocks_ref,
    out_ref,
    rows_ref, cols_ref, cnt_ref, mask_ref,
    blk, blkt, keep, tbuf, ubuf, uloc, ids, pick, pickt, stat, rowband, colband,
    tab, selm, rsel, ulast, uprev, cparts, pprev, prevp, dense, rz,
    xa, za, ta, zb, xb, tb, wstat, stz, sty, stx,
    in_sem, blk_sem, ids_ss, ids_rs, tab_ss, tab_rs, sel_ss, sel_rs, up_ss, up_rs,
    cp_ss, cp_rs, pp_ss, pp_rs, dz_ss, dz_rs, xa_ss, xa_rs, za_ss, za_rs,
    zb_ss, zb_rs, xb_ss, xb_rs, ws_ss, ws_rs,
    sz_ss, sz_rs, sy_ss, sy_rs, sx_ss, sx_rs,
):
    row = lax.axis_index("row")
    col = lax.axis_index("col")
    zl = row // 8
    yc = lax.rem(row, 8)
    y = yc // 2
    core = lax.rem(row, 2)
    x = col // 2
    zh = lax.rem(col, 2)
    z = zh * 4 + zl
    half = BS // 2
    hub = core == 1
    worker = core == 0
    inner = jnp.where(zl < 2, 2, 6)
    two = (inner, 8 - inner)

    def chip(xx, yy, zz, cc):
        return (lax.rem(zz, 4) * 8 + yy * 2 + cc, xx * 2 + zz // 4)

    def z_peer(o, c):
        return chip(x, y, lax.rem(z + o, 8), c)

    def y_peer(o, c):
        return chip(x, lax.rem(y + o, 4), z, c)

    def x_peer(o, c):
        return chip(lax.rem(x + o, 4), y, z, c)

    def sibling(c):
        return chip(x, y, z, c)

    def step_peer(o):
        wrap = 7 if o == 1 else 0
        q = jnp.where(yc == wrap, lax.rem(z + o, 8), z)
        return (lax.rem(q, 4) * 8 + lax.rem(yc + o, 8), x * 2 + q // 4)

    def copy(src, dst, ss, rs, dev):
        return pltpu.make_async_remote_copy(
            src_ref=src, dst_ref=dst, send_sem=ss, recv_sem=rs,
            device_id=dev, device_id_type=MESH,
        )

    def seg(q, c):
        return pl.ds(pl.multiple_of(q * 2 * RB + c * RB, RB), RB)

    def eight(i):
        return pl.ds(pl.multiple_of(i * 8, 8), 8)

    own = seg(zl, core)
    mine = eight(yc)

    def tab_copies(s, c):
        out = [
            copy(tab.at[s, own], tab.at[s, own], tab_ss.at[s, i], tab_rs.at[s, i, c], z_peer(o, 1))
            for i, o in enumerate((two[c], 1, 7))
        ]
        if c == 0:
            out.append(copy(tab.at[s, own], tab.at[s, own], tab_ss.at[s, 3], tab_rs.at[s, 3, 0], sibling(1)))
        return out

    def ids_copies(c):
        out = [copy(ids.at[yc], ids.at[yc], ids_ss.at[o - 1], ids_rs.at[o - 1, c], y_peer(o, 1)) for o in RING]
        if c == 0:
            out.append(copy(ids.at[yc], ids.at[yc], ids_ss.at[3], ids_rs.at[3, 0], sibling(1)))
        return out

    def cp_copies(s, c):
        out = [
            copy(cparts.at[s, mine], cparts.at[s, mine], cp_ss.at[s, o - 1], cp_rs.at[s, o - 1, c], y_peer(o, 1))
            for o in RING
        ]
        if c == 0:
            out.append(copy(cparts.at[s, mine], cparts.at[s, mine], cp_ss.at[s, 3], cp_rs.at[s, 3, 0], sibling(1)))
        return out

    def up_copy(s):
        return copy(ulast.at[s], uprev.at[s], up_ss.at[s], up_rs.at[s], step_peer(1))

    def pp_copy(s):
        return copy(pprev.at[s], prevp.at[s], pp_ss.at[s], pp_rs.at[s], step_peer(7))

    def sel_copies(s):
        out = [
            copy(selm.at[s, eight(lax.rem(y + o, 4) * 2 + c)], rsel.at[s, y],
                 sel_ss.at[s, o - 1, c], sel_rs.at[s, o - 1], y_peer(o, c))
            for o in RING for c in (0, 1)
        ]
        return out + [copy(selm.at[s, eight(y * 2)], rsel.at[s, y], sel_ss.at[s, 3, 0], sel_rs.at[s, 3], sibling(0))]

    def dz_copies(s):
        out = [
            copy(dense.at[s, seg(lax.rem(zl + o, 4), c)], rz.at[s, i],
                 dz_ss.at[s, i, c], dz_rs.at[s, i], z_peer(o, c))
            for c in (0, 1) for i, o in enumerate((two[c], 1, 7))
        ]
        return out + [copy(dense.at[s, seg(zl, 0)], rz.at[s, 3], dz_ss.at[s, 3, 0], dz_rs.at[s, 3], sibling(0))]

    def xa_copies(s, c):
        out = [
            copy(xa.at[s, c, x], xa.at[s, c, x], xa_ss.at[s, o - 1], xa_rs.at[s, o - 1, c], x_peer(o, 1))
            for o in RING
        ]
        if c == 0:
            out.append(copy(xa.at[s, 0, x], xa.at[s, 0, x], xa_ss.at[s, 3], xa_rs.at[s, 3, 0], sibling(1)))
        return out

    def za_copies(s):
        return [
            copy(za.at[s], ta.at[s, 1], za_ss.at[s, 0], za_rs.at[s, 1], z_peer(4, 0)),
            copy(ta.at[s, 0], ta.at[s, 1], za_ss.at[s, 1], za_rs.at[s, 1], z_peer(4, 1)),
            copy(za.at[s], ta.at[s, 0], za_ss.at[s, 2], za_rs.at[s, 0], sibling(0)),
        ]

    def zb_copies(s, c):
        out = [copy(zb.at[s, c, 0], zb.at[s, c, 1], zb_ss.at[s, 0], zb_rs.at[s, 0, c], z_peer(4, 1))]
        if c == 0:
            out.append(copy(zb.at[s, 0, 0], zb.at[s, 0, 0], zb_ss.at[s, 1], zb_rs.at[s, 1, 0], sibling(1)))
        return out

    def xb_copies(s):
        out = []
        for o in RING:
            out.append(copy(xb.at[s], tb.at[s, x], xb_ss.at[s, o - 1, 0], xb_rs.at[s, o - 1], x_peer(o, 0)))
            out.append(copy(tb.at[s, x], tb.at[s, x], xb_ss.at[s, o - 1, 1], xb_rs.at[s, o - 1], x_peer(o, 1)))
        return out + [copy(xb.at[s], tb.at[s, x], xb_ss.at[s, 3, 0], xb_rs.at[s, 3], sibling(0))]

    def sx_copies():
        out = [
            copy(stx.at[x], stx.at[x], sx_ss.at[o - 1, c], sx_rs.at[o - 1], x_peer(o, c))
            for o in RING for c in (0, 1)
        ]
        return out + [copy(stx.at[x], stx.at[x], sx_ss.at[3, 0], sx_rs.at[3], sibling(0))]

    def start(copies):
        for c in copies:
            c.start()

    def sent(copies):
        for c in copies:
            c.wait_send()

    def arrived(sems, like):
        for r in sems:
            pltpu.make_async_copy(like, like, r).wait()

    def by_core(f):
        pl.when(worker)(lambda: f(0))
        pl.when(hub)(lambda: f(1))

    both = [(i, c) for i in range(3) for c in (0, 1)] + [(3, 0)]

    loads = [
        pltpu.make_async_copy(src, dst, in_sem.at[i])
        for i, (src, dst) in enumerate((
            (rows_hbm, rows_ref), (cols_hbm, cols_ref), (cnt_hbm, cnt_ref), (mask_hbm, mask_ref),
        ))
    ] + [
        pltpu.make_async_copy(blocks_ref.at[k], blk.at[k], blk_sem.at[k])
        for k in (*range(BAND, SLOTS), *range(BAND))
    ]
    loads[3].start()

    barrier = pltpu.get_barrier_semaphore()

    def greet(c):
        if c == 0:
            peers = (
                [z_peer(o, 1) for o in (2, 6, 1, 7)] + [y_peer(o, 1) for o in RING]
                + [x_peer(o, 1) for o in RING] + [sibling(1), step_peer(7)]
            )
        else:
            peers = (
                [z_peer(o, d) for o in (2, 6, 1, 7) for d in (0, 1)]
                + [y_peer(o, d) for o in RING for d in (0, 1)]
                + [x_peer(o, d) for o in RING for d in (0, 1)]
                + [sibling(0), step_peer(1)]
            )
        return peers

    def signal_peers(c):
        for dev in greet(c):
            pl.semaphore_signal(barrier, inc=1, device_id=dev, device_id_type=MESH)

    by_core(signal_peers)
    start([*loads[:3], *loads[4:]])
    for c in loads[:4]:
        c.wait()

    live = cnt_ref[0]
    row_l = [lax.rem(rows_ref[k], RB) for k in range(SLOTS)]
    col_l = [cols_ref[k] - row * RB for k in range(BAND)]
    here = [(c >= 0) & (c < RB) for c in col_l]
    lane = lax.broadcasted_iota(jnp.int32, (8, 128), 1)
    iota8 = lax.broadcasted_iota(jnp.int32, (8, BS), 0)
    iota16 = lax.broadcasted_iota(jnp.int32, (RB, BS), 0)
    iota24 = lax.broadcasted_iota(jnp.int32, (RB + 8, BS), 0)

    idv = jnp.zeros((8, 128), jnp.int32)
    for k in range(IR_MAX):
        code = jnp.where(k < live, cols_ref[BAND + k] + 1, 0)
        idv = jnp.where(lane == yc * 8 + k, code, idv)
    ids[yc] = idv
    for q in range(4):
        keep[:, q * 128:(q + 1) * 128] = mask_ref[pl.ds(q, RB, stride=4), :].astype(F32)
    tbuf[0] = jnp.full((RB, BS), 4.0, F32)
    uloc[...] = jnp.zeros_like(uloc)

    def total_of(v):
        return jnp.sum(jnp.sum(v, axis=1, keepdims=True), axis=0, keepdims=True)

    sub = lax.broadcasted_iota(jnp.int32, (8, 128), 0)
    stat[...] = jnp.where(sub == 0, total_of(keep[...]), 0.0)

    def add_share(s, v):
        stat[...] += jnp.where(sub == s + 1, total_of(v), 0.0)

    def weights(s):
        u = jnp.where(keep[...] > 0, 4.0 / tbuf[s], 0.0)
        ubuf[s] = u
        tab[s, own] = u
        uloc[0:RB] = u
        ulast[s] = u[RB - 1:]

    def inter_columns(s):
        m = full_max(uloc[0:RB])
        inv = 1.0 / m
        acc = None
        for k in range(IR_MAX):
            vec = uloc[pl.ds(row_l[BAND + k], 1), :] * inv
            target = jnp.where(k < live, k, -1)
            lhs = split2(jnp.where(iota8 == target, vec, 0.0))
            part = jnp.dot(lhs, blk[BAND + k], preferred_element_type=F32)
            acc = part if acc is None else acc + part
        cparts[s, mine] = (acc[:8] + acc[8:]) * m

    def band_columns(s):
        m = full_max(uloc[0:RB])
        inv = 1.0 / m
        acc = None
        for k in range(BAND):
            vec = uloc[pl.ds(row_l[k], 1), :] * inv
            target = jnp.where(here[k], col_l[k], RB)
            lhs = split2(jnp.where(iota24 == target, vec, 0.0))
            part = jnp.dot(lhs, blk[k], preferred_element_type=F32)
            acc = part if acc is None else acc + part
        acc = (acc[:RB + 8] + acc[RB + 8:]) * m
        colband[...] = acc[:RB]
        pprev[s] = acc[RB:RB + 1]

    def transpose_inter():
        def one(k, carry):
            blkt[k] = blk[BAND + k].T
            return carry

        lax.fori_loop(0, IR_MAX, one, 0)

    def open_up(c):
        pl.semaphore_wait(barrier, len(greet(c)))
        start(ids_copies(c))

    by_core(open_up)

    def sweep(s, carry):
        first = s == 0
        last = s == SWEEPS - 1

        weights(s)
        by_core(lambda c: start(tab_copies(s, c)))
        up_copy(s).start()

        @pl.when(first)
        def _():
            for c in loads[4:4 + IR_MAX]:
                c.wait()

        inter_columns(s)
        by_core(lambda c: start(cp_copies(s, c)))

        @pl.when(first)
        def _():
            for c in loads[4 + IR_MAX:]:
                c.wait()

        band_columns(s)
        pp_copy(s).start()
        pl.when(first)(transpose_inter)

        up_copy(s).wait_recv()
        uloc[RB:RB + 1] = uprev[s]
        m = full_max(uloc[...])
        inv = 1.0 / m
        acc = None
        for k in range(BAND):
            vec = uloc[pl.ds(jnp.where(here[k], col_l[k], RB), 1), :] * inv
            lhs = split2(jnp.where(iota16 == row_l[k], vec, 0.0))
            part = lax.dot_general(
                lhs, blk[k], (((1,), (1,)), ((), ())), preferred_element_type=F32
            )
            acc = part if acc is None else acc + part
        rowband[...] = (acc[:RB] + acc[RB:]) * m

        @pl.when(worker)
        def _():
            add_share(s, uloc[0:RB] * rowband[...])

            @pl.when(last)
            def _():
                copy(stat, wstat, ws_ss, ws_rs, sibling(1)).start()

        @pl.when(hub)
        def _():
            @pl.when(first)
            def _():
                arrived([ids_rs.at[i, c] for i, c in both], ids.at[0])
                code = ids[0]
                for p in range(1, 8):
                    code = code + ids[p]
                code = code[0:1]
                cc = jnp.maximum(code - 1, 0)
                want = jnp.where(
                    (code > 0) & (((cc // 32) % 4) == y), (cc // 128) * 32 + cc % 32, -1
                )
                full = jnp.where(
                    lax.broadcasted_iota(jnp.int32, (128, 128), 0) == want, 1.0, 0.0
                )
                pick[...] = full[:, :SEL].astype(BF16)
                pickt[...] = full.T[:SEL].astype(BF16)

            arrived([tab_rs.at[s, i, c] for i, c in both], tab.at[s, own])
            selm[s] = two_term_pick(pickt[...], tab[s])
            start(sel_copies(s))
            rsel[s, y] = selm[s, mine]

            arrived([cp_rs.at[s, i, c] for i, c in both], cparts.at[s, mine])
            dense[s] = two_term_pick(pick[...], cparts[s])
            start(dz_copies(s))
            rz[s, 3] = dense[s, own]

            @pl.when(last)
            def _():
                arrived([ws_rs], wstat)
                add_share(s, dense[s] * tab[s])
                add_share(s, uloc[0:RB] * rowband[...])
                stz[z] = stat[...] + wstat[...]
                for o in range(1, 8):
                    copy(stz.at[z], stz.at[z], sz_ss.at[o - 1], sz_rs.at[o - 1], z_peer(o, 1)).start()

        arrived([sel_rs.at[s, i] for i in range(3)], rsel.at[s, 0])
        pl.when(worker)(lambda: arrived([sel_rs.at[s, 3]], rsel.at[s, 0]))
        ucol = (rsel[s, 0] + rsel[s, 1]) + (rsel[s, 2] + rsel[s, 3])
        m2 = full_max(ucol)
        ucol = ucol * (1.0 / m2)
        acc = None
        for k in range(IR_MAX):
            target = jnp.where(k < live, row_l[BAND + k], -1)
            lhs = split2(jnp.where(iota16 == target, ucol[k:k + 1], 0.0))
            part = jnp.dot(lhs, blkt[k], preferred_element_type=F32)
            acc = part if acc is None else acc + part
        total = (acc[:RB] + acc[RB:]) * m2 + rowband[...] + colband[...]

        pp_copy(s).wait_recv()
        total = total + jnp.where(iota16 == RB - 1, prevp[s], 0.0)
        arrived([dz_rs.at[s, i] for i in range(3)], rz.at[s, 0])
        pl.when(worker)(lambda: arrived([dz_rs.at[s, 3]], rz.at[s, 0]))
        total = total + ((rz[s, 0] + rz[s, 1]) + (rz[s, 2] + rz[s, 3]))

        zb[s, core, 0] = total[:, half:]
        by_core(lambda c: start(zb_copies(s, c)))
        xa[s, core, x] = total[:, :half]
        by_core(lambda c: start(xa_copies(s, c)))

        @pl.when(worker)
        def _():
            sent([*tab_copies(s, 0), up_copy(s), *cp_copies(s, 0), pp_copy(s)])

        @pl.when(hub)
        def _():
            @pl.when(jnp.logical_not(last))
            def _():
                add_share(s, dense[s] * tab[s])
                add_share(s, uloc[0:RB] * rowband[...])

            @pl.when(last)
            def _():
                for o in range(1, 8):
                    copy(stz.at[z], stz.at[z], sz_ss.at[o - 1], sz_rs.at[o - 1], z_peer(o, 1)).wait()
                v = stz[0]
                for p in range(1, 8):
                    v = v + stz[p]
                sty[y] = v
                for o in RING:
                    copy(sty.at[y], sty.at[y], sy_ss.at[o - 1], sy_rs.at[o - 1], y_peer(o, 1)).start()

            sent([*tab_copies(s, 1), up_copy(s), *cp_copies(s, 1), pp_copy(s), *sel_copies(s), *dz_copies(s)])

            arrived([xa_rs.at[s, i, c] for i, c in both], xa.at[s, 0, 0])
            za[s] = (xa[s, 0, 0] + xa[s, 0, 1]) + (xa[s, 0, 2] + xa[s, 0, 3])
            ta[s, 0] = (xa[s, 1, 0] + xa[s, 1, 1]) + (xa[s, 1, 2] + xa[s, 1, 3])
            start(za_copies(s))

            @pl.when(last)
            def _():
                for o in RING:
                    copy(sty.at[y], sty.at[y], sy_ss.at[o - 1], sy_rs.at[o - 1], y_peer(o, 1)).wait()
                stx[x] = (sty[0] + sty[1]) + (sty[2] + sty[3])
                start(sx_copies())

            arrived([zb_rs.at[s, 0, 0], zb_rs.at[s, 0, 1], zb_rs.at[s, 1, 0]], zb.at[s, 0, 0])
            xb[s] = zb[s, 0, 0] + zb[s, 0, 1]
            tb[s, x] = zb[s, 1, 0] + zb[s, 1, 1]
            start(xb_copies(s))

            sent([*za_copies(s), *xb_copies(s)])

        by_core(lambda c: sent([*xa_copies(s, c), *zb_copies(s, c)]))
        arrived([xb_rs.at[s, i] for i in range(3)], tb.at[s, 0])
        pl.when(worker)(lambda: arrived([xb_rs.at[s, 3], za_rs.at[s, 0]], tb.at[s, 0]))
        arrived([za_rs.at[s, 1]], tb.at[s, 0])
        tbuf[s + 1, :, :half] = ta[s, 0] + ta[s, 1]
        tbuf[s + 1, :, half:] = (tb[s, 0] + tb[s, 1]) + (tb[s, 2] + tb[s, 3])

        return carry

    lax.fori_loop(0, SWEEPS, sweep, 0)

    arrived([sx_rs.at[i] for i in range(3)], stx.at[0])

    @pl.when(hub)
    def _():
        sent([*ids_copies(1), *sx_copies()])

    @pl.when(worker)
    def _():
        sent([copy(stat, wstat, ws_ss, ws_rs, sibling(1)), *ids_copies(0)])
        arrived([sx_rs.at[3]], stx.at[0])

    v = (stx[0] + stx[1]) + (stx[2] + stx[3])
    count = v[0:1, 0:1] * 0.125
    mean1 = v[1:2, 0:1] * 2.0 / count
    mean2 = v[2:3, 0:1] * 2.0 / count
    mean3 = v[3:4, 0:1] * 2.0 / count
    scale = mean1 * mean2 * 0.0625 * mean3
    b3 = tbuf[SWEEPS]
    bias = jnp.where(keep[...] > 0, b3 / scale, 1.0)
    balance = b3 * ubuf[SWEEPS - 1] / mean3
    for q in range(4):
        out_ref[pl.ds(q, RB, stride=4), :] = bias[:, q * 128:(q + 1) * 128]
        out_ref[pl.ds(4 * RB + q, RB, stride=4), :] = balance[:, q * 128:(q + 1) * 128]


def body(blocks, block_rows, block_cols, inter_counts, keep_mask):
    seg = keep_mask.shape[0]
    vm = pl.BlockSpec(memory_space=pltpu.VMEM)
    hbm = pl.BlockSpec(memory_space=pl.ANY)
    S = SWEEPS
    H = BS // 2
    dma = pltpu.SemaphoreType.DMA
    i32 = jnp.int32
    out = jax.ShapeDtypeStruct((seg // 64, 128), F32)

    def vf(*shape):
        return pltpu.VMEM(shape, F32)

    both = pl.pallas_call(
        kernel,
        out_shape=out,
        in_specs=[hbm] * 5,
        out_specs=vm,
        scratch_shapes=[
            pltpu.SMEM((SLOTS,), i32),
            pltpu.SMEM((SLOTS,), i32),
            pltpu.SMEM((1,), i32),
            pltpu.VMEM((seg // 128, 128), i32),
            pltpu.VMEM((SLOTS, BS, BS), BF16),
            pltpu.VMEM((IR_MAX, BS, BS), BF16),
            vf(RB, BS),
            vf(S + 1, RB, BS),
            vf(S, RB, BS),
            vf(RB + 8, BS),
            pltpu.VMEM((8, 8, 128), i32),
            pltpu.VMEM((128, SEL), BF16),
            pltpu.VMEM((SEL, 128), BF16),
            vf(8, 128),
            vf(RB, BS),
            vf(RB, BS),
            vf(S, 128, BS),
            vf(S, SEL, BS),
            vf(S, 4, 8, BS),
            vf(S, 1, BS),
            vf(S, 1, BS),
            vf(S, SEL, BS),
            vf(S, 1, BS),
            vf(S, 1, BS),
            vf(S, 128, BS),
            vf(S, 4, RB, BS),
            vf(S, 2, 4, RB, H),
            vf(S, RB, H),
            vf(S, 2, RB, H),
            vf(S, 2, 2, RB, H),
            vf(S, RB, H),
            vf(S, 4, RB, H),
            vf(8, 128),
            vf(8, 8, 128),
            vf(4, 8, 128),
            vf(4, 8, 128),
            dma((4,)),
            dma((SLOTS,)),
            dma((4,)), dma((4, 2)),
            dma((S, 4)), dma((S, 4, 2)),
            dma((S, 4, 2)), dma((S, 4)),
            dma((S,)), dma((S,)),
            dma((S, 4)), dma((S, 4, 2)),
            dma((S,)), dma((S,)),
            dma((S, 4, 2)), dma((S, 4)),
            dma((S, 4)), dma((S, 4, 2)),
            dma((S, 3)), dma((S, 2)),
            dma((S, 2)), dma((S, 2, 2)),
            dma((S, 4, 2)), dma((S, 4)),
            dma, dma,
            dma((7,)), dma((7,)),
            dma((3,)), dma((3,)),
            dma((4, 2)), dma((4,)),
        ],
        compiler_params=pltpu.CompilerParams(
            collective_id=0, has_side_effects=True, vmem_limit_bytes=VMEM_LIMIT
        ),
        name="balance",
    )(block_rows, block_cols, inter_counts, keep_mask.reshape(seg // 128, 128), blocks)
    bias, balance = both[:seg // 128], both[seg // 128:]
    return bias.reshape(seg), balance.reshape(seg)


def solution(mesh):
    return jax.shard_map(
        body,
        mesh=mesh,
        in_specs=(
            P(("row", "col"), None, None),
            P(("row", "col")),
            P(("row", "col")),
            P(("row", "col")),
            P("row"),
        ),
        out_specs=(P("row"), P("row")),
        check_vma=False,
    )
```

```python
import jax
import jax.numpy as jnp
from jax import lax
from jax.experimental import pallas as pl
from jax.experimental.pallas import tpu as pltpu
from jax.sharding import PartitionSpec as P

IR_MAX = 8
SWEEPS = 3
RB = 16
BS = 512
SLOTS = 12
BAND = SLOTS - IR_MAX
SEL = 64
VMEM_LIMIT = 58 * 2**20

F32 = jnp.float32
BF16 = jnp.bfloat16
MESH = pl.DeviceIdType.MESH
RING = (2, 1, 3)


def split2(v):
    hi = v.astype(BF16)
    lo = (v - hi.astype(F32)).astype(BF16)
    return jnp.concatenate([hi, lo], axis=0)


def two_term_pick(pick, v):
    hi = v.astype(BF16)
    lo = (v - hi.astype(F32)).astype(BF16)
    return jnp.dot(pick, hi, preferred_element_type=F32) + jnp.dot(pick, lo, preferred_element_type=F32)


def full_max(v):
    m = jnp.max(jnp.max(v, axis=1, keepdims=True), axis=0, keepdims=True)
    return jnp.where(m > 0, m, 1.0)


def kernel(
    rows_hbm, cols_hbm, cnt_hbm, mask_hbm, blocks_ref,
    out_ref,
    rows_ref, cols_ref, cnt_ref, mask_ref,
    blk, blkt, keep, tbuf, ubuf, uloc, ids, pick, pickt, stat, rowband, colband,
    tab, selm, rsel, ulast, uprev, cparts, pprev, prevp, dense, rz,
    xa, za, ta, zb, xb, tb, wstat, stz, sty, stx,
    in_sem, blk_sem, ids_ss, ids_rs, tab_ss, tab_rs, sel_ss, sel_rs, up_ss, up_rs,
    cp_ss, cp_rs, pp_ss, pp_rs, dz_ss, dz_rs, xa_ss, xa_rs, za_ss, za_rs,
    zb_ss, zb_rs, xb_ss, xb_rs, ws_ss, ws_rs,
    sz_ss, sz_rs, sy_ss, sy_rs, sx_ss, sx_rs,
):
    row = lax.axis_index("row")
    col = lax.axis_index("col")
    zl = row // 8
    yc = lax.rem(row, 8)
    y = yc // 2
    core = lax.rem(row, 2)
    x = col // 2
    zh = lax.rem(col, 2)
    z = zh * 4 + zl
    half = BS // 2
    hub = core == 1
    worker = core == 0
    inner = jnp.where(zl < 2, 2, 6)
    two = (inner, 8 - inner)

    def chip(xx, yy, zz, cc):
        return (lax.rem(zz, 4) * 8 + yy * 2 + cc, xx * 2 + zz // 4)

    def z_peer(o, c):
        return chip(x, y, lax.rem(z + o, 8), c)

    def y_peer(o, c):
        return chip(x, lax.rem(y + o, 4), z, c)

    def x_peer(o, c):
        return chip(lax.rem(x + o, 4), y, z, c)

    def sibling(c):
        return chip(x, y, z, c)

    def step_peer(o):
        wrap = 7 if o == 1 else 0
        q = jnp.where(yc == wrap, lax.rem(z + o, 8), z)
        return (lax.rem(q, 4) * 8 + lax.rem(yc + o, 8), x * 2 + q // 4)

    def copy(src, dst, ss, rs, dev):
        return pltpu.make_async_remote_copy(
            src_ref=src, dst_ref=dst, send_sem=ss, recv_sem=rs,
            device_id=dev, device_id_type=MESH,
        )

    def seg(q, c):
        return pl.ds(pl.multiple_of(q * 2 * RB + c * RB, RB), RB)

    def eight(i):
        return pl.ds(pl.multiple_of(i * 8, 8), 8)

    own = seg(zl, core)
    mine = eight(yc)

    def tab_copies(s, c):
        out = [
            copy(tab.at[s, own], tab.at[s, own], tab_ss.at[s], tab_rs.at[s], z_peer(o, 1))
            for i, o in enumerate((two[c], 1, 7))
        ]
        if c == 0:
            out.append(copy(tab.at[s, own], tab.at[s, own], tab_ss.at[s], tab_rs.at[s], sibling(1)))
        return out

    def ids_copies(c):
        out = [copy(ids.at[yc], ids.at[yc], ids_ss, ids_rs, y_peer(o, 1)) for o in RING]
        if c == 0:
            out.append(copy(ids.at[yc], ids.at[yc], ids_ss, ids_rs, sibling(1)))
        return out

    def cp_copies(s, c):
        out = [
            copy(cparts.at[s, mine], cparts.at[s, mine], cp_ss.at[s], cp_rs.at[s], y_peer(o, 1))
            for o in RING
        ]
        if c == 0:
            out.append(copy(cparts.at[s, mine], cparts.at[s, mine], cp_ss.at[s], cp_rs.at[s], sibling(1)))
        return out

    def up_copy(s):
        return copy(ulast.at[s], uprev.at[s], up_ss.at[s], up_rs.at[s], step_peer(1))

    def pp_copy(s):
        return copy(pprev.at[s], prevp.at[s], pp_ss.at[s], pp_rs.at[s], step_peer(7))

    def sel_copies(s):
        out = [
            copy(selm.at[s, eight(lax.rem(y + o, 4) * 2 + c)], rsel.at[s, y],
                 sel_ss.at[s], sel_rs.at[s], y_peer(o, c))
            for o in RING for c in (0, 1)
        ]
        return out + [copy(selm.at[s, eight(y * 2)], rsel.at[s, y], sel_ss.at[s], sel_rs.at[s], sibling(0))]

    def dz_copies(s):
        out = [
            copy(dense.at[s, seg(lax.rem(zl + o, 4), c)], rz.at[s, i],
                 dz_ss.at[s], dz_rs.at[s], z_peer(o, c))
            for c in (0, 1) for i, o in enumerate((two[c], 1, 7))
        ]
        return out + [copy(dense.at[s, seg(zl, 0)], rz.at[s, 3], dz_ss.at[s], dz_rs.at[s], sibling(0))]

    def xa_copies(s, c):
        out = [
            copy(xa.at[s, c, x], xa.at[s, c, x], xa_ss.at[s], xa_rs.at[s, c], x_peer(o, 1))
            for o in RING
        ]
        if c == 0:
            out.append(copy(xa.at[s, 0, x], xa.at[s, 0, x], xa_ss.at[s], xa_rs.at[s, c], sibling(1)))
        return out

    def za_copies(s):
        return [
            copy(za.at[s], ta.at[s, 1], za_ss.at[s], za_rs.at[s], z_peer(4, 0)),
            copy(ta.at[s, 0], ta.at[s, 1], za_ss.at[s], za_rs.at[s], z_peer(4, 1)),
            copy(za.at[s], ta.at[s, 0], za_ss.at[s], za_rs.at[s], sibling(0)),
        ]

    def zb_copies(s, c):
        out = [copy(zb.at[s, c, 0], zb.at[s, c, 1], zb_ss.at[s], zb_rs.at[s, c], z_peer(4, 1))]
        if c == 0:
            out.append(copy(zb.at[s, 0, 0], zb.at[s, 0, 0], zb_ss.at[s], zb_rs.at[s, c], sibling(1)))
        return out

    def xb_copies(s):
        out = []
        for o in RING:
            out.append(copy(xb.at[s], tb.at[s, x], xb_ss.at[s], xb_rs.at[s], x_peer(o, 0)))
            out.append(copy(tb.at[s, x], tb.at[s, x], xb_ss.at[s], xb_rs.at[s], x_peer(o, 1)))
        return out + [copy(xb.at[s], tb.at[s, x], xb_ss.at[s], xb_rs.at[s], sibling(0))]

    def sx_copies():
        out = [
            copy(stx.at[x], stx.at[x], sx_ss, sx_rs, x_peer(o, c))
            for o in RING for c in (0, 1)
        ]
        return out + [copy(stx.at[x], stx.at[x], sx_ss, sx_rs, sibling(0))]

    def start(copies):
        for c in copies:
            c.start()

    def done(sem, like):
        pltpu.make_async_copy(like, like, sem).wait()

    def by_core(f):
        pl.when(worker)(lambda: f(0))
        pl.when(hub)(lambda: f(1))

    loads = [
        pltpu.make_async_copy(src, dst, in_sem.at[i])
        for i, (src, dst) in enumerate((
            (rows_hbm, rows_ref), (cols_hbm, cols_ref), (cnt_hbm, cnt_ref), (mask_hbm, mask_ref),
        ))
    ] + [
        pltpu.make_async_copy(blocks_ref.at[k], blk.at[k], blk_sem.at[k])
        for k in (*range(BAND, SLOTS), *range(BAND))
    ]
    loads[3].start()

    barrier = pltpu.get_barrier_semaphore()

    def greet(c):
        if c == 0:
            peers = (
                [z_peer(o, 1) for o in (2, 6, 1, 7)] + [y_peer(o, 1) for o in RING]
                + [x_peer(o, 1) for o in RING] + [sibling(1), step_peer(7)]
            )
        else:
            peers = (
                [z_peer(o, d) for o in (2, 6, 1, 7) for d in (0, 1)]
                + [y_peer(o, d) for o in RING for d in (0, 1)]
                + [x_peer(o, d) for o in RING for d in (0, 1)]
                + [sibling(0), step_peer(1)]
            )
        return peers

    def signal_peers(c):
        for dev in greet(c):
            pl.semaphore_signal(barrier, inc=1, device_id=dev, device_id_type=MESH)

    by_core(signal_peers)
    start([*loads[:3], *loads[4:]])
    for c in loads[:4]:
        c.wait()

    live = cnt_ref[0]
    row_l = [lax.rem(rows_ref[k], RB) for k in range(SLOTS)]
    col_l = [cols_ref[k] - row * RB for k in range(BAND)]
    here = [(c >= 0) & (c < RB) for c in col_l]
    lane = lax.broadcasted_iota(jnp.int32, (8, 128), 1)
    iota8 = lax.broadcasted_iota(jnp.int32, (8, BS), 0)
    iota16 = lax.broadcasted_iota(jnp.int32, (RB, BS), 0)
    iota24 = lax.broadcasted_iota(jnp.int32, (RB + 8, BS), 0)

    idv = jnp.zeros((8, 128), jnp.int32)
    for k in range(IR_MAX):
        code = jnp.where(k < live, cols_ref[BAND + k] + 1, 0)
        idv = jnp.where(lane == yc * 8 + k, code, idv)
    ids[yc] = idv
    for q in range(4):
        keep[:, q * 128:(q + 1) * 128] = mask_ref[pl.ds(q, RB, stride=4), :].astype(F32)
    tbuf[0] = jnp.full((RB, BS), 4.0, F32)
    uloc[...] = jnp.zeros_like(uloc)

    def total_of(v):
        return jnp.sum(jnp.sum(v, axis=1, keepdims=True), axis=0, keepdims=True)

    sub = lax.broadcasted_iota(jnp.int32, (8, 128), 0)
    stat[...] = jnp.where(sub == 0, total_of(keep[...]), 0.0)

    def add_share(s, v):
        stat[...] += jnp.where(sub == s + 1, total_of(v), 0.0)

    def weights(s):
        u = jnp.where(keep[...] > 0, 4.0 / tbuf[s], 0.0)
        ubuf[s] = u
        tab[s, own] = u
        uloc[0:RB] = u
        ulast[s] = u[RB - 1:]

    def inter_columns(s):
        m = full_max(uloc[0:RB])
        inv = 1.0 / m
        acc = None
        for k in range(IR_MAX):
            vec = uloc[pl.ds(row_l[BAND + k], 1), :] * inv
            target = jnp.where(k < live, k, -1)
            lhs = split2(jnp.where(iota8 == target, vec, 0.0))
            part = jnp.dot(lhs, blk[BAND + k], preferred_element_type=F32)
            acc = part if acc is None else acc + part
        cparts[s, mine] = (acc[:8] + acc[8:]) * m

    def band_columns(s):
        m = full_max(uloc[0:RB])
        inv = 1.0 / m
        acc = None
        for k in range(BAND):
            vec = uloc[pl.ds(row_l[k], 1), :] * inv
            target = jnp.where(here[k], col_l[k], RB)
            lhs = split2(jnp.where(iota24 == target, vec, 0.0))
            part = jnp.dot(lhs, blk[k], preferred_element_type=F32)
            acc = part if acc is None else acc + part
        acc = (acc[:RB + 8] + acc[RB + 8:]) * m
        colband[...] = acc[:RB]
        pprev[s] = acc[RB:RB + 1]

    def transpose_inter():
        def one(k, carry):
            blkt[k] = blk[BAND + k].T
            return carry

        lax.fori_loop(0, IR_MAX, one, 0)

    def open_up(c):
        pl.semaphore_wait(barrier, len(greet(c)))
        start(ids_copies(c))

    by_core(open_up)

    def sweep(s, carry):
        first = s == 0
        last = s == SWEEPS - 1

        weights(s)
        by_core(lambda c: start(tab_copies(s, c)))
        up_copy(s).start()

        @pl.when(first)
        def _():
            for c in loads[4:4 + IR_MAX]:
                c.wait()

        inter_columns(s)
        by_core(lambda c: start(cp_copies(s, c)))

        @pl.when(first)
        def _():
            for c in loads[4 + IR_MAX:]:
                c.wait()

        band_columns(s)
        pp_copy(s).start()
        pl.when(first)(transpose_inter)

        up_copy(s).wait_recv()
        uloc[RB:RB + 1] = uprev[s]
        m = full_max(uloc[...])
        inv = 1.0 / m
        acc = None
        for k in range(BAND):
            vec = uloc[pl.ds(jnp.where(here[k], col_l[k], RB), 1), :] * inv
            lhs = split2(jnp.where(iota16 == row_l[k], vec, 0.0))
            part = lax.dot_general(
                lhs, blk[k], (((1,), (1,)), ((), ())), preferred_element_type=F32
            )
            acc = part if acc is None else acc + part
        rowband[...] = (acc[:RB] + acc[RB:]) * m

        @pl.when(worker)
        def _():
            add_share(s, uloc[0:RB] * rowband[...])

            @pl.when(last)
            def _():
                copy(stat, wstat, ws_ss, ws_rs, sibling(1)).start()

        @pl.when(hub)
        def _():
            @pl.when(first)
            def _():
                done(ids_rs, ids.at[0:7])
                code = ids[0]
                for p in range(1, 8):
                    code = code + ids[p]
                code = code[0:1]
                cc = jnp.maximum(code - 1, 0)
                want = jnp.where(
                    (code > 0) & (((cc // 32) % 4) == y), (cc // 128) * 32 + cc % 32, -1
                )
                full = jnp.where(
                    lax.broadcasted_iota(jnp.int32, (128, 128), 0) == want, 1.0, 0.0
                )
                pick[...] = full[:, :SEL].astype(BF16)
                pickt[...] = full.T[:SEL].astype(BF16)

            done(tab_rs.at[s], tab.at[s, 0:7 * RB])
            selm[s] = two_term_pick(pickt[...], tab[s])
            start(sel_copies(s))
            rsel[s, y] = selm[s, mine]

            done(cp_rs.at[s], cparts.at[s, 0:56])
            dense[s] = two_term_pick(pick[...], cparts[s])
            start(dz_copies(s))
            rz[s, 3] = dense[s, own]

            @pl.when(last)
            def _():
                done(ws_rs, wstat)
                add_share(s, dense[s] * tab[s])
                add_share(s, uloc[0:RB] * rowband[...])
                stz[z] = stat[...] + wstat[...]
                for o in range(1, 8):
                    copy(stz.at[z], stz.at[z], sz_ss, sz_rs, z_peer(o, 1)).start()

        by_core(lambda c: done(sel_rs.at[s], rsel.at[s, 0:4 - c]))
        ucol = (rsel[s, 0] + rsel[s, 1]) + (rsel[s, 2] + rsel[s, 3])
        m2 = full_max(ucol)
        ucol = ucol * (1.0 / m2)
        acc = None
        for k in range(IR_MAX):
            target = jnp.where(k < live, row_l[BAND + k], -1)
            lhs = split2(jnp.where(iota16 == target, ucol[k:k + 1], 0.0))
            part = jnp.dot(lhs, blkt[k], preferred_element_type=F32)
            acc = part if acc is None else acc + part
        total = (acc[:RB] + acc[RB:]) * m2 + rowband[...] + colband[...]

        pp_copy(s).wait_recv()
        total = total + jnp.where(iota16 == RB - 1, prevp[s], 0.0)
        by_core(lambda c: done(dz_rs.at[s], rz.at[s, 0:4 - c]))
        total = total + ((rz[s, 0] + rz[s, 1]) + (rz[s, 2] + rz[s, 3]))

        zb[s, core, 0] = total[:, half:]
        by_core(lambda c: start(zb_copies(s, c)))
        xa[s, core, x] = total[:, :half]
        by_core(lambda c: start(xa_copies(s, c)))

        @pl.when(worker)
        def _():
            done(tab_ss.at[s], tab.at[s, 0:4 * RB])
            done(cp_ss.at[s], cparts.at[s, 0:32])
            up_copy(s).wait_send()
            pp_copy(s).wait_send()

        @pl.when(hub)
        def _():
            @pl.when(jnp.logical_not(last))
            def _():
                add_share(s, dense[s] * tab[s])
                add_share(s, uloc[0:RB] * rowband[...])

            @pl.when(last)
            def _():
                done(sz_ss, stz.at[0:7])
                done(sz_rs, stz.at[0:7])
                v = stz[0]
                for p in range(1, 8):
                    v = v + stz[p]
                sty[y] = v
                for o in RING:
                    copy(sty.at[y], sty.at[y], sy_ss, sy_rs, y_peer(o, 1)).start()

            done(tab_ss.at[s], tab.at[s, 0:3 * RB])
            done(cp_ss.at[s], cparts.at[s, 0:24])
            up_copy(s).wait_send()
            pp_copy(s).wait_send()
            done(sel_ss.at[s], selm.at[s, 0:56])
            done(dz_ss.at[s], dense.at[s, 0:7 * RB])

            done(xa_rs.at[s, 0], xa.at[s, 0])
            done(xa_rs.at[s, 1], xa.at[s, 1, 0:3])
            za[s] = (xa[s, 0, 0] + xa[s, 0, 1]) + (xa[s, 0, 2] + xa[s, 0, 3])
            ta[s, 0] = (xa[s, 1, 0] + xa[s, 1, 1]) + (xa[s, 1, 2] + xa[s, 1, 3])
            start(za_copies(s))

            @pl.when(last)
            def _():
                done(sy_ss, sty.at[0:3])
                done(sy_rs, sty.at[0:3])
                stx[x] = (sty[0] + sty[1]) + (sty[2] + sty[3])
                start(sx_copies())

            done(zb_rs.at[s, 0], zb.at[s, 0])
            done(zb_rs.at[s, 1], zb.at[s, 1, 0])
            xb[s] = zb[s, 0, 0] + zb[s, 0, 1]
            tb[s, x] = zb[s, 1, 0] + zb[s, 1, 1]
            start(xb_copies(s))

            done(za_ss.at[s], xa.at[s, 0, 0:3])
            done(xb_ss.at[s], selm.at[s, 0:56])

        def rest(c):
            done(xa_ss.at[s], xa.at[s, 0, 0:4 - c])
            done(zb_ss.at[s], zb.at[s, 0, 0:2 - c])
            done(xb_rs.at[s], tb.at[s, 0:4 - c])
            done(za_rs.at[s], ta.at[s, 0:2 - c])

        by_core(rest)
        tbuf[s + 1, :, :half] = ta[s, 0] + ta[s, 1]
        tbuf[s + 1, :, half:] = (tb[s, 0] + tb[s, 1]) + (tb[s, 2] + tb[s, 3])

        return carry

    lax.fori_loop(0, SWEEPS, sweep, 0)

    def finish(c):
        done(sx_rs, stx.at[0:4 - c])
        done(ids_ss, ids.at[0:4 - c])
        if c == 0:
            done(ws_ss, stat)
        else:
            done(sx_ss, stz.at[0:7])

    by_core(finish)
    v = (stx[0] + stx[1]) + (stx[2] + stx[3])
    count = v[0:1, 0:1] * 0.125
    mean1 = v[1:2, 0:1] * 2.0 / count
    mean2 = v[2:3, 0:1] * 2.0 / count
    mean3 = v[3:4, 0:1] * 2.0 / count
    scale = mean1 * mean2 * 0.0625 * mean3
    b3 = tbuf[SWEEPS]
    bias = jnp.where(keep[...] > 0, b3 / scale, 1.0)
    balance = b3 * ubuf[SWEEPS - 1] / mean3
    for q in range(4):
        out_ref[pl.ds(q, RB, stride=4), :] = bias[:, q * 128:(q + 1) * 128]
        out_ref[pl.ds(4 * RB + q, RB, stride=4), :] = balance[:, q * 128:(q + 1) * 128]


def body(blocks, block_rows, block_cols, inter_counts, keep_mask):
    seg = keep_mask.shape[0]
    vm = pl.BlockSpec(memory_space=pltpu.VMEM)
    hbm = pl.BlockSpec(memory_space=pl.ANY)
    S = SWEEPS
    H = BS // 2
    dma = pltpu.SemaphoreType.DMA
    i32 = jnp.int32
    out = jax.ShapeDtypeStruct((seg // 64, 128), F32)

    def vf(*shape):
        return pltpu.VMEM(shape, F32)

    both = pl.pallas_call(
        kernel,
        out_shape=out,
        in_specs=[hbm] * 5,
        out_specs=vm,
        scratch_shapes=[
            pltpu.SMEM((SLOTS,), i32),
            pltpu.SMEM((SLOTS,), i32),
            pltpu.SMEM((1,), i32),
            pltpu.VMEM((seg // 128, 128), i32),
            pltpu.VMEM((SLOTS, BS, BS), BF16),
            pltpu.VMEM((IR_MAX, BS, BS), BF16),
            vf(RB, BS),
            vf(S + 1, RB, BS),
            vf(S, RB, BS),
            vf(RB + 8, BS),
            pltpu.VMEM((8, 8, 128), i32),
            pltpu.VMEM((128, SEL), BF16),
            pltpu.VMEM((SEL, 128), BF16),
            vf(8, 128),
            vf(RB, BS),
            vf(RB, BS),
            vf(S, 128, BS),
            vf(S, SEL, BS),
            vf(S, 4, 8, BS),
            vf(S, 1, BS),
            vf(S, 1, BS),
            vf(S, SEL, BS),
            vf(S, 1, BS),
            vf(S, 1, BS),
            vf(S, 128, BS),
            vf(S, 4, RB, BS),
            vf(S, 2, 4, RB, H),
            vf(S, RB, H),
            vf(S, 2, RB, H),
            vf(S, 2, 2, RB, H),
            vf(S, RB, H),
            vf(S, 4, RB, H),
            vf(8, 128),
            vf(8, 8, 128),
            vf(4, 8, 128),
            vf(4, 8, 128),
            dma((4,)),
            dma((SLOTS,)),
            dma, dma,
            dma((S,)), dma((S,)),
            dma((S,)), dma((S,)),
            dma((S,)), dma((S,)),
            dma((S,)), dma((S,)),
            dma((S,)), dma((S,)),
            dma((S,)), dma((S,)),
            dma((S,)), dma((S, 2)),
            dma((S,)), dma((S,)),
            dma((S,)), dma((S, 2)),
            dma((S,)), dma((S,)),
            dma, dma,
            dma, dma,
            dma, dma,
            dma, dma,
        ],
        compiler_params=pltpu.CompilerParams(
            collective_id=0, has_side_effects=True, vmem_limit_bytes=VMEM_LIMIT
        ),
        name="balance",
    )(block_rows, block_cols, inter_counts, keep_mask.reshape(seg // 128, 128), blocks)
    bias, balance = both[:seg // 128], both[seg // 128:]
    return bias.reshape(seg), balance.reshape(seg)


def solution(mesh):
    return jax.shard_map(
        body,
        mesh=mesh,
        in_specs=(
            P(("row", "col"), None, None),
            P(("row", "col")),
            P(("row", "col")),
            P(("row", "col")),
            P("row"),
        ),
        out_specs=(P("row"), P("row")),
        check_vma=False,
    )
```

```python
import jax
import jax.numpy as jnp
from jax import lax
from jax.experimental import pallas as pl
from jax.experimental.pallas import tpu as pltpu
from jax.sharding import PartitionSpec as P

IR_MAX = 8
SWEEPS = 3
RB = 16
BS = 512
SLOTS = 12
BAND = SLOTS - IR_MAX
SEL = 64
VMEM_LIMIT = 58 * 2**20

F32 = jnp.float32
BF16 = jnp.bfloat16
MESH = pl.DeviceIdType.MESH
RING = (2, 1, 3)


def split2(v):
    hi = v.astype(BF16)
    lo = (v - hi.astype(F32)).astype(BF16)
    return jnp.concatenate([hi, lo], axis=0)


def two_term_pick(pick, v):
    hi = v.astype(BF16)
    lo = (v - hi.astype(F32)).astype(BF16)
    return jnp.dot(pick, hi, preferred_element_type=F32) + jnp.dot(pick, lo, preferred_element_type=F32)


def full_max(v):
    m = jnp.max(jnp.max(v, axis=1, keepdims=True), axis=0, keepdims=True)
    return jnp.where(m > 0, m, 1.0)


def kernel(
    rows_hbm, cols_hbm, cnt_hbm, mask_hbm, blocks_ref,
    out_ref,
    rows_ref, cols_ref, cnt_ref, mask_ref,
    blk, blkt, keep, tbuf, ubuf, uloc, ids, pick, pickt, stat, rowband, colband,
    tab, selm, rsel, ulast, uprev, cparts, pprev, prevp, dense, rz,
    xa, za, ta, zb, xb, tb, wstat, stz, sty, stx,
    in_sem, blk_sem, ids_ss, ids_rs, tab_ss, tab_rs, sel_ss, sel_rs, up_ss, up_rs,
    cp_ss, cp_rs, pp_ss, pp_rs, dz_ss, dz_rs, xa_ss, xa_rs, za_ss, za_rs,
    zb_ss, zb_rs, xb_ss, xb_rs, ws_ss, ws_rs,
    sz_ss, sz_rs, sy_ss, sy_rs, sx_ss, sx_rs,
):
    row = lax.axis_index("row")
    col = lax.axis_index("col")
    zl = row // 8
    yc = lax.rem(row, 8)
    y = yc // 2
    core = lax.rem(row, 2)
    x = col // 2
    zh = lax.rem(col, 2)
    z = zh * 4 + zl
    half = BS // 2
    hub = core == 1
    worker = core == 0
    inner = jnp.where(zl < 2, 2, 6)
    two = (inner, 8 - inner)

    def chip(xx, yy, zz, cc):
        return (lax.rem(zz, 4) * 8 + yy * 2 + cc, xx * 2 + zz // 4)

    def z_peer(o, c):
        return chip(x, y, lax.rem(z + o, 8), c)

    def y_peer(o, c):
        return chip(x, lax.rem(y + o, 4), z, c)

    def x_peer(o, c):
        return chip(lax.rem(x + o, 4), y, z, c)

    def sibling(c):
        return chip(x, y, z, c)

    def step_peer(o):
        wrap = 7 if o == 1 else 0
        q = jnp.where(yc == wrap, lax.rem(z + o, 8), z)
        return (lax.rem(q, 4) * 8 + lax.rem(yc + o, 8), x * 2 + q // 4)

    def copy(src, dst, ss, rs, dev):
        return pltpu.make_async_remote_copy(
            src_ref=src, dst_ref=dst, send_sem=ss, recv_sem=rs,
            device_id=dev, device_id_type=MESH,
        )

    def seg(q, c):
        return pl.ds(pl.multiple_of(q * 2 * RB + c * RB, RB), RB)

    def eight(i):
        return pl.ds(pl.multiple_of(i * 8, 8), 8)

    own = seg(zl, core)
    mine = eight(yc)

    def tab_copies(s, h, c):
        out = [
            copy(tab.at[s, h, own], tab.at[s, h, own], tab_ss.at[s, h], tab_rs.at[s, h], z_peer(o, 1))
            for i, o in enumerate((two[c], 1, 7))
        ]
        if c == 0:
            out.append(copy(tab.at[s, h, own], tab.at[s, h, own], tab_ss.at[s, h], tab_rs.at[s, h], sibling(1)))
        return out

    def ids_copies(c):
        out = [copy(ids.at[yc], ids.at[yc], ids_ss, ids_rs, y_peer(o, 1)) for o in RING]
        if c == 0:
            out.append(copy(ids.at[yc], ids.at[yc], ids_ss, ids_rs, sibling(1)))
        return out

    def cp_copies(s, c):
        out = [
            copy(cparts.at[s, mine], cparts.at[s, mine], cp_ss.at[s], cp_rs.at[s], y_peer(o, 1))
            for o in RING
        ]
        if c == 0:
            out.append(copy(cparts.at[s, mine], cparts.at[s, mine], cp_ss.at[s], cp_rs.at[s], sibling(1)))
        return out

    def up_copy(s):
        return copy(ulast.at[s], uprev.at[s], up_ss.at[s], up_rs.at[s], step_peer(1))

    def pp_copy(s):
        return copy(pprev.at[s], prevp.at[s], pp_ss.at[s], pp_rs.at[s], step_peer(7))

    def sel_copies(s, h):
        out = [
            copy(selm.at[s, h, eight(lax.rem(y + o, 4) * 2 + c)], rsel.at[s, h, y],
                 sel_ss.at[s, h], sel_rs.at[s, h], y_peer(o, c))
            for o in RING for c in (0, 1)
        ]
        return out + [
            copy(selm.at[s, h, eight(y * 2)], rsel.at[s, h, y], sel_ss.at[s, h], sel_rs.at[s, h], sibling(0))
        ]

    def dz_copies(s):
        out = [
            copy(dense.at[s, seg(lax.rem(zl + o, 4), c)], rz.at[s, i],
                 dz_ss.at[s], dz_rs.at[s], z_peer(o, c))
            for c in (0, 1) for i, o in enumerate((two[c], 1, 7))
        ]
        return out + [copy(dense.at[s, seg(zl, 0)], rz.at[s, 3], dz_ss.at[s], dz_rs.at[s], sibling(0))]

    def xa_copies(s, c):
        out = [
            copy(xa.at[s, c, x], xa.at[s, c, x], xa_ss.at[s], xa_rs.at[s], x_peer(o, 1))
            for o in RING
        ]
        if c == 0:
            out.append(copy(xa.at[s, 0, x], xa.at[s, 0, x], xa_ss.at[s], xa_rs.at[s], sibling(1)))
        return out

    def za_copies(s):
        return [
            copy(za.at[s], ta.at[s, 1], za_ss.at[s], za_rs.at[s], z_peer(4, 0)),
            copy(ta.at[s, 0], ta.at[s, 1], za_ss.at[s], za_rs.at[s], z_peer(4, 1)),
            copy(za.at[s], ta.at[s, 0], za_ss.at[s], za_rs.at[s], sibling(0)),
        ]

    def zb_copies(s, c):
        out = [copy(zb.at[s, c, 0], zb.at[s, c, 1], zb_ss.at[s], zb_rs.at[s], z_peer(4, 1))]
        if c == 0:
            out.append(copy(zb.at[s, 0, 0], zb.at[s, 0, 0], zb_ss.at[s], zb_rs.at[s], sibling(1)))
        return out

    def xb_copies(s):
        out = []
        for o in RING:
            out.append(copy(xb.at[s], tb.at[s, x], xb_ss.at[s], xb_rs.at[s], x_peer(o, 0)))
            out.append(copy(tb.at[s, x], tb.at[s, x], xb_ss.at[s], xb_rs.at[s], x_peer(o, 1)))
        return out + [copy(xb.at[s], tb.at[s, x], xb_ss.at[s], xb_rs.at[s], sibling(0))]

    def sx_copies():
        out = [
            copy(stx.at[x], stx.at[x], sx_ss, sx_rs, x_peer(o, c))
            for o in RING for c in (0, 1)
        ]
        return out + [copy(stx.at[x], stx.at[x], sx_ss, sx_rs, sibling(0))]

    def start(copies):
        for c in copies:
            c.start()

    def done(sem, like):
        pltpu.make_async_copy(like, like, sem).wait()

    def by_core(f):
        pl.when(worker)(lambda: f(0))
        pl.when(hub)(lambda: f(1))

    loads = [
        pltpu.make_async_copy(src, dst, in_sem.at[i])
        for i, (src, dst) in enumerate((
            (rows_hbm, rows_ref), (cols_hbm, cols_ref), (cnt_hbm, cnt_ref), (mask_hbm, mask_ref),
        ))
    ] + [
        pltpu.make_async_copy(blocks_ref.at[k], blk.at[k], blk_sem.at[k])
        for k in (*range(BAND, SLOTS), *range(BAND))
    ]
    loads[3].start()

    barrier = pltpu.get_barrier_semaphore()

    def greet(c):
        if c == 0:
            peers = (
                [z_peer(o, 1) for o in (2, 6, 1, 7)] + [y_peer(o, 1) for o in RING]
                + [x_peer(o, 1) for o in RING] + [sibling(1), step_peer(7)]
            )
        else:
            peers = (
                [z_peer(o, d) for o in (2, 6, 1, 7) for d in (0, 1)]
                + [y_peer(o, d) for o in RING for d in (0, 1)]
                + [x_peer(o, d) for o in RING for d in (0, 1)]
                + [sibling(0), step_peer(1)]
            )
        return peers

    def signal_peers(c):
        for dev in greet(c):
            pl.semaphore_signal(barrier, inc=1, device_id=dev, device_id_type=MESH)

    by_core(signal_peers)
    start([*loads[:3], *loads[4:]])
    for c in loads[:4]:
        c.wait()

    live = cnt_ref[0]
    row_l = [lax.rem(rows_ref[k], RB) for k in range(SLOTS)]
    col_l = [cols_ref[k] - row * RB for k in range(BAND)]
    here = [(c >= 0) & (c < RB) for c in col_l]
    lane = lax.broadcasted_iota(jnp.int32, (8, 128), 1)
    iota8 = lax.broadcasted_iota(jnp.int32, (8, BS), 0)
    iota16 = lax.broadcasted_iota(jnp.int32, (RB, BS), 0)
    iota24 = lax.broadcasted_iota(jnp.int32, (RB + 8, BS), 0)

    idv = jnp.zeros((8, 128), jnp.int32)
    for k in range(IR_MAX):
        code = jnp.where(k < live, cols_ref[BAND + k] + 1, 0)
        idv = jnp.where(lane == yc * 8 + k, code, idv)
    ids[yc] = idv
    for q in range(4):
        keep[:, q * 128:(q + 1) * 128] = mask_ref[pl.ds(q, RB, stride=4), :].astype(F32)
    tbuf[0] = jnp.full((RB, BS), 4.0, F32)
    uloc[...] = jnp.zeros_like(uloc)

    def total_of(v):
        return jnp.sum(jnp.sum(v, axis=1, keepdims=True), axis=0, keepdims=True)

    sub = lax.broadcasted_iota(jnp.int32, (8, 128), 0)
    stat[...] = jnp.where(sub == 0, total_of(keep[...]), 0.0)

    def add_share(s, v):
        stat[...] += jnp.where(sub == s + 1, total_of(v), 0.0)

    def weights(s, h, send=True):
        lanes = slice(h * half, (h + 1) * half)
        u = jnp.where(keep[:, lanes] > 0, 4.0 / tbuf[s, :, lanes], 0.0)
        tab[s, h, own] = u
        if send:
            by_core(lambda c: start(tab_copies(s, h, c)))
        ubuf[s, :, lanes] = u
        uloc[0:RB, lanes] = u
        ulast[s, :, lanes] = u[RB - 1:]

    def inter_columns(s):
        m = full_max(uloc[0:RB])
        inv = 1.0 / m
        acc = None
        for k in range(IR_MAX):
            vec = uloc[pl.ds(row_l[BAND + k], 1), :] * inv
            target = jnp.where(k < live, k, -1)
            lhs = split2(jnp.where(iota8 == target, vec, 0.0))
            part = jnp.dot(lhs, blk[BAND + k], preferred_element_type=F32)
            acc = part if acc is None else acc + part
        cparts[s, mine] = (acc[:8] + acc[8:]) * m

    def band_columns(s):
        m = full_max(uloc[0:RB])
        inv = 1.0 / m
        acc = None
        for k in range(BAND):
            vec = uloc[pl.ds(row_l[k], 1), :] * inv
            target = jnp.where(here[k], col_l[k], RB)
            lhs = split2(jnp.where(iota24 == target, vec, 0.0))
            part = jnp.dot(lhs, blk[k], preferred_element_type=F32)
            acc = part if acc is None else acc + part
        acc = (acc[:RB + 8] + acc[RB + 8:]) * m
        colband[...] = acc[:RB]
        pprev[s] = acc[RB:RB + 1]

    def transpose_inter():
        def one(k, carry):
            blkt[k] = blk[BAND + k].T
            return carry

        lax.fori_loop(0, IR_MAX, one, 0)

    weights(0, 0, send=False)
    weights(0, 1, send=False)

    def open_up(c):
        pl.semaphore_wait(barrier, len(greet(c)))
        start([*tab_copies(0, 0, c), *tab_copies(0, 1, c), up_copy(0), *ids_copies(c)])

    by_core(open_up)

    def sweep(s, carry):
        first = s == 0
        last = s == SWEEPS - 1

        @pl.when(first)
        def _():
            for c in loads[4:4 + IR_MAX]:
                c.wait()

        inter_columns(s)
        by_core(lambda c: start(cp_copies(s, c)))

        @pl.when(first)
        def _():
            for c in loads[4 + IR_MAX:]:
                c.wait()

        band_columns(s)
        pp_copy(s).start()
        pl.when(first)(transpose_inter)

        up_copy(s).wait_recv()
        uloc[RB:RB + 1] = uprev[s]
        add_share(s, uloc[0:RB] * colband[...])
        add_share(s, uprev[s] * pprev[s])

        @pl.when(worker & last)
        def _():
            copy(stat, wstat, ws_ss, ws_rs, sibling(1)).start()

        @pl.when(hub)
        def _():
            @pl.when(first)
            def _():
                done(ids_rs, ids.at[0:7])
                code = ids[0]
                for p in range(1, 8):
                    code = code + ids[p]
                code = code[0:1]
                cc = jnp.maximum(code - 1, 0)
                want = jnp.where(
                    (code > 0) & (((cc // 32) % 4) == y), (cc // 128) * 32 + cc % 32, -1
                )
                full = jnp.where(
                    lax.broadcasted_iota(jnp.int32, (128, 128), 0) == want, 1.0, 0.0
                )
                pick[...] = full[:, :SEL].astype(BF16)
                pickt[...] = full.T[:SEL].astype(BF16)

            for h in (0, 1):
                done(tab_rs.at[s, h], tab.at[s, h, 0:7 * RB])
                selm[s, h] = two_term_pick(pickt[...], tab[s, h])
                start(sel_copies(s, h))
                rsel[s, h, y] = selm[s, h, mine]

            done(cp_rs.at[s], cparts.at[s, 0:56])
            dense[s] = two_term_pick(pick[...], cparts[s])
            start(dz_copies(s))
            rz[s, 3] = dense[s, own]

            @pl.when(last)
            def _():
                done(ws_rs, wstat)
                add_share(s, dense[s, :, :half] * tab[s, 0] + dense[s, :, half:] * tab[s, 1])
                stz[z] = stat[...] + wstat[...]
                for o in range(1, 8):
                    copy(stz.at[z], stz.at[z], sz_ss, sz_rs, z_peer(o, 1)).start()

        m = full_max(uloc[...])
        inv = 1.0 / m
        acc = None
        for k in range(BAND):
            vec = uloc[pl.ds(jnp.where(here[k], col_l[k], RB), 1), :] * inv
            lhs = split2(jnp.where(iota16 == row_l[k], vec, 0.0))
            part = lax.dot_general(
                lhs, blk[k], (((1,), (1,)), ((), ())), preferred_element_type=F32
            )
            acc = part if acc is None else acc + part
        rowband[...] = (acc[:RB] + acc[RB:]) * m

        total = rowband[...] + colband[...]
        for h in (0, 1):
            by_core(lambda c, h=h: done(sel_rs.at[s, h], rsel.at[s, h, 0:4 - c]))
            ucol = (rsel[s, h, 0] + rsel[s, h, 1]) + (rsel[s, h, 2] + rsel[s, h, 3])
            m2 = full_max(ucol)
            ucol = ucol * (1.0 / m2)
            acc = None
            for k in range(IR_MAX):
                target = jnp.where(k < live, row_l[BAND + k], -1)
                lhs = split2(jnp.where(iota16[:, :half] == target, ucol[k:k + 1], 0.0))
                part = jnp.dot(lhs, blkt[k, h * half:(h + 1) * half, :], preferred_element_type=F32)
                acc = part if acc is None else acc + part
            total = total + (acc[:RB] + acc[RB:]) * m2

        pp_copy(s).wait_recv()
        total = total + jnp.where(iota16 == RB - 1, prevp[s], 0.0)

        by_core(lambda c: done(dz_rs.at[s], rz.at[s, 0:4 - c]))
        total = total + ((rz[s, 0] + rz[s, 1]) + (rz[s, 2] + rz[s, 3]))

        zb[s, core, 0] = total[:, half:]
        by_core(lambda c: start(zb_copies(s, c)))
        xa[s, core, x] = total[:, :half]
        by_core(lambda c: start(xa_copies(s, c)))

        @pl.when(worker)
        def _():
            for h in (0, 1):
                done(tab_ss.at[s, h], tab.at[s, h, 0:4 * RB])
            done(cp_ss.at[s], cparts.at[s, 0:32])
            up_copy(s).wait_send()
            pp_copy(s).wait_send()

        @pl.when(hub)
        def _():
            @pl.when(jnp.logical_not(last))
            def _():
                add_share(s, dense[s, :, :half] * tab[s, 0] + dense[s, :, half:] * tab[s, 1])

            @pl.when(last)
            def _():
                done(sz_ss, stz.at[0:7])
                done(sz_rs, stz.at[0:7])
                v = stz[0]
                for p in range(1, 8):
                    v = v + stz[p]
                sty[y] = v
                for o in RING:
                    copy(sty.at[y], sty.at[y], sy_ss, sy_rs, y_peer(o, 1)).start()

            for h in (0, 1):
                done(tab_ss.at[s, h], tab.at[s, h, 0:3 * RB])
                done(sel_ss.at[s, h], selm.at[s, h, 0:56])
            done(cp_ss.at[s], cparts.at[s, 0:24])
            done(dz_ss.at[s], dense.at[s, 0:7 * RB])
            up_copy(s).wait_send()
            pp_copy(s).wait_send()

            done(xa_rs.at[s], dense.at[s, 0:56])
            za[s] = (xa[s, 0, 0] + xa[s, 0, 1]) + (xa[s, 0, 2] + xa[s, 0, 3])
            ta[s, 0] = (xa[s, 1, 0] + xa[s, 1, 1]) + (xa[s, 1, 2] + xa[s, 1, 3])
            start(za_copies(s))

            @pl.when(last)
            def _():
                done(sy_ss, sty.at[0:3])
                done(sy_rs, sty.at[0:3])
                stx[x] = (sty[0] + sty[1]) + (sty[2] + sty[3])
                start(sx_copies())

            done(zb_rs.at[s], dense.at[s, 0:24])
            xb[s] = zb[s, 0, 0] + zb[s, 0, 1]
            tb[s, x] = zb[s, 1, 0] + zb[s, 1, 1]
            start(xb_copies(s))

            done(za_ss.at[s], dense.at[s, 0:24])
            done(xb_ss.at[s], dense.at[s, 0:56])

        def rest(c):
            done(xa_ss.at[s], xa.at[s, 0, 0:4 - c])
            done(zb_ss.at[s], zb.at[s, 0, 0:2 - c])
            done(za_rs.at[s], ta.at[s, 0:2 - c])

        by_core(rest)
        n = s + 1
        tbuf[n, :, :half] = ta[s, 0] + ta[s, 1]
        pl.when(jnp.logical_not(last))(lambda: weights(n, 0))
        by_core(lambda c: done(xb_rs.at[s], tb.at[s, 0:4 - c]))
        tbuf[n, :, half:] = (tb[s, 0] + tb[s, 1]) + (tb[s, 2] + tb[s, 3])

        @pl.when(jnp.logical_not(last))
        def _():
            weights(n, 1)
            up_copy(n).start()

        return carry

    lax.fori_loop(0, SWEEPS, sweep, 0)

    def finish(c):
        done(sx_rs, stx.at[0:4 - c])
        done(ids_ss, ids.at[0:4 - c])
        if c == 0:
            done(ws_ss, stat)
        else:
            done(sx_ss, stz.at[0:7])

    by_core(finish)
    v = (stx[0] + stx[1]) + (stx[2] + stx[3])
    count = v[0:1, 0:1] * 0.125
    mean1 = v[1:2, 0:1] * 2.0 / count
    mean2 = v[2:3, 0:1] * 2.0 / count
    mean3 = v[3:4, 0:1] * 2.0 / count
    scale = mean1 * mean2 * 0.0625 * mean3
    b3 = tbuf[SWEEPS]
    bias = jnp.where(keep[...] > 0, b3 / scale, 1.0)
    balance = b3 * ubuf[SWEEPS - 1] / mean3
    for q in range(4):
        out_ref[pl.ds(q, RB, stride=4), :] = bias[:, q * 128:(q + 1) * 128]
        out_ref[pl.ds(4 * RB + q, RB, stride=4), :] = balance[:, q * 128:(q + 1) * 128]


def body(blocks, block_rows, block_cols, inter_counts, keep_mask):
    seg = keep_mask.shape[0]
    vm = pl.BlockSpec(memory_space=pltpu.VMEM)
    hbm = pl.BlockSpec(memory_space=pl.ANY)
    S = SWEEPS
    H = BS // 2
    dma = pltpu.SemaphoreType.DMA
    i32 = jnp.int32
    out = jax.ShapeDtypeStruct((seg // 64, 128), F32)

    def vf(*shape):
        return pltpu.VMEM(shape, F32)

    both = pl.pallas_call(
        kernel,
        out_shape=out,
        in_specs=[hbm] * 5,
        out_specs=vm,
        scratch_shapes=[
            pltpu.SMEM((SLOTS,), i32),
            pltpu.SMEM((SLOTS,), i32),
            pltpu.SMEM((1,), i32),
            pltpu.VMEM((seg // 128, 128), i32),
            pltpu.VMEM((SLOTS, BS, BS), BF16),
            pltpu.VMEM((IR_MAX, BS, BS), BF16),
            vf(RB, BS),
            vf(S + 1, RB, BS),
            vf(S, RB, BS),
            vf(RB + 8, BS),
            pltpu.VMEM((8, 8, 128), i32),
            pltpu.VMEM((128, SEL), BF16),
            pltpu.VMEM((SEL, 128), BF16),
            vf(8, 128),
            vf(RB, BS),
            vf(RB, BS),
            vf(S, 2, 128, H),
            vf(S, 2, SEL, H),
            vf(S, 2, 4, 8, H),
            vf(S, 1, BS),
            vf(S, 1, BS),
            vf(S, SEL, BS),
            vf(S, 1, BS),
            vf(S, 1, BS),
            vf(S, 128, BS),
            vf(S, 4, RB, BS),
            vf(S, 2, 4, RB, H),
            vf(S, RB, H),
            vf(S, 2, RB, H),
            vf(S, 2, 2, RB, H),
            vf(S, RB, H),
            vf(S, 4, RB, H),
            vf(8, 128),
            vf(8, 8, 128),
            vf(4, 8, 128),
            vf(4, 8, 128),
            dma((4,)),
            dma((SLOTS,)),
            dma, dma,
            dma((S, 2)), dma((S, 2)),
            dma((S, 2)), dma((S, 2)),
            dma((S,)), dma((S,)),
            dma((S,)), dma((S,)),
            dma((S,)), dma((S,)),
            dma((S,)), dma((S,)),
            dma((S,)), dma((S,)),
            dma((S,)), dma((S,)),
            dma((S,)), dma((S,)),
            dma((S,)), dma((S,)),
            dma, dma,
            dma, dma,
            dma, dma,
            dma, dma,
        ],
        compiler_params=pltpu.CompilerParams(
            collective_id=0, has_side_effects=True, vmem_limit_bytes=VMEM_LIMIT
        ),
        name="balance",
    )(block_rows, block_cols, inter_counts, keep_mask.reshape(seg // 128, 128), blocks)
    bias, balance = both[:seg // 128], both[seg // 128:]
    return bias.reshape(seg), balance.reshape(seg)


def solution(mesh):
    return jax.shard_map(
        body,
        mesh=mesh,
        in_specs=(
            P(("row", "col"), None, None),
            P(("row", "col")),
            P(("row", "col")),
            P(("row", "col")),
            P("row"),
        ),
        out_specs=(P("row"), P("row")),
        check_vma=False,
    )
```

```python
import jax
import jax.numpy as jnp
from jax import lax
from jax.experimental import pallas as pl
from jax.experimental.pallas import tpu as pltpu
from jax.sharding import PartitionSpec as P

IR_MAX = 8
SWEEPS = 3
RB = 16
BS = 512
SLOTS = 12
BAND = SLOTS - IR_MAX
SEL = 64
VMEM_LIMIT = 58 * 2**20

F32 = jnp.float32
BF16 = jnp.bfloat16
MESH = pl.DeviceIdType.MESH
RING = (2, 1, 3)


def split2(v):
    hi = v.astype(BF16)
    lo = (v - hi.astype(F32)).astype(BF16)
    return jnp.concatenate([hi, lo], axis=0)


def two_term_pick(pick, v):
    hi = v.astype(BF16)
    lo = (v - hi.astype(F32)).astype(BF16)
    return jnp.dot(pick, hi, preferred_element_type=F32) + jnp.dot(pick, lo, preferred_element_type=F32)


def full_max(v):
    m = jnp.max(jnp.max(v, axis=1, keepdims=True), axis=0, keepdims=True)
    return jnp.where(m > 0, m, 1.0)


def kernel(
    rows_hbm, cols_hbm, cnt_hbm, mask_hbm, blocks_ref,
    out_ref,
    rows_ref, cols_ref, cnt_ref, mask_ref,
    blk, blkt, keep, tbuf, ubuf, uloc, ids, pick, pickt, stat, rowband, colband,
    tab, selm, rsel, ulast, uprev, cparts, pprev, prevp, dense, rz,
    xa, za, ta, zb, xb, tb, wstat, stz, sty, stx,
    in_sem, blk_sem, ids_ss, ids_rs, tab_ss, tab_rs, sel_ss, sel_rs, up_ss, up_rs,
    cp_ss, cp_rs, pp_ss, pp_rs, dz_ss, dz_rs, xa_ss, xa_rs, za_ss, za_rs,
    zb_ss, zb_rs, xb_ss, xb_rs, ws_ss, ws_rs,
    sz_ss, sz_rs, sy_ss, sy_rs, sx_ss, sx_rs,
):
    row = lax.axis_index("row")
    col = lax.axis_index("col")
    zl = row // 8
    yc = lax.rem(row, 8)
    y = yc // 2
    core = lax.rem(row, 2)
    x = col // 2
    zh = lax.rem(col, 2)
    z = zh * 4 + zl
    half = BS // 2
    hub = core == 1
    worker = core == 0
    inner = jnp.where(zl < 2, 2, 6)
    two = (inner, 8 - inner)

    def chip(xx, yy, zz, cc):
        return (lax.rem(zz, 4) * 8 + yy * 2 + cc, xx * 2 + zz // 4)

    def z_peer(o, c):
        return chip(x, y, lax.rem(z + o, 8), c)

    def y_peer(o, c):
        return chip(x, lax.rem(y + o, 4), z, c)

    def x_peer(o, c):
        return chip(lax.rem(x + o, 4), y, z, c)

    def sibling(c):
        return chip(x, y, z, c)

    def step_peer(o):
        wrap = 7 if o == 1 else 0
        q = jnp.where(yc == wrap, lax.rem(z + o, 8), z)
        return (lax.rem(q, 4) * 8 + lax.rem(yc + o, 8), x * 2 + q // 4)

    def copy(src, dst, ss, rs, dev):
        return pltpu.make_async_remote_copy(
            src_ref=src, dst_ref=dst, send_sem=ss, recv_sem=rs,
            device_id=dev, device_id_type=MESH,
        )

    def seg(q, c):
        return pl.ds(pl.multiple_of(q * 2 * RB + c * RB, RB), RB)

    def eight(i):
        return pl.ds(pl.multiple_of(i * 8, 8), 8)

    own = seg(zl, core)
    mine = eight(yc)

    def tab_copies(s, h, c):
        out = [
            copy(tab.at[s, h, own], tab.at[s, h, own], tab_ss.at[h], tab_rs.at[s, h], z_peer(o, 1))
            for i, o in enumerate((two[c], 1, 7))
        ]
        if c == 0:
            out.append(copy(tab.at[s, h, own], tab.at[s, h, own], tab_ss.at[h], tab_rs.at[s, h], sibling(1)))
        return out

    def ids_copies(c):
        out = [copy(ids.at[yc], ids.at[yc], ids_ss, ids_rs, y_peer(o, 1)) for o in RING]
        if c == 0:
            out.append(copy(ids.at[yc], ids.at[yc], ids_ss, ids_rs, sibling(1)))
        return out

    def cp_copies(s, c):
        out = [
            copy(cparts.at[s, mine], cparts.at[s, mine], cp_ss, cp_rs.at[s], y_peer(o, 1))
            for o in RING
        ]
        if c == 0:
            out.append(copy(cparts.at[s, mine], cparts.at[s, mine], cp_ss, cp_rs.at[s], sibling(1)))
        return out

    def up_copy(s):
        return copy(ulast.at[s], uprev.at[s], up_ss, up_rs.at[s], step_peer(1))

    def pp_copy(s):
        return copy(pprev.at[s], prevp.at[s], pp_ss, pp_rs.at[s], step_peer(7))

    def sel_copies(s, h):
        out = [
            copy(selm.at[s, h, eight(lax.rem(y + o, 4) * 2 + c)], rsel.at[s, h, y],
                 sel_ss.at[h], sel_rs.at[s, h], y_peer(o, c))
            for o in RING for c in (0, 1)
        ]
        return out + [
            copy(selm.at[s, h, eight(y * 2)], rsel.at[s, h, y], sel_ss.at[h], sel_rs.at[s, h], sibling(0))
        ]

    def dz_copies(s):
        out = [
            copy(dense.at[s, seg(lax.rem(zl + o, 4), c)], rz.at[s, i],
                 dz_ss, dz_rs.at[s], z_peer(o, c))
            for c in (0, 1) for i, o in enumerate((two[c], 1, 7))
        ]
        return out + [copy(dense.at[s, seg(zl, 0)], rz.at[s, 3], dz_ss, dz_rs.at[s], sibling(0))]

    def xa_copies(s, c):
        out = [
            copy(xa.at[s, c, x], xa.at[s, c, x], xa_ss, xa_rs.at[s], x_peer(o, 1))
            for o in RING
        ]
        if c == 0:
            out.append(copy(xa.at[s, 0, x], xa.at[s, 0, x], xa_ss, xa_rs.at[s], sibling(1)))
        return out

    def za_copies(s):
        return [
            copy(za.at[s], ta.at[s, 1], za_ss, za_rs.at[s], z_peer(4, 0)),
            copy(ta.at[s, 0], ta.at[s, 1], za_ss, za_rs.at[s], z_peer(4, 1)),
            copy(za.at[s], ta.at[s, 0], za_ss, za_rs.at[s], sibling(0)),
        ]

    def zb_copies(s, c):
        out = [copy(zb.at[s, c, 0], zb.at[s, c, 1], zb_ss, zb_rs.at[s], z_peer(4, 1))]
        if c == 0:
            out.append(copy(zb.at[s, 0, 0], zb.at[s, 0, 0], zb_ss, zb_rs.at[s], sibling(1)))
        return out

    def xb_copies(s):
        out = []
        for o in RING:
            out.append(copy(xb.at[s], tb.at[s, x], xb_ss, xb_rs.at[s], x_peer(o, 0)))
            out.append(copy(tb.at[s, x], tb.at[s, x], xb_ss, xb_rs.at[s], x_peer(o, 1)))
        return out + [copy(xb.at[s], tb.at[s, x], xb_ss, xb_rs.at[s], sibling(0))]

    def sx_copies():
        out = [
            copy(stx.at[x], stx.at[x], sx_ss, sx_rs, x_peer(o, c))
            for o in RING for c in (0, 1)
        ]
        return out + [copy(stx.at[x], stx.at[x], sx_ss, sx_rs, sibling(0))]

    def start(copies):
        for c in copies:
            c.start()

    def done(sem, like):
        pltpu.make_async_copy(like, like, sem).wait()

    def by_core(f):
        pl.when(worker)(lambda: f(0))
        pl.when(hub)(lambda: f(1))

    loads = [
        pltpu.make_async_copy(src, dst, in_sem.at[i])
        for i, (src, dst) in enumerate((
            (rows_hbm, rows_ref), (cols_hbm, cols_ref), (cnt_hbm, cnt_ref), (mask_hbm, mask_ref),
        ))
    ] + [
        pltpu.make_async_copy(blocks_ref.at[k], blk.at[k], blk_sem.at[1 if k < BAND else 0])
        for k in (*range(BAND, SLOTS), *range(BAND))
    ]
    loads[3].start()

    barrier = pltpu.get_barrier_semaphore()

    def greet(c):
        if c == 0:
            peers = (
                [z_peer(o, 1) for o in (2, 6, 1, 7)] + [y_peer(o, 1) for o in RING]
                + [x_peer(o, 1) for o in RING] + [sibling(1), step_peer(7)]
            )
        else:
            peers = (
                [z_peer(o, d) for o in (2, 6, 1, 7) for d in (0, 1)]
                + [y_peer(o, d) for o in RING for d in (0, 1)]
                + [x_peer(o, d) for o in RING for d in (0, 1)]
                + [sibling(0), step_peer(1)]
            )
        return peers

    def signal_peers(c):
        for dev in greet(c):
            pl.semaphore_signal(barrier, inc=1, device_id=dev, device_id_type=MESH)

    by_core(signal_peers)
    start([*loads[:3], *loads[4:]])
    for c in loads[:4]:
        c.wait()

    live = cnt_ref[0]
    row_l = [lax.rem(rows_ref[k], RB) for k in range(SLOTS)]
    col_l = [cols_ref[k] - row * RB for k in range(BAND)]
    here = [(c >= 0) & (c < RB) for c in col_l]
    lane = lax.broadcasted_iota(jnp.int32, (8, 128), 1)
    iota8 = lax.broadcasted_iota(jnp.int32, (8, BS), 0)
    iota16 = lax.broadcasted_iota(jnp.int32, (RB, BS), 0)
    iota24 = lax.broadcasted_iota(jnp.int32, (RB + 8, BS), 0)

    idv = jnp.zeros((8, 128), jnp.int32)
    for k in range(IR_MAX):
        code = jnp.where(k < live, cols_ref[BAND + k] + 1, 0)
        idv = jnp.where(lane == yc * 8 + k, code, idv)
    ids[yc] = idv
    for q in range(4):
        keep[:, q * 128:(q + 1) * 128] = mask_ref[pl.ds(q, RB, stride=4), :].astype(F32)
    tbuf[0] = jnp.full((RB, BS), 4.0, F32)
    uloc[...] = jnp.zeros_like(uloc)

    def total_of(v):
        return jnp.sum(jnp.sum(v, axis=1, keepdims=True), axis=0, keepdims=True)

    sub = lax.broadcasted_iota(jnp.int32, (8, 128), 0)
    stat[...] = jnp.where(sub == 0, total_of(keep[...]), 0.0)

    def add_share(s, v):
        stat[...] += jnp.where(sub == s + 1, total_of(v), 0.0)

    def weights(s, h, send=True):
        lanes = slice(h * half, (h + 1) * half)
        u = jnp.where(keep[:, lanes] > 0, 4.0 / tbuf[s, :, lanes], 0.0)
        tab[s, h, own] = u
        if send:
            by_core(lambda c: start(tab_copies(s, h, c)))
        ubuf[s, :, lanes] = u
        uloc[0:RB, lanes] = u
        ulast[s, :, lanes] = u[RB - 1:]

    def inter_columns(s):
        m = full_max(uloc[0:RB])
        inv = 1.0 / m
        acc = None
        for k in range(IR_MAX):
            vec = uloc[pl.ds(row_l[BAND + k], 1), :] * inv
            target = jnp.where(k < live, k, -1)
            lhs = split2(jnp.where(iota8 == target, vec, 0.0))
            part = jnp.dot(lhs, blk[BAND + k], preferred_element_type=F32)
            acc = part if acc is None else acc + part
        cparts[s, mine] = (acc[:8] + acc[8:]) * m

    def band_columns(s):
        m = full_max(uloc[0:RB])
        inv = 1.0 / m
        acc = None
        for k in range(BAND):
            vec = uloc[pl.ds(row_l[k], 1), :] * inv
            target = jnp.where(here[k], col_l[k], RB)
            lhs = split2(jnp.where(iota24 == target, vec, 0.0))
            part = jnp.dot(lhs, blk[k], preferred_element_type=F32)
            acc = part if acc is None else acc + part
        acc = (acc[:RB + 8] + acc[RB + 8:]) * m
        colband[...] = acc[:RB]
        pprev[s] = acc[RB:RB + 1]

    def transpose_inter():
        def one(k, carry):
            blkt[k] = blk[BAND + k].T
            return carry

        lax.fori_loop(0, IR_MAX, one, 0)

    weights(0, 0, send=False)
    weights(0, 1, send=False)

    def open_up(c):
        pl.semaphore_wait(barrier, len(greet(c)))
        start([*tab_copies(0, 0, c), *tab_copies(0, 1, c), up_copy(0), *ids_copies(c)])

    by_core(open_up)

    def sweep(s, carry):
        first = s == 0
        last = s == SWEEPS - 1

        @pl.when(first)
        def _():
            done(blk_sem.at[0], blk.at[BAND:])

        inter_columns(s)
        by_core(lambda c: start(cp_copies(s, c)))

        @pl.when(first)
        def _():
            done(blk_sem.at[1], blk.at[:BAND])

        band_columns(s)
        pp_copy(s).start()
        pl.when(first)(transpose_inter)

        up_copy(s).wait_recv()
        uloc[RB:RB + 1] = uprev[s]
        add_share(s, uloc[0:RB] * colband[...])
        add_share(s, uprev[s] * pprev[s])

        @pl.when(worker & last)
        def _():
            copy(stat, wstat, ws_ss, ws_rs, sibling(1)).start()

        @pl.when(hub)
        def _():
            @pl.when(first)
            def _():
                done(ids_rs, ids.at[0:7])
                code = ids[0]
                for p in range(1, 8):
                    code = code + ids[p]
                code = code[0:1]
                cc = jnp.maximum(code - 1, 0)
                want = jnp.where(
                    (code > 0) & (((cc // 32) % 4) == y), (cc // 128) * 32 + cc % 32, -1
                )
                full = jnp.where(
                    lax.broadcasted_iota(jnp.int32, (128, 128), 0) == want, 1.0, 0.0
                )
                pick[...] = full[:, :SEL].astype(BF16)
                pickt[...] = full.T[:SEL].astype(BF16)

            for h in (0, 1):
                done(tab_rs.at[s, h], tab.at[s, h, 0:7 * RB])
                selm[s, h] = two_term_pick(pickt[...], tab[s, h])
                start(sel_copies(s, h))
                rsel[s, h, y] = selm[s, h, mine]

            done(cp_rs.at[s], cparts.at[s, 0:56])
            dense[s] = two_term_pick(pick[...], cparts[s])
            start(dz_copies(s))
            rz[s, 3] = dense[s, own]

            @pl.when(last)
            def _():
                done(ws_rs, wstat)
                add_share(s, dense[s, :, :half] * tab[s, 0] + dense[s, :, half:] * tab[s, 1])
                stz[z] = stat[...] + wstat[...]
                for o in range(1, 8):
                    copy(stz.at[z], stz.at[z], sz_ss, sz_rs, z_peer(o, 1)).start()

        m = full_max(uloc[...])
        inv = 1.0 / m
        acc = None
        for k in range(BAND):
            vec = uloc[pl.ds(jnp.where(here[k], col_l[k], RB), 1), :] * inv
            lhs = split2(jnp.where(iota16 == row_l[k], vec, 0.0))
            part = lax.dot_general(
                lhs, blk[k], (((1,), (1,)), ((), ())), preferred_element_type=F32
            )
            acc = part if acc is None else acc + part
        rowband[...] = (acc[:RB] + acc[RB:]) * m

        total = rowband[...] + colband[...]
        for h in (0, 1):
            by_core(lambda c, h=h: done(sel_rs.at[s, h], rsel.at[s, h, 0:4 - c]))
            ucol = (rsel[s, h, 0] + rsel[s, h, 1]) + (rsel[s, h, 2] + rsel[s, h, 3])
            m2 = full_max(ucol)
            ucol = ucol * (1.0 / m2)
            acc = None
            for k in range(IR_MAX):
                target = jnp.where(k < live, row_l[BAND + k], -1)
                lhs = split2(jnp.where(iota16[:, :half] == target, ucol[k:k + 1], 0.0))
                part = jnp.dot(lhs, blkt[k, h * half:(h + 1) * half, :], preferred_element_type=F32)
                acc = part if acc is None else acc + part
            total = total + (acc[:RB] + acc[RB:]) * m2

        pp_copy(s).wait_recv()
        total = total + jnp.where(iota16 == RB - 1, prevp[s], 0.0)

        by_core(lambda c: done(dz_rs.at[s], rz.at[s, 0:4 - c]))
        total = total + ((rz[s, 0] + rz[s, 1]) + (rz[s, 2] + rz[s, 3]))

        zb[s, core, 0] = total[:, half:]
        xa[s, core, x] = total[:, :half]
        by_core(lambda c: start([*xa_copies(s, c), *zb_copies(s, c)]))

        @pl.when(worker)
        def _():
            for h in (0, 1):
                done(tab_ss.at[h], tab.at[s, h, 0:4 * RB])
            done(cp_ss, cparts.at[s, 0:32])
            up_copy(s).wait_send()
            pp_copy(s).wait_send()

        @pl.when(hub)
        def _():
            @pl.when(jnp.logical_not(last))
            def _():
                add_share(s, dense[s, :, :half] * tab[s, 0] + dense[s, :, half:] * tab[s, 1])

            @pl.when(last)
            def _():
                done(sz_ss, stz.at[0:7])
                done(sz_rs, stz.at[0:7])
                v = stz[0]
                for p in range(1, 8):
                    v = v + stz[p]
                sty[y] = v
                for o in RING:
                    copy(sty.at[y], sty.at[y], sy_ss, sy_rs, y_peer(o, 1)).start()

            for h in (0, 1):
                done(tab_ss.at[h], tab.at[s, h, 0:3 * RB])
                done(sel_ss.at[h], selm.at[s, h, 0:56])
            done(cp_ss, cparts.at[s, 0:24])
            done(dz_ss, dense.at[s, 0:7 * RB])
            up_copy(s).wait_send()
            pp_copy(s).wait_send()

            done(xa_rs.at[s], dense.at[s, 0:56])
            za[s] = (xa[s, 0, 0] + xa[s, 0, 1]) + (xa[s, 0, 2] + xa[s, 0, 3])
            ta[s, 0] = (xa[s, 1, 0] + xa[s, 1, 1]) + (xa[s, 1, 2] + xa[s, 1, 3])
            start(za_copies(s))

            @pl.when(last)
            def _():
                done(sy_ss, sty.at[0:3])
                done(sy_rs, sty.at[0:3])
                stx[x] = (sty[0] + sty[1]) + (sty[2] + sty[3])
                start(sx_copies())

            done(zb_rs.at[s], dense.at[s, 0:24])
            xb[s] = zb[s, 0, 0] + zb[s, 0, 1]
            tb[s, x] = zb[s, 1, 0] + zb[s, 1, 1]
            start(xb_copies(s))

            done(za_ss, dense.at[s, 0:24])
            done(xb_ss, dense.at[s, 0:56])

        def rest(c):
            done(xa_ss, xa.at[s, 0, 0:4 - c])
            done(zb_ss, zb.at[s, 0, 0:2 - c])
            done(za_rs.at[s], ta.at[s, 0:2 - c])

        by_core(rest)
        n = s + 1
        tbuf[n, :, :half] = ta[s, 0] + ta[s, 1]
        pl.when(jnp.logical_not(last))(lambda: weights(n, 0))
        by_core(lambda c: done(xb_rs.at[s], tb.at[s, 0:4 - c]))
        tbuf[n, :, half:] = (tb[s, 0] + tb[s, 1]) + (tb[s, 2] + tb[s, 3])

        @pl.when(jnp.logical_not(last))
        def _():
            weights(n, 1)
            up_copy(n).start()

        return carry

    lax.fori_loop(0, SWEEPS, sweep, 0)

    def finish(c):
        done(sx_rs, stx.at[0:4 - c])
        done(ids_ss, ids.at[0:4 - c])
        if c == 0:
            done(ws_ss, stat)
        else:
            done(sx_ss, stz.at[0:7])

    by_core(finish)
    v = (stx[0] + stx[1]) + (stx[2] + stx[3])
    count = v[0:1, 0:1] * 0.125
    mean1 = v[1:2, 0:1] * 2.0 / count
    mean2 = v[2:3, 0:1] * 2.0 / count
    mean3 = v[3:4, 0:1] * 2.0 / count
    scale = mean1 * mean2 * 0.0625 * mean3
    b3 = tbuf[SWEEPS]
    bias = jnp.where(keep[...] > 0, b3 / scale, 1.0)
    balance = b3 * ubuf[SWEEPS - 1] / mean3
    for q in range(4):
        out_ref[pl.ds(q, RB, stride=4), :] = bias[:, q * 128:(q + 1) * 128]
        out_ref[pl.ds(4 * RB + q, RB, stride=4), :] = balance[:, q * 128:(q + 1) * 128]


def body(blocks, block_rows, block_cols, inter_counts, keep_mask):
    seg = keep_mask.shape[0]
    vm = pl.BlockSpec(memory_space=pltpu.VMEM)
    hbm = pl.BlockSpec(memory_space=pl.ANY)
    S = SWEEPS
    H = BS // 2
    dma = pltpu.SemaphoreType.DMA
    i32 = jnp.int32
    out = jax.ShapeDtypeStruct((seg // 64, 128), F32)

    def vf(*shape):
        return pltpu.VMEM(shape, F32)

    both = pl.pallas_call(
        kernel,
        out_shape=out,
        in_specs=[hbm] * 5,
        out_specs=vm,
        scratch_shapes=[
            pltpu.SMEM((SLOTS,), i32),
            pltpu.SMEM((SLOTS,), i32),
            pltpu.SMEM((1,), i32),
            pltpu.VMEM((seg // 128, 128), i32),
            pltpu.VMEM((SLOTS, BS, BS), BF16),
            pltpu.VMEM((IR_MAX, BS, BS), BF16),
            vf(RB, BS),
            vf(S + 1, RB, BS),
            vf(S, RB, BS),
            vf(RB + 8, BS),
            pltpu.VMEM((8, 8, 128), i32),
            pltpu.VMEM((128, SEL), BF16),
            pltpu.VMEM((SEL, 128), BF16),
            vf(8, 128),
            vf(RB, BS),
            vf(RB, BS),
            vf(S, 2, 128, H),
            vf(S, 2, SEL, H),
            vf(S, 2, 4, 8, H),
            vf(S, 1, BS),
            vf(S, 1, BS),
            vf(S, SEL, BS),
            vf(S, 1, BS),
            vf(S, 1, BS),
            vf(S, 128, BS),
            vf(S, 4, RB, BS),
            vf(S, 2, 4, RB, H),
            vf(S, RB, H),
            vf(S, 2, RB, H),
            vf(S, 2, 2, RB, H),
            vf(S, RB, H),
            vf(S, 4, RB, H),
            vf(8, 128),
            vf(8, 8, 128),
            vf(4, 8, 128),
            vf(4, 8, 128),
            dma((4,)),
            dma((2,)),
            dma, dma,
            dma((2,)), dma((S, 2)),
            dma((2,)), dma((S, 2)),
            dma, dma((S,)),
            dma, dma((S,)),
            dma, dma((S,)),
            dma, dma((S,)),
            dma, dma((S,)),
            dma, dma((S,)),
            dma, dma((S,)),
            dma, dma((S,)),
            dma, dma,
            dma, dma,
            dma, dma,
            dma, dma,
        ],
        compiler_params=pltpu.CompilerParams(
            collective_id=0, has_side_effects=True, vmem_limit_bytes=VMEM_LIMIT
        ),
        name="balance",
    )(block_rows, block_cols, inter_counts, keep_mask.reshape(seg // 128, 128), blocks)
    bias, balance = both[:seg // 128], both[seg // 128:]
    return bias.reshape(seg), balance.reshape(seg)


def solution(mesh):
    return jax.shard_map(
        body,
        mesh=mesh,
        in_specs=(
            P(("row", "col"), None, None),
            P(("row", "col")),
            P(("row", "col")),
            P(("row", "col")),
            P("row"),
        ),
        out_specs=(P("row"), P("row")),
        check_vma=False,
    )
```

```python
import jax
import jax.numpy as jnp
from jax import lax
from jax.experimental import pallas as pl
from jax.experimental.pallas import tpu as pltpu
from jax.sharding import PartitionSpec as P

IR_MAX = 8
SWEEPS = 3
RB = 16
BS = 512
SLOTS = 12
BAND = SLOTS - IR_MAX
SEL = 64
VMEM_LIMIT = 58 * 2**20

F32 = jnp.float32
BF16 = jnp.bfloat16
MESH = pl.DeviceIdType.MESH
RING = (2, 1, 3)


def split2(v):
    hi = v.astype(BF16)
    lo = (v - hi.astype(F32)).astype(BF16)
    return jnp.concatenate([hi, lo], axis=0)


def two_term_pick(pick, v):
    hi = v.astype(BF16)
    lo = (v - hi.astype(F32)).astype(BF16)
    return jnp.dot(pick, hi, preferred_element_type=F32) + jnp.dot(pick, lo, preferred_element_type=F32)


def full_max(v):
    m = jnp.max(jnp.max(v, axis=1, keepdims=True), axis=0, keepdims=True)
    return jnp.where(m > 0, m, 1.0)


def kernel(
    rows_hbm, cols_hbm, cnt_hbm, mask_hbm, blocks_ref,
    out_ref,
    rows_ref, cols_ref, cnt_ref, mask_ref,
    blk, blkt, keep, tbuf, ubuf, uloc, ids, pick, pickt, stat, rowband, colband,
    tab, selm, rsel, ulast, uprev, cparts, pprev, prevp, dense, rz,
    xa, za, ta, zb, xb, tb, wstat, stz, sty, stx,
    in_sem, blk_sem, ids_ss, ids_rs, tab_ss, tab_rs, sel_ss, sel_rs, up_ss, up_rs,
    cp_ss, cp_rs, pp_ss, pp_rs, dz_ss, dz_rs, xa_ss, xa_rs, za_ss, za_rs,
    zb_ss, zb_rs, xb_ss, xb_rs, ws_ss, ws_rs,
    sz_ss, sz_rs, sy_ss, sy_rs, sx_ss, sx_rs,
):
    row = lax.axis_index("row")
    col = lax.axis_index("col")
    zl = row // 8
    yc = lax.rem(row, 8)
    y = yc // 2
    core = lax.rem(row, 2)
    x = col // 2
    zh = lax.rem(col, 2)
    z = zh * 4 + zl
    half = BS // 2
    hub = core == 1
    worker = core == 0
    inner = jnp.where(zl < 2, 2, 6)
    two = (inner, 8 - inner)

    def chip(xx, yy, zz, cc):
        return (lax.rem(zz, 4) * 8 + yy * 2 + cc, xx * 2 + zz // 4)

    def z_peer(o, c):
        return chip(x, y, lax.rem(z + o, 8), c)

    def y_peer(o, c):
        return chip(x, lax.rem(y + o, 4), z, c)

    def x_peer(o, c):
        return chip(lax.rem(x + o, 4), y, z, c)

    def sibling(c):
        return chip(x, y, z, c)

    def step_peer(o):
        wrap = 7 if o == 1 else 0
        q = jnp.where(yc == wrap, lax.rem(z + o, 8), z)
        return (lax.rem(q, 4) * 8 + lax.rem(yc + o, 8), x * 2 + q // 4)

    def copy(src, dst, ss, rs, dev):
        return pltpu.make_async_remote_copy(
            src_ref=src, dst_ref=dst, send_sem=ss, recv_sem=rs,
            device_id=dev, device_id_type=MESH,
        )

    def seg(q, c):
        return pl.ds(pl.multiple_of(q * 2 * RB + c * RB, RB), RB)

    def eight(i):
        return pl.ds(pl.multiple_of(i * 8, 8), 8)

    own = seg(zl, core)
    mine = eight(yc)

    def turn(s):
        return s % 2 if isinstance(s, int) else lax.rem(s, 2)

    def tab_copies(s, h, c):
        out = [
            copy(tab.at[s, h, own], tab.at[s, h, own], tab_ss.at[h], tab_rs.at[turn(s), h], z_peer(o, 1))
            for i, o in enumerate((two[c], 1, 7))
        ]
        if c == 0:
            out.append(copy(tab.at[s, h, own], tab.at[s, h, own], tab_ss.at[h], tab_rs.at[turn(s), h], sibling(1)))
        return out

    def ids_copies(c):
        out = [copy(ids.at[yc], ids.at[yc], ids_ss, ids_rs, y_peer(o, 1)) for o in RING]
        if c == 0:
            out.append(copy(ids.at[yc], ids.at[yc], ids_ss, ids_rs, sibling(1)))
        return out

    def cp_copies(s, c):
        out = [
            copy(cparts.at[s, mine], cparts.at[s, mine], cp_ss, cp_rs.at[turn(s)], y_peer(o, 1))
            for o in RING
        ]
        if c == 0:
            out.append(copy(cparts.at[s, mine], cparts.at[s, mine], cp_ss, cp_rs.at[turn(s)], sibling(1)))
        return out

    def up_copy(s):
        return copy(ulast.at[s], uprev.at[s], up_ss, up_rs.at[turn(s)], step_peer(1))

    def pp_copy(s):
        return copy(pprev.at[s], prevp.at[s], pp_ss, pp_rs.at[turn(s)], step_peer(7))

    def sel_copies(s, h):
        out = [
            copy(selm.at[s, h, eight(lax.rem(y + o, 4) * 2 + c)], rsel.at[s, h, y],
                 sel_ss.at[h], sel_rs.at[turn(s), h], y_peer(o, c))
            for o in RING for c in (0, 1)
        ]
        return out + [
            copy(selm.at[s, h, eight(y * 2)], rsel.at[s, h, y], sel_ss.at[h], sel_rs.at[turn(s), h], sibling(0))
        ]

    def dz_copies(s):
        out = [
            copy(dense.at[s, seg(lax.rem(zl + o, 4), c)], rz.at[s, i],
                 dz_ss, dz_rs.at[turn(s)], z_peer(o, c))
            for c in (0, 1) for i, o in enumerate((two[c], 1, 7))
        ]
        return out + [copy(dense.at[s, seg(zl, 0)], rz.at[s, 3], dz_ss, dz_rs.at[turn(s)], sibling(0))]

    def xa_copies(s, c):
        out = [
            copy(xa.at[s, c, x], xa.at[s, c, x], xa_ss, xa_rs.at[turn(s)], x_peer(o, 1))
            for o in RING
        ]
        if c == 0:
            out.append(copy(xa.at[s, 0, x], xa.at[s, 0, x], xa_ss, xa_rs.at[turn(s)], sibling(1)))
        return out

    def za_copies(s):
        return [
            copy(za.at[s], ta.at[s, 1], za_ss, za_rs.at[turn(s)], z_peer(4, 0)),
            copy(ta.at[s, 0], ta.at[s, 1], za_ss, za_rs.at[turn(s)], z_peer(4, 1)),
            copy(za.at[s], ta.at[s, 0], za_ss, za_rs.at[turn(s)], sibling(0)),
        ]

    def zb_copies(s, c):
        out = [copy(zb.at[s, c, 0], zb.at[s, c, 1], zb_ss, zb_rs.at[turn(s)], z_peer(4, 1))]
        if c == 0:
            out.append(copy(zb.at[s, 0, 0], zb.at[s, 0, 0], zb_ss, zb_rs.at[turn(s)], sibling(1)))
        return out

    def xb_copies(s):
        out = []
        for o in RING:
            out.append(copy(xb.at[s], tb.at[s, x], xb_ss, xb_rs.at[turn(s)], x_peer(o, 0)))
            out.append(copy(tb.at[s, x], tb.at[s, x], xb_ss, xb_rs.at[turn(s)], x_peer(o, 1)))
        return out + [copy(xb.at[s], tb.at[s, x], xb_ss, xb_rs.at[turn(s)], sibling(0))]

    def sx_copies():
        out = [
            copy(stx.at[x], stx.at[x], sx_ss, sx_rs, x_peer(o, c))
            for o in RING for c in (0, 1)
        ]
        return out + [copy(stx.at[x], stx.at[x], sx_ss, sx_rs, sibling(0))]

    def start(copies):
        for c in copies:
            c.start()

    def done(sem, like):
        pltpu.make_async_copy(like, like, sem).wait()

    def by_core(f):
        pl.when(worker)(lambda: f(0))
        pl.when(hub)(lambda: f(1))

    loads = [
        pltpu.make_async_copy(src, dst, in_sem.at[i])
        for i, (src, dst) in enumerate((
            (rows_hbm, rows_ref), (cols_hbm, cols_ref), (cnt_hbm, cnt_ref), (mask_hbm, mask_ref),
        ))
    ] + [
        pltpu.make_async_copy(blocks_ref.at[k], blk.at[k], blk_sem.at[1 if k < BAND else 0])
        for k in (*range(BAND, SLOTS), *range(BAND))
    ]
    loads[3].start()

    barrier = pltpu.get_barrier_semaphore()

    def greet(c):
        if c == 0:
            peers = (
                [z_peer(o, 1) for o in (2, 6, 1, 7)] + [y_peer(o, 1) for o in RING]
                + [x_peer(o, 1) for o in RING] + [sibling(1), step_peer(7)]
            )
        else:
            peers = (
                [z_peer(o, d) for o in (2, 6, 1, 7) for d in (0, 1)]
                + [y_peer(o, d) for o in RING for d in (0, 1)]
                + [x_peer(o, d) for o in RING for d in (0, 1)]
                + [sibling(0), step_peer(1)]
            )
        return peers

    def signal_peers(c):
        for dev in greet(c):
            pl.semaphore_signal(barrier, inc=1, device_id=dev, device_id_type=MESH)

    by_core(signal_peers)
    start([*loads[:3], *loads[4:]])
    for c in loads[:4]:
        c.wait()

    live = cnt_ref[0]
    row_l = [lax.rem(rows_ref[k], RB) for k in range(SLOTS)]
    col_l = [cols_ref[k] - row * RB for k in range(BAND)]
    here = [(c >= 0) & (c < RB) for c in col_l]
    lane = lax.broadcasted_iota(jnp.int32, (8, 128), 1)
    iota8 = lax.broadcasted_iota(jnp.int32, (8, BS), 0)
    iota16 = lax.broadcasted_iota(jnp.int32, (RB, BS), 0)
    iota24 = lax.broadcasted_iota(jnp.int32, (RB + 8, BS), 0)

    idv = jnp.zeros((8, 128), jnp.int32)
    for k in range(IR_MAX):
        code = jnp.where(k < live, cols_ref[BAND + k] + 1, 0)
        idv = jnp.where(lane == yc * 8 + k, code, idv)
    ids[yc] = idv
    for q in range(4):
        keep[:, q * 128:(q + 1) * 128] = mask_ref[pl.ds(q, RB, stride=4), :].astype(F32)
    tbuf[0] = jnp.full((RB, BS), 4.0, F32)
    uloc[...] = jnp.zeros_like(uloc)

    def total_of(v):
        return jnp.sum(jnp.sum(v, axis=1, keepdims=True), axis=0, keepdims=True)

    sub = lax.broadcasted_iota(jnp.int32, (8, 128), 0)
    stat[...] = jnp.where(sub == 0, total_of(keep[...]), 0.0)

    def add_share(s, v):
        stat[...] += jnp.where(sub == s + 1, total_of(v), 0.0)

    def weights(s, h, send=True):
        lanes = slice(h * half, (h + 1) * half)
        u = jnp.where(keep[:, lanes] > 0, 4.0 / tbuf[s, :, lanes], 0.0)
        tab[s, h, own] = u
        if send:
            by_core(lambda c: start(tab_copies(s, h, c)))
        ubuf[s, :, lanes] = u
        uloc[0:RB, lanes] = u
        ulast[s, :, lanes] = u[RB - 1:]

    def inter_columns(s):
        m = full_max(uloc[0:RB])
        inv = 1.0 / m
        acc = None
        for k in range(IR_MAX):
            vec = uloc[pl.ds(row_l[BAND + k], 1), :] * inv
            target = jnp.where(k < live, k, -1)
            lhs = split2(jnp.where(iota8 == target, vec, 0.0))
            part = jnp.dot(lhs, blk[BAND + k], preferred_element_type=F32)
            acc = part if acc is None else acc + part
        cparts[s, mine] = (acc[:8] + acc[8:]) * m

    def band_columns(s):
        m = full_max(uloc[0:RB])
        inv = 1.0 / m
        acc = None
        for k in range(BAND):
            vec = uloc[pl.ds(row_l[k], 1), :] * inv
            target = jnp.where(here[k], col_l[k], RB)
            lhs = split2(jnp.where(iota24 == target, vec, 0.0))
            part = jnp.dot(lhs, blk[k], preferred_element_type=F32)
            acc = part if acc is None else acc + part
        acc = (acc[:RB + 8] + acc[RB + 8:]) * m
        colband[...] = acc[:RB]
        pprev[s] = acc[RB:RB + 1]

    def transpose_inter():
        def one(k, carry):
            blkt[k] = blk[BAND + k].T
            return carry

        lax.fori_loop(0, IR_MAX, one, 0)

    weights(0, 0, send=False)
    weights(0, 1, send=False)

    def open_up(c):
        pl.semaphore_wait(barrier, len(greet(c)))
        start([*tab_copies(0, 0, c), *tab_copies(0, 1, c), up_copy(0), *ids_copies(c)])

    by_core(open_up)

    def sweep(s, carry):
        first = s == 0
        last = s == SWEEPS - 1

        @pl.when(first)
        def _():
            done(blk_sem.at[0], blk.at[BAND:])

        inter_columns(s)
        by_core(lambda c: start(cp_copies(s, c)))

        @pl.when(first)
        def _():
            done(blk_sem.at[1], blk.at[:BAND])

        band_columns(s)
        pp_copy(s).start()
        pl.when(first)(transpose_inter)

        up_copy(s).wait_recv()
        uloc[RB:RB + 1] = uprev[s]
        add_share(s, uloc[0:RB] * colband[...])
        add_share(s, uprev[s] * pprev[s])

        @pl.when(worker & last)
        def _():
            copy(stat, wstat, ws_ss, ws_rs, sibling(1)).start()

        @pl.when(hub)
        def _():
            @pl.when(first)
            def _():
                done(ids_rs, ids.at[0:7])
                code = ids[0]
                for p in range(1, 8):
                    code = code + ids[p]
                code = code[0:1]
                cc = jnp.maximum(code - 1, 0)
                want = jnp.where(
                    (code > 0) & (((cc // 32) % 4) == y), (cc // 128) * 32 + cc % 32, -1
                )
                full = jnp.where(
                    lax.broadcasted_iota(jnp.int32, (128, 128), 0) == want, 1.0, 0.0
                )
                pick[...] = full[:, :SEL].astype(BF16)
                pickt[...] = full.T[:SEL].astype(BF16)

            for h in (0, 1):
                done(tab_rs.at[turn(s), h], tab.at[s, h, 0:7 * RB])
                selm[s, h] = two_term_pick(pickt[...], tab[s, h])
                start(sel_copies(s, h))
                rsel[s, h, y] = selm[s, h, mine]

            done(cp_rs.at[turn(s)], cparts.at[s, 0:56])
            dense[s] = two_term_pick(pick[...], cparts[s])
            start(dz_copies(s))
            rz[s, 3] = dense[s, own]

            @pl.when(last)
            def _():
                done(ws_rs, wstat)
                add_share(s, dense[s, :, :half] * tab[s, 0] + dense[s, :, half:] * tab[s, 1])
                stz[z] = stat[...] + wstat[...]
                for o in range(1, 8):
                    copy(stz.at[z], stz.at[z], sz_ss, sz_rs, z_peer(o, 1)).start()

        m = full_max(uloc[...])
        inv = 1.0 / m
        acc = None
        for k in range(BAND):
            vec = uloc[pl.ds(jnp.where(here[k], col_l[k], RB), 1), :] * inv
            lhs = split2(jnp.where(iota16 == row_l[k], vec, 0.0))
            part = lax.dot_general(
                lhs, blk[k], (((1,), (1,)), ((), ())), preferred_element_type=F32
            )
            acc = part if acc is None else acc + part
        rowband[...] = (acc[:RB] + acc[RB:]) * m

        total = rowband[...] + colband[...]
        for h in (0, 1):
            by_core(lambda c, h=h: done(sel_rs.at[turn(s), h], rsel.at[s, h, 0:4 - c]))
            ucol = (rsel[s, h, 0] + rsel[s, h, 1]) + (rsel[s, h, 2] + rsel[s, h, 3])
            m2 = full_max(ucol)
            ucol = ucol * (1.0 / m2)
            acc = None
            for k in range(IR_MAX):
                target = jnp.where(k < live, row_l[BAND + k], -1)
                lhs = split2(jnp.where(iota16[:, :half] == target, ucol[k:k + 1], 0.0))
                part = jnp.dot(lhs, blkt[k, h * half:(h + 1) * half, :], preferred_element_type=F32)
                acc = part if acc is None else acc + part
            total = total + (acc[:RB] + acc[RB:]) * m2

        pp_copy(s).wait_recv()
        total = total + jnp.where(iota16 == RB - 1, prevp[s], 0.0)

        by_core(lambda c: done(dz_rs.at[turn(s)], rz.at[s, 0:4 - c]))
        total = total + ((rz[s, 0] + rz[s, 1]) + (rz[s, 2] + rz[s, 3]))

        zb[s, core, 0] = total[:, half:]
        xa[s, core, x] = total[:, :half]
        by_core(lambda c: start([*xa_copies(s, c), *zb_copies(s, c)]))

        @pl.when(worker)
        def _():
            for h in (0, 1):
                done(tab_ss.at[h], tab.at[s, h, 0:4 * RB])
            done(cp_ss, cparts.at[s, 0:32])
            up_copy(s).wait_send()
            pp_copy(s).wait_send()

        @pl.when(hub)
        def _():
            @pl.when(jnp.logical_not(last))
            def _():
                add_share(s, dense[s, :, :half] * tab[s, 0] + dense[s, :, half:] * tab[s, 1])

            @pl.when(last)
            def _():
                done(sz_ss, stz.at[0:7])
                done(sz_rs, stz.at[0:7])
                v = stz[0]
                for p in range(1, 8):
                    v = v + stz[p]
                sty[y] = v
                for o in RING:
                    copy(sty.at[y], sty.at[y], sy_ss, sy_rs, y_peer(o, 1)).start()

            for h in (0, 1):
                done(tab_ss.at[h], tab.at[s, h, 0:3 * RB])
                done(sel_ss.at[h], selm.at[s, h, 0:56])
            done(cp_ss, cparts.at[s, 0:24])
            done(dz_ss, dense.at[s, 0:7 * RB])
            up_copy(s).wait_send()
            pp_copy(s).wait_send()

            done(xa_rs.at[turn(s)], dense.at[s, 0:56])
            za[s] = (xa[s, 0, 0] + xa[s, 0, 1]) + (xa[s, 0, 2] + xa[s, 0, 3])
            ta[s, 0] = (xa[s, 1, 0] + xa[s, 1, 1]) + (xa[s, 1, 2] + xa[s, 1, 3])
            start(za_copies(s))

            @pl.when(last)
            def _():
                done(sy_ss, sty.at[0:3])
                done(sy_rs, sty.at[0:3])
                stx[x] = (sty[0] + sty[1]) + (sty[2] + sty[3])
                start(sx_copies())

            done(zb_rs.at[turn(s)], dense.at[s, 0:24])
            xb[s] = zb[s, 0, 0] + zb[s, 0, 1]
            tb[s, x] = zb[s, 1, 0] + zb[s, 1, 1]
            start(xb_copies(s))

            done(za_ss, dense.at[s, 0:24])
            done(xb_ss, dense.at[s, 0:56])

        def rest(c):
            done(xa_ss, xa.at[s, 0, 0:4 - c])
            done(zb_ss, zb.at[s, 0, 0:2 - c])
            done(za_rs.at[turn(s)], ta.at[s, 0:2 - c])

        by_core(rest)
        n = s + 1
        tbuf[n, :, :half] = ta[s, 0] + ta[s, 1]
        pl.when(jnp.logical_not(last))(lambda: weights(n, 0))
        by_core(lambda c: done(xb_rs.at[turn(s)], tb.at[s, 0:4 - c]))
        tbuf[n, :, half:] = (tb[s, 0] + tb[s, 1]) + (tb[s, 2] + tb[s, 3])

        @pl.when(jnp.logical_not(last))
        def _():
            weights(n, 1)
            up_copy(n).start()

        return carry

    lax.fori_loop(0, SWEEPS, sweep, 0)

    def finish(c):
        done(sx_rs, stx.at[0:4 - c])
        done(ids_ss, ids.at[0:4 - c])
        if c == 0:
            done(ws_ss, stat)
        else:
            done(sx_ss, stz.at[0:7])

    by_core(finish)
    v = (stx[0] + stx[1]) + (stx[2] + stx[3])
    count = v[0:1, 0:1] * 0.125
    mean1 = v[1:2, 0:1] * 2.0 / count
    mean2 = v[2:3, 0:1] * 2.0 / count
    mean3 = v[3:4, 0:1] * 2.0 / count
    scale = mean1 * mean2 * 0.0625 * mean3
    b3 = tbuf[SWEEPS]
    bias = jnp.where(keep[...] > 0, b3 * (1.0 / scale), 1.0)
    balance = b3 * ubuf[SWEEPS - 1] * (1.0 / mean3)
    for q in range(4):
        out_ref[pl.ds(q, RB, stride=4), :] = bias[:, q * 128:(q + 1) * 128]
        out_ref[pl.ds(4 * RB + q, RB, stride=4), :] = balance[:, q * 128:(q + 1) * 128]


def body(blocks, block_rows, block_cols, inter_counts, keep_mask):
    seg = keep_mask.shape[0]
    vm = pl.BlockSpec(memory_space=pltpu.VMEM)
    hbm = pl.BlockSpec(memory_space=pl.ANY)
    S = SWEEPS
    H = BS // 2
    dma = pltpu.SemaphoreType.DMA
    i32 = jnp.int32
    out = jax.ShapeDtypeStruct((seg // 64, 128), F32)

    def vf(*shape):
        return pltpu.VMEM(shape, F32)

    both = pl.pallas_call(
        kernel,
        out_shape=out,
        in_specs=[hbm] * 5,
        out_specs=vm,
        scratch_shapes=[
            pltpu.SMEM((SLOTS,), i32),
            pltpu.SMEM((SLOTS,), i32),
            pltpu.SMEM((1,), i32),
            pltpu.VMEM((seg // 128, 128), i32),
            pltpu.VMEM((SLOTS, BS, BS), BF16),
            pltpu.VMEM((IR_MAX, BS, BS), BF16),
            vf(RB, BS),
            vf(S + 1, RB, BS),
            vf(S, RB, BS),
            vf(RB + 8, BS),
            pltpu.VMEM((8, 8, 128), i32),
            pltpu.VMEM((128, SEL), BF16),
            pltpu.VMEM((SEL, 128), BF16),
            vf(8, 128),
            vf(RB, BS),
            vf(RB, BS),
            vf(S, 2, 128, H),
            vf(S, 2, SEL, H),
            vf(S, 2, 4, 8, H),
            vf(S, 1, BS),
            vf(S, 1, BS),
            vf(S, SEL, BS),
            vf(S, 1, BS),
            vf(S, 1, BS),
            vf(S, 128, BS),
            vf(S, 4, RB, BS),
            vf(S, 2, 4, RB, H),
            vf(S, RB, H),
            vf(S, 2, RB, H),
            vf(S, 2, 2, RB, H),
            vf(S, RB, H),
            vf(S, 4, RB, H),
            vf(8, 128),
            vf(8, 8, 128),
            vf(4, 8, 128),
            vf(4, 8, 128),
            dma((4,)),
            dma((2,)),
            dma, dma,
            dma((2,)), dma((2, 2)),
            dma((2,)), dma((2, 2)),
            dma, dma((2,)),
            dma, dma((2,)),
            dma, dma((2,)),
            dma, dma((2,)),
            dma, dma((2,)),
            dma, dma((2,)),
            dma, dma((2,)),
            dma, dma((2,)),
            dma, dma,
            dma, dma,
            dma, dma,
            dma, dma,
        ],
        compiler_params=pltpu.CompilerParams(
            collective_id=0, has_side_effects=True, vmem_limit_bytes=VMEM_LIMIT
        ),
        name="balance",
    )(block_rows, block_cols, inter_counts, keep_mask.reshape(seg // 128, 128), blocks)
    bias, balance = both[:seg // 128], both[seg // 128:]
    return bias.reshape(seg), balance.reshape(seg)


def solution(mesh):
    return jax.shard_map(
        body,
        mesh=mesh,
        in_specs=(
            P(("row", "col"), None, None),
            P(("row", "col")),
            P(("row", "col")),
            P(("row", "col")),
            P("row"),
        ),
        out_specs=(P("row"), P("row")),
        check_vma=False,
    )
```

```python
import jax
import jax.numpy as jnp
from jax import lax
from jax.experimental import pallas as pl
from jax.experimental.pallas import tpu as pltpu
from jax.sharding import PartitionSpec as P

IR_MAX = 8
SWEEPS = 3
RB = 16
BS = 512
SLOTS = 12
BAND = SLOTS - IR_MAX
SEL = 64
VMEM_LIMIT = 58 * 2**20

F32 = jnp.float32
BF16 = jnp.bfloat16
MESH = pl.DeviceIdType.MESH
RING = (2, 1, 3)


def split2(v):
    hi = v.astype(BF16)
    lo = (v - hi.astype(F32)).astype(BF16)
    return jnp.concatenate([hi, lo], axis=0)


def two_term_pick(pick, v):
    hi = v.astype(BF16)
    lo = (v - hi.astype(F32)).astype(BF16)
    return jnp.dot(pick, hi, preferred_element_type=F32) + jnp.dot(pick, lo, preferred_element_type=F32)


def full_max(v):
    m = jnp.max(jnp.max(v, axis=1, keepdims=True), axis=0, keepdims=True)
    return jnp.where(m > 0, m, 1.0)


def kernel(
    rows_hbm, cols_hbm, cnt_hbm, mask_hbm, blocks_ref,
    out_ref,
    rows_ref, cols_ref, cnt_ref, mask_ref,
    blk, blkt, keep, tbuf, ubuf, uloc, ids, pick, pickt, stat, rowband, colband,
    tab, selm, rsel, ulast, uprev, cparts, pprev, prevp, dense, rz,
    xa, za, ta, zb, xb, tb, wstat, stz, sty, stx,
    in_sem, blk_sem, ids_ss, ids_rs, tab_ss, tab_rs, sel_ss, sel_rs, up_ss, up_rs,
    cp_ss, cp_rs, pp_ss, pp_rs, dz_ss, dz_rs, xa_ss, xa_rs, za_ss, za_rs,
    zb_ss, zb_rs, xb_ss, xb_rs, ws_ss, ws_rs,
    sz_ss, sz_rs, sy_ss, sy_rs, sx_ss, sx_rs,
):
    row = lax.axis_index("row")
    col = lax.axis_index("col")
    zl = row // 8
    yc = lax.rem(row, 8)
    y = yc // 2
    core = lax.rem(row, 2)
    x = col // 2
    zh = lax.rem(col, 2)
    z = zh * 4 + zl
    half = BS // 2
    hub = core == 1
    worker = core == 0
    inner = jnp.where(zl < 2, 2, 6)
    two = (inner, 8 - inner)

    def chip(xx, yy, zz, cc):
        return (lax.rem(zz, 4) * 8 + yy * 2 + cc, xx * 2 + zz // 4)

    def z_peer(o, c):
        return chip(x, y, lax.rem(z + o, 8), c)

    def y_peer(o, c):
        return chip(x, lax.rem(y + o, 4), z, c)

    def x_peer(o, c):
        return chip(lax.rem(x + o, 4), y, z, c)

    def sibling(c):
        return chip(x, y, z, c)

    def step_peer(o):
        wrap = 7 if o == 1 else 0
        q = jnp.where(yc == wrap, lax.rem(z + o, 8), z)
        return (lax.rem(q, 4) * 8 + lax.rem(yc + o, 8), x * 2 + q // 4)

    def copy(src, dst, ss, rs, dev):
        return pltpu.make_async_remote_copy(
            src_ref=src, dst_ref=dst, send_sem=ss, recv_sem=rs,
            device_id=dev, device_id_type=MESH,
        )

    def seg(q, c):
        return pl.ds(pl.multiple_of(q * 2 * RB + c * RB, RB), RB)

    def eight(i):
        return pl.ds(pl.multiple_of(i * 8, 8), 8)

    own = seg(zl, core)
    mine = eight(yc)

    def turn(s):
        return s % 2 if isinstance(s, int) else lax.rem(s, 2)

    def tab_copies(s, h, c):
        out = [
            copy(tab.at[s, h, own], tab.at[s, h, own], tab_ss.at[h], tab_rs.at[turn(s), h], z_peer(o, 1))
            for i, o in enumerate((two[c], 1, 7))
        ]
        if c == 0:
            out.append(copy(tab.at[s, h, own], tab.at[s, h, own], tab_ss.at[h], tab_rs.at[turn(s), h], sibling(1)))
        return out

    def ids_copies(c):
        out = [copy(ids.at[yc], ids.at[yc], ids_ss, ids_rs, y_peer(o, 1)) for o in RING]
        if c == 0:
            out.append(copy(ids.at[yc], ids.at[yc], ids_ss, ids_rs, sibling(1)))
        return out

    def cp_copies(s, c):
        out = [
            copy(cparts.at[s, mine], cparts.at[s, mine], cp_ss, cp_rs.at[turn(s)], y_peer(o, 1))
            for o in RING
        ]
        if c == 0:
            out.append(copy(cparts.at[s, mine], cparts.at[s, mine], cp_ss, cp_rs.at[turn(s)], sibling(1)))
        return out

    def up_copy(s):
        return copy(ulast.at[s], uprev.at[s], up_ss, up_rs.at[turn(s)], step_peer(1))

    def pp_copy(s):
        return copy(pprev.at[s], prevp.at[s], pp_ss, pp_rs.at[turn(s)], step_peer(7))

    def sel_copies(s, h):
        out = [
            copy(selm.at[s, h, eight(lax.rem(y + o, 4) * 2 + c)], rsel.at[s, h, y],
                 sel_ss.at[h], sel_rs.at[turn(s), h], y_peer(o, c))
            for o in RING for c in (0, 1)
        ]
        return out + [
            copy(selm.at[s, h, eight(y * 2)], rsel.at[s, h, y], sel_ss.at[h], sel_rs.at[turn(s), h], sibling(0))
        ]

    def dz_copies(s):
        out = [
            copy(dense.at[s, seg(lax.rem(zl + o, 4), c)], rz.at[s, i],
                 dz_ss, dz_rs.at[turn(s)], z_peer(o, c))
            for i, offsets in enumerate((two, (1, 1), (7, 7))) for c, o in enumerate(offsets)
        ]
        return out + [copy(dense.at[s, seg(zl, 0)], rz.at[s, 3], dz_ss, dz_rs.at[turn(s)], sibling(0))]

    def xa_copies(s, c):
        out = [
            copy(xa.at[s, c, x], xa.at[s, c, x], xa_ss, xa_rs.at[turn(s)], x_peer(o, 1))
            for o in RING
        ]
        if c == 0:
            out.append(copy(xa.at[s, 0, x], xa.at[s, 0, x], xa_ss, xa_rs.at[turn(s)], sibling(1)))
        return out

    def za_copies(s):
        return [
            copy(za.at[s], ta.at[s, 1], za_ss, za_rs.at[turn(s)], z_peer(4, 0)),
            copy(ta.at[s, 0], ta.at[s, 1], za_ss, za_rs.at[turn(s)], z_peer(4, 1)),
            copy(za.at[s], ta.at[s, 0], za_ss, za_rs.at[turn(s)], sibling(0)),
        ]

    def zb_copies(s, c):
        out = [copy(zb.at[s, c, 0], zb.at[s, c, 1], zb_ss, zb_rs.at[turn(s)], z_peer(4, 1))]
        if c == 0:
            out.append(copy(zb.at[s, 0, 0], zb.at[s, 0, 0], zb_ss, zb_rs.at[turn(s)], sibling(1)))
        return out

    def xb_copies(s):
        out = []
        for o in RING:
            out.append(copy(xb.at[s], tb.at[s, x], xb_ss, xb_rs.at[turn(s)], x_peer(o, 0)))
            out.append(copy(tb.at[s, x], tb.at[s, x], xb_ss, xb_rs.at[turn(s)], x_peer(o, 1)))
        return out + [copy(xb.at[s], tb.at[s, x], xb_ss, xb_rs.at[turn(s)], sibling(0))]

    def sx_copies():
        out = [
            copy(stx.at[x], stx.at[x], sx_ss, sx_rs, x_peer(o, c))
            for o in RING for c in (0, 1)
        ]
        return out + [copy(stx.at[x], stx.at[x], sx_ss, sx_rs, sibling(0))]

    def start(copies):
        for c in copies:
            c.start()

    def done(sem, like):
        pltpu.make_async_copy(like, like, sem).wait()

    def by_core(f):
        pl.when(worker)(lambda: f(0))
        pl.when(hub)(lambda: f(1))

    loads = [
        pltpu.make_async_copy(src, dst, in_sem.at[i])
        for i, (src, dst) in enumerate((
            (rows_hbm, rows_ref), (cols_hbm, cols_ref), (cnt_hbm, cnt_ref), (mask_hbm, mask_ref),
        ))
    ] + [
        pltpu.make_async_copy(blocks_ref.at[k], blk.at[k], blk_sem.at[1 if k < BAND else 0])
        for k in (*range(BAND, SLOTS), *range(BAND))
    ]
    loads[3].start()

    barrier = pltpu.get_barrier_semaphore()

    def greet(c):
        if c == 0:
            peers = (
                [z_peer(o, 1) for o in (2, 6, 1, 7)] + [y_peer(o, 1) for o in RING]
                + [x_peer(o, 1) for o in RING] + [sibling(1), step_peer(7)]
            )
        else:
            peers = (
                [z_peer(o, d) for o in (2, 6, 1, 7) for d in (0, 1)]
                + [y_peer(o, d) for o in RING for d in (0, 1)]
                + [x_peer(o, d) for o in RING for d in (0, 1)]
                + [sibling(0), step_peer(1)]
            )
        return peers

    def signal_peers(c):
        for dev in greet(c):
            pl.semaphore_signal(barrier, inc=1, device_id=dev, device_id_type=MESH)

    by_core(signal_peers)
    start([*loads[:3], *loads[4:]])
    for c in loads[:4]:
        c.wait()

    live = cnt_ref[0]
    row_l = [lax.rem(rows_ref[k], RB) for k in range(SLOTS)]
    col_l = [cols_ref[k] - row * RB for k in range(BAND)]
    here = [(c >= 0) & (c < RB) for c in col_l]
    lane = lax.broadcasted_iota(jnp.int32, (8, 128), 1)
    iota8 = lax.broadcasted_iota(jnp.int32, (8, BS), 0)
    iota16 = lax.broadcasted_iota(jnp.int32, (RB, BS), 0)
    iota24 = lax.broadcasted_iota(jnp.int32, (RB + 8, BS), 0)

    idv = jnp.zeros((8, 128), jnp.int32)
    for k in range(IR_MAX):
        code = jnp.where(k < live, cols_ref[BAND + k] + 1, 0)
        idv = jnp.where(lane == yc * 8 + k, code, idv)
    ids[yc] = idv
    for q in range(4):
        keep[:, q * 128:(q + 1) * 128] = mask_ref[pl.ds(q, RB, stride=4), :].astype(F32)
    tbuf[0] = jnp.full((RB, BS), 4.0, F32)
    uloc[...] = jnp.zeros_like(uloc)

    def total_of(v):
        return jnp.sum(jnp.sum(v, axis=1, keepdims=True), axis=0, keepdims=True)

    sub = lax.broadcasted_iota(jnp.int32, (8, 128), 0)
    stat[...] = jnp.where(sub == 0, total_of(keep[...]), 0.0)

    def add_share(s, v):
        stat[...] += jnp.where(sub == s + 1, total_of(v), 0.0)

    def weights(s, h, send=True):
        lanes = slice(h * half, (h + 1) * half)
        u = jnp.where(keep[:, lanes] > 0, 4.0 / tbuf[s, :, lanes], 0.0)
        tab[s, h, own] = u
        if send:
            by_core(lambda c: start(tab_copies(s, h, c)))
        ubuf[s, :, lanes] = u
        uloc[0:RB, lanes] = u
        ulast[s, :, lanes] = u[RB - 1:]

    def inter_columns(s):
        m = full_max(uloc[0:RB])
        inv = 1.0 / m
        acc = None
        for k in range(IR_MAX):
            vec = uloc[pl.ds(row_l[BAND + k], 1), :] * inv
            target = jnp.where(k < live, k, -1)
            lhs = split2(jnp.where(iota8 == target, vec, 0.0))
            part = jnp.dot(lhs, blk[BAND + k], preferred_element_type=F32)
            acc = part if acc is None else acc + part
        cparts[s, mine] = (acc[:8] + acc[8:]) * m

    def band_columns(s):
        m = full_max(uloc[0:RB])
        inv = 1.0 / m
        acc = None
        for k in range(BAND):
            vec = uloc[pl.ds(row_l[k], 1), :] * inv
            target = jnp.where(here[k], col_l[k], RB)
            lhs = split2(jnp.where(iota24 == target, vec, 0.0))
            part = jnp.dot(lhs, blk[k], preferred_element_type=F32)
            acc = part if acc is None else acc + part
        acc = (acc[:RB + 8] + acc[RB + 8:]) * m
        colband[...] = acc[:RB]
        pprev[s] = acc[RB:RB + 1]

    def transpose_inter():
        def one(k, carry):
            blkt[k] = blk[BAND + k].T
            return carry

        lax.fori_loop(0, IR_MAX, one, 0)

    weights(0, 0, send=False)
    weights(0, 1, send=False)

    def open_up(c):
        pl.semaphore_wait(barrier, len(greet(c)))
        start([*tab_copies(0, 0, c), *tab_copies(0, 1, c), up_copy(0), *ids_copies(c)])

    by_core(open_up)

    def sweep(s, carry):
        first = s == 0
        last = s == SWEEPS - 1

        @pl.when(first)
        def _():
            done(blk_sem.at[0], blk.at[BAND:])

        inter_columns(s)
        by_core(lambda c: start(cp_copies(s, c)))

        @pl.when(first)
        def _():
            done(blk_sem.at[1], blk.at[:BAND])

        band_columns(s)
        pp_copy(s).start()
        pl.when(first)(transpose_inter)

        up_copy(s).wait_recv()
        uloc[RB:RB + 1] = uprev[s]
        add_share(s, uloc[0:RB] * colband[...])
        add_share(s, uprev[s] * pprev[s])

        @pl.when(worker & last)
        def _():
            copy(stat, wstat, ws_ss, ws_rs, sibling(1)).start()

        @pl.when(hub)
        def _():
            @pl.when(first)
            def _():
                done(ids_rs, ids.at[0:7])
                code = ids[0]
                for p in range(1, 8):
                    code = code + ids[p]
                code = code[0:1]
                cc = jnp.maximum(code - 1, 0)
                want = jnp.where(
                    (code > 0) & (((cc // 32) % 4) == y), (cc // 128) * 32 + cc % 32, -1
                )
                full = jnp.where(
                    lax.broadcasted_iota(jnp.int32, (128, 128), 0) == want, 1.0, 0.0
                )
                pick[...] = full[:, :SEL].astype(BF16)
                pickt[...] = full.T[:SEL].astype(BF16)

            for h in (0, 1):
                done(tab_rs.at[turn(s), h], tab.at[s, h, 0:7 * RB])
                selm[s, h] = two_term_pick(pickt[...], tab[s, h])
                start(sel_copies(s, h))
                rsel[s, h, y] = selm[s, h, mine]

            done(cp_rs.at[turn(s)], cparts.at[s, 0:56])
            dense[s] = two_term_pick(pick[...], cparts[s])
            start(dz_copies(s))
            rz[s, 3] = dense[s, own]

            @pl.when(last)
            def _():
                done(ws_rs, wstat)
                add_share(s, dense[s, :, :half] * tab[s, 0] + dense[s, :, half:] * tab[s, 1])
                stz[z] = stat[...] + wstat[...]
                for o in range(1, 8):
                    copy(stz.at[z], stz.at[z], sz_ss, sz_rs, z_peer(o, 1)).start()

        m = full_max(uloc[...])
        inv = 1.0 / m
        acc = None
        for k in range(BAND):
            vec = uloc[pl.ds(jnp.where(here[k], col_l[k], RB), 1), :] * inv
            lhs = split2(jnp.where(iota16 == row_l[k], vec, 0.0))
            part = lax.dot_general(
                lhs, blk[k], (((1,), (1,)), ((), ())), preferred_element_type=F32
            )
            acc = part if acc is None else acc + part
        rowband[...] = (acc[:RB] + acc[RB:]) * m

        total = rowband[...] + colband[...]
        for h in (0, 1):
            by_core(lambda c, h=h: done(sel_rs.at[turn(s), h], rsel.at[s, h, 0:4 - c]))
            ucol = (rsel[s, h, 0] + rsel[s, h, 1]) + (rsel[s, h, 2] + rsel[s, h, 3])
            m2 = full_max(ucol)
            ucol = ucol * (1.0 / m2)
            acc = None
            for k in range(IR_MAX):
                target = jnp.where(k < live, row_l[BAND + k], -1)
                lhs = split2(jnp.where(iota16[:, :half] == target, ucol[k:k + 1], 0.0))
                part = jnp.dot(lhs, blkt[k, h * half:(h + 1) * half, :], preferred_element_type=F32)
                acc = part if acc is None else acc + part
            total = total + (acc[:RB] + acc[RB:]) * m2

        pp_copy(s).wait_recv()
        total = total + jnp.where(iota16 == RB - 1, prevp[s], 0.0)

        by_core(lambda c: done(dz_rs.at[turn(s)], rz.at[s, 0:4 - c]))
        total = total + ((rz[s, 0] + rz[s, 1]) + (rz[s, 2] + rz[s, 3]))

        zb[s, core, 0] = total[:, half:]
        xa[s, core, x] = total[:, :half]
        by_core(lambda c: start([*xa_copies(s, c), *zb_copies(s, c)]))

        @pl.when(worker)
        def _():
            for h in (0, 1):
                done(tab_ss.at[h], tab.at[s, h, 0:4 * RB])
            done(cp_ss, cparts.at[s, 0:32])
            up_copy(s).wait_send()
            pp_copy(s).wait_send()

        @pl.when(hub)
        def _():
            @pl.when(jnp.logical_not(last))
            def _():
                add_share(s, dense[s, :, :half] * tab[s, 0] + dense[s, :, half:] * tab[s, 1])

            @pl.when(last)
            def _():
                done(sz_ss, stz.at[0:7])
                done(sz_rs, stz.at[0:7])
                v = stz[0]
                for p in range(1, 8):
                    v = v + stz[p]
                sty[y] = v
                for o in RING:
                    copy(sty.at[y], sty.at[y], sy_ss, sy_rs, y_peer(o, 1)).start()

            for h in (0, 1):
                done(tab_ss.at[h], tab.at[s, h, 0:3 * RB])
                done(sel_ss.at[h], selm.at[s, h, 0:56])
            done(cp_ss, cparts.at[s, 0:24])
            done(dz_ss, dense.at[s, 0:7 * RB])
            up_copy(s).wait_send()
            pp_copy(s).wait_send()

            done(xa_rs.at[turn(s)], dense.at[s, 0:56])
            za[s] = (xa[s, 0, 0] + xa[s, 0, 1]) + (xa[s, 0, 2] + xa[s, 0, 3])
            ta[s, 0] = (xa[s, 1, 0] + xa[s, 1, 1]) + (xa[s, 1, 2] + xa[s, 1, 3])
            start(za_copies(s))

            @pl.when(last)
            def _():
                done(sy_ss, sty.at[0:3])
                done(sy_rs, sty.at[0:3])
                stx[x] = (sty[0] + sty[1]) + (sty[2] + sty[3])
                start(sx_copies())

            done(zb_rs.at[turn(s)], dense.at[s, 0:24])
            xb[s] = zb[s, 0, 0] + zb[s, 0, 1]
            tb[s, x] = zb[s, 1, 0] + zb[s, 1, 1]
            start(xb_copies(s))

            done(za_ss, dense.at[s, 0:24])
            done(xb_ss, dense.at[s, 0:56])

        def rest(c):
            done(xa_ss, xa.at[s, 0, 0:4 - c])
            done(zb_ss, zb.at[s, 0, 0:2 - c])
            done(za_rs.at[turn(s)], ta.at[s, 0:2 - c])

        by_core(rest)
        n = s + 1
        tbuf[n, :, :half] = ta[s, 0] + ta[s, 1]
        pl.when(jnp.logical_not(last))(lambda: weights(n, 0))
        by_core(lambda c: done(xb_rs.at[turn(s)], tb.at[s, 0:4 - c]))
        tbuf[n, :, half:] = (tb[s, 0] + tb[s, 1]) + (tb[s, 2] + tb[s, 3])

        @pl.when(jnp.logical_not(last))
        def _():
            weights(n, 1)
            up_copy(n).start()

        return carry

    lax.fori_loop(0, SWEEPS, sweep, 0)

    def finish(c):
        done(sx_rs, stx.at[0:4 - c])
        done(ids_ss, ids.at[0:4 - c])
        if c == 0:
            done(ws_ss, stat)
        else:
            done(sx_ss, stz.at[0:7])

    by_core(finish)
    v = (stx[0] + stx[1]) + (stx[2] + stx[3])
    count = v[0:1, 0:1] * 0.125
    mean1 = v[1:2, 0:1] * 2.0 / count
    mean2 = v[2:3, 0:1] * 2.0 / count
    mean3 = v[3:4, 0:1] * 2.0 / count
    scale = mean1 * mean2 * 0.0625 * mean3
    b3 = tbuf[SWEEPS]
    bias = jnp.where(keep[...] > 0, b3 * (1.0 / scale), 1.0)
    balance = b3 * ubuf[SWEEPS - 1] * (1.0 / mean3)
    for q in range(4):
        out_ref[pl.ds(q, RB, stride=4), :] = bias[:, q * 128:(q + 1) * 128]
        out_ref[pl.ds(4 * RB + q, RB, stride=4), :] = balance[:, q * 128:(q + 1) * 128]


def body(blocks, block_rows, block_cols, inter_counts, keep_mask):
    seg = keep_mask.shape[0]
    vm = pl.BlockSpec(memory_space=pltpu.VMEM)
    hbm = pl.BlockSpec(memory_space=pl.ANY)
    S = SWEEPS
    H = BS // 2
    dma = pltpu.SemaphoreType.DMA
    i32 = jnp.int32
    out = jax.ShapeDtypeStruct((seg // 64, 128), F32)

    def vf(*shape):
        return pltpu.VMEM(shape, F32)

    both = pl.pallas_call(
        kernel,
        out_shape=out,
        in_specs=[hbm] * 5,
        out_specs=vm,
        scratch_shapes=[
            pltpu.SMEM((SLOTS,), i32),
            pltpu.SMEM((SLOTS,), i32),
            pltpu.SMEM((1,), i32),
            pltpu.VMEM((seg // 128, 128), i32),
            pltpu.VMEM((SLOTS, BS, BS), BF16),
            pltpu.VMEM((IR_MAX, BS, BS), BF16),
            vf(RB, BS),
            vf(S + 1, RB, BS),
            vf(S, RB, BS),
            vf(RB + 8, BS),
            pltpu.VMEM((8, 8, 128), i32),
            pltpu.VMEM((128, SEL), BF16),
            pltpu.VMEM((SEL, 128), BF16),
            vf(8, 128),
            vf(RB, BS),
            vf(RB, BS),
            vf(S, 2, 128, H),
            vf(S, 2, SEL, H),
            vf(S, 2, 4, 8, H),
            vf(S, 1, BS),
            vf(S, 1, BS),
            vf(S, SEL, BS),
            vf(S, 1, BS),
            vf(S, 1, BS),
            vf(S, 128, BS),
            vf(S, 4, RB, BS),
            vf(S, 2, 4, RB, H),
            vf(S, RB, H),
            vf(S, 2, RB, H),
            vf(S, 2, 2, RB, H),
            vf(S, RB, H),
            vf(S, 4, RB, H),
            vf(8, 128),
            vf(8, 8, 128),
            vf(4, 8, 128),
            vf(4, 8, 128),
            dma((4,)),
            dma((2,)),
            dma, dma,
            dma((2,)), dma((2, 2)),
            dma((2,)), dma((2, 2)),
            dma, dma((2,)),
            dma, dma((2,)),
            dma, dma((2,)),
            dma, dma((2,)),
            dma, dma((2,)),
            dma, dma((2,)),
            dma, dma((2,)),
            dma, dma((2,)),
            dma, dma,
            dma, dma,
            dma, dma,
            dma, dma,
        ],
        compiler_params=pltpu.CompilerParams(
            collective_id=0, has_side_effects=True, vmem_limit_bytes=VMEM_LIMIT
        ),
        name="balance",
    )(block_rows, block_cols, inter_counts, keep_mask.reshape(seg // 128, 128), blocks)
    bias, balance = both[:seg // 128], both[seg // 128:]
    return bias.reshape(seg), balance.reshape(seg)


def solution(mesh):
    return jax.shard_map(
        body,
        mesh=mesh,
        in_specs=(
            P(("row", "col"), None, None),
            P(("row", "col")),
            P(("row", "col")),
            P(("row", "col")),
            P("row"),
        ),
        out_specs=(P("row"), P("row")),
        check_vma=False,
    )
```
